32 devices in a mesh: row: 8 (over z, y), col: 4 (over x, core).
Axes of the slice: x: 2, y: 2, z: 4, core: 2. Of those that a mesh axis runs over, the one named last changes fastest.
Arguments:
- blocks: bfloat16 [512, 3, 128, 128], P(('row', 'col')), may hold values from -0.3984375 to 0.3984375
- rows: int32 [512, 3], P(('row', 'col')), may hold values from 0 to 63, as said below
- counts: int32 [512], P(('row', 'col')), may hold values from 1 to 3
- sketch: bfloat16 [65536, 128], P(('row', 'col')), may hold values from -6 to 6
- weights: float32 [8192], replicated, may hold values from 0.35 to 2.8
Outputs:
- basis_out: float32 [8192, 128], P(('row', 'col'))
- right_factors: bfloat16 [65536, 128], P(('row', 'col'))
The draws below stay inside these ranges and needn't reach their ends.
Inputs may be any that keep to these rules, and one draw needn't show every extreme that they name: `rows`: the 3 entries of each document block are distinct feature blocks.
All inputs are finite; a program needn't handle non-finite values.
Results may differ from the reference program's by a relative error of at most 0.0049.
Values may be sent and summed in bfloat16 or wider, within the bound.
No kernel may reach another device: no remote copies, remote signals or barrier semaphores. Data moves between devices by JAX's collectives and lax.ppermute only.
A program may use at most 64 MiB of HBM per device.

```python
import jax
import jax.numpy as jnp
from jax import lax

F = 8192
BLK = 128
L = 128
SLOTS = 3
POWER = 0
DB_DEV = 16
FB = 64
DOCB = 512
DOCS = 65536


def draw_rows(key, part):
    row_keys = jax.random.split(jax.random.fold_in(key, 17), DOCB)

    def choose_rows(one_key):
        return jax.random.permutation(one_key, FB)[:SLOTS]
    return jax.vmap(choose_rows)(row_keys).astype(jnp.int32)


def draw_weights(key, part):
    position = jnp.arange(F, dtype=jnp.float32) / F
    trend = 0.6 * jnp.exp(jnp.log(3.0) * position)
    rough_key = jax.random.fold_in(key, 29)
    rough = jnp.exp(jax.random.uniform(rough_key, (F,), jnp.float32, jnp.log(0.7), jnp.log(1.4)))
    return (trend * rough).astype(jnp.float32)


def place_ends(entries, own_key, low, high):
    index_at = [jax.random.randint(jax.random.fold_in(own_key, axis), (), 0, length) for axis, length in enumerate(entries.shape)]
    longest = entries.shape.index(max(entries.shape))
    beside = index_at[:longest] + [(index_at[longest] + 1) % entries.shape[longest]] + index_at[longest + 1:]
    return entries.at[tuple(index_at)].set(low).at[tuple(beside)].set(high)


def block_levels(rng, shape, cuts, low, top_value):
    def one(dim, blocks):
        heights = jax.random.uniform(jax.random.fold_in(jax.random.fold_in(rng, 6), dim), (blocks,), jnp.float32, low / len(cuts), top_value / len(cuts))
        return jnp.repeat(jnp.exp(heights), shape[dim] // blocks).reshape((-1,) + (1,) * (len(shape) - dim - 1))

    gain = one(*cuts[0])
    for cut in cuts[1:]:
        gain = gain * one(*cut)
    return gain


def gaussian(own_key, extent, spread, limit, cuts=(), held_as=jnp.bfloat16):
    entries = jax.random.normal(own_key, extent, jnp.float32) * spread
    if len(cuts) > 0:
        entries = block_levels(own_key, extent, cuts, -0.22, 0.18) * entries
    return jnp.clip(entries, min=-limit, max=limit).astype(held_as)


def setup_inputs(seed: int = 0) -> dict:
    key_of = jax.random.split(jax.random.key(seed), 6)
    return {
        "blocks": gaussian(key_of[0], (DOCB, SLOTS, BLK, BLK), 0.0625, 0.3984375, ((0, 32),)),
        "rows": draw_rows(jax.random.fold_in(key_of[5], 71), 0),
        "counts": place_ends(jax.random.randint(key_of[2], (DOCB,), 1, SLOTS + 1), jax.random.fold_in(key_of[2], 1), 1, SLOTS).astype(jnp.int32),
        "sketch": gaussian(key_of[3], (DOCS, L), 1.0, 6.0, ((0, 32),)),
        "weights": draw_weights(jax.random.fold_in(key_of[5], 71), 0),
    }


def right_product(block_groups, id_groups, documents):
    groups = block_groups.shape[0]
    doc_groups = documents.reshape(groups, DB_DEV, BLK, L)

    def add_group(total, packed):
        tile_group, id_group, doc_group = packed
        terms = jnp.einsum('dsfk,dkl->dsfl', tile_group.astype(jnp.float32), doc_group.astype(jnp.float32), precision=lax.Precision.HIGHEST)
        summed = jax.ops.segment_sum(terms.reshape(DB_DEV * SLOTS, BLK, L), id_group, num_segments=FB + 1)
        return (total + summed, None)
    start_total = jnp.zeros((FB + 1, BLK, L), jnp.float32)
    total, _ = lax.scan(add_group, start_total, (block_groups, id_groups, doc_groups))
    return total[:FB].reshape(F, L)

def left_product(block_groups, row_groups, use_groups, weighted):
    weighted_blocks = weighted.reshape(FB, BLK, L)

    def one_group(packed):
        tile_group, row_group, use_group = packed
        picked = weighted_blocks[row_group].astype(jnp.float32)
        picked = jnp.where(use_group[:, :, None, None], picked, jnp.zeros((), jnp.float32))
        return jnp.einsum('dsfl,dsfk->dkl', picked, tile_group.astype(jnp.float32), precision=lax.Precision.HIGHEST)
    product = lax.map(one_group, (block_groups, row_groups, use_groups))
    return product.reshape(DOCS, L)

def normalize(summed):
    gram = jnp.dot(summed.T, summed, precision=lax.Precision.HIGHEST) / F
    chol_factor = jnp.linalg.cholesky(gram)
    inverse = jax.scipy.linalg.solve_triangular(chol_factor, jnp.eye(L, dtype=gram.dtype), lower=True)
    return jnp.dot(summed, inverse.T, precision=lax.Precision.HIGHEST)

def reference(blocks, rows, counts, sketch, weights):
    groups = DOCB // DB_DEV
    in_use = lax.broadcasted_iota(jnp.int32, (DOCB, SLOTS), 1) < counts[:, None]
    segment_ids = jnp.where(in_use, rows, FB).astype(jnp.int32)
    block_groups = blocks.reshape(groups, DB_DEV, SLOTS, BLK, BLK)
    id_groups = segment_ids.reshape(groups, DB_DEV * SLOTS)
    row_groups = rows.reshape(groups, DB_DEV, SLOTS)
    use_groups = in_use.reshape(groups, DB_DEV, SLOTS)
    scaling = weights[:, None]
    current = normalize(right_product(block_groups, id_groups, sketch) * scaling)
    for repeat in range(POWER):
        weighted = (current * scaling).astype(jnp.bfloat16)
        middle = left_product(block_groups, row_groups, use_groups, weighted).astype(jnp.bfloat16)
        current = normalize(right_product(block_groups, id_groups, middle) * scaling)
    weighted = (current * scaling).astype(jnp.bfloat16)
    factors = left_product(block_groups, row_groups, use_groups, weighted).astype(jnp.bfloat16)
    return (current, factors)
```

```python
import functools

import jax
import jax.numpy as jnp
from jax import lax
from jax.experimental import pallas as pl
from jax.experimental.pallas import tpu as pltpu
from jax.sharding import PartitionSpec as P

F32 = jnp.float32
BF16 = jnp.bfloat16
HIGHEST = lax.Precision.HIGHEST
AXES = ("row", "col")
VMEM_BYTES = 48 * 1024 * 1024


def whole():
    return pl.BlockSpec(memory_space=pltpu.VMEM)


def scalars():
    return pl.BlockSpec(memory_space=pltpu.SMEM)


class Plan:
    def __init__(self, rows, cols, features, block):
        self.count = rows * cols
        self.cols = cols
        self.plane_bits = cols.bit_length() - 1
        self.plane = cols
        self.rest = self.count // 2 // cols
        assert self.plane * self.rest * 2 == self.count and self.count & (self.count - 1) == 0
        self.flat = features // self.count
        self.piece = min(self.flat, block)
        self.pieces = block // self.piece
        self.per_slice = self.flat // self.piece

    def me(self):
        return lax.axis_index("row") * self.cols + lax.axis_index("col")

    def start(self, me, feature_block, piece):
        unit = feature_block * self.pieces + piece
        owner = unit // self.per_slice if self.per_slice > 1 else unit
        inside = unit - owner * self.per_slice
        apart = owner ^ me
        core = apart & 1
        plane = (apart >> 1) & (self.plane - 1)
        rest = apart >> (1 + self.plane_bits)
        at = (core * self.plane + plane) * self.rest + rest
        return pl.multiple_of(at * self.flat + inside * self.piece, self.piece)

    def swap(self, value, mask):
        return lax.ppermute(value, AXES, [(d, d ^ mask) for d in range(self.count)])


def sum_kernel(plan, rows_ref, counts_ref, blocks_ref, sketch_ref, keep_ref, send_ref, total_ref):
    me = plan.me()
    documents, slots, block, _ = blocks_ref.shape
    half = keep_ref.shape[0]
    total_ref[...] = jnp.zeros_like(total_ref)
    for d in range(documents):
        docs = sketch_ref[d * block : (d + 1) * block, :]
        for s in range(slots):
            def add(d=d, s=s, docs=docs):
                term = jnp.dot(blocks_ref[d, s], docs, preferred_element_type=F32)
                for p in range(plan.pieces):
                    at = pl.ds(plan.start(me, rows_ref[d, s], p), plan.piece)
                    total_ref[at, :] += term[p * plan.piece : (p + 1) * plan.piece]

            pl.when(s < counts_ref[d])(add)
    keep_ref[...] = total_ref[:half, :]
    send_ref[...] = total_ref[half:, :].astype(BF16)


def tiles_kernel(rows_ref, counts_ref, blocks_ref, weights_ref, out_ref):
    documents, slots, block, _ = blocks_ref.shape
    for d in range(documents):
        for s in range(slots):
            scale = weights_ref[pl.ds(rows_ref[d, s], 1), :]
            scale = jnp.where(s < counts_ref[d], scale, 0.0)
            tile = blocks_ref[d, s].T.astype(F32) * scale
            out_ref[d, :, s * block : (s + 1) * block] = tile.astype(BF16)


def split(value):
    high = value.astype(BF16)
    return high, (value - high.astype(F32)).astype(BF16)


def dot_t(a, b):
    return lax.dot_general(a, b, (((1,), (1,)), ((), ())), preferred_element_type=F32)


def dot_t3(a, b):
    a_high, a_low = split(a)
    b_high, b_low = split(b)
    return dot_t(a_high, b_high) + (dot_t(a_high, b_low) + dot_t(a_low, b_high))


def gram_kernel(own_ref, other_ref, gram_ref, *, features):
    total = jnp.zeros(gram_ref.shape, F32)
    for ref in (own_ref, other_ref):
        step = min(1024, ref.shape[0])
        for at in range(0, ref.shape[0], step):
            part = ref[at : at + step, :]
            total += lax.dot_general(part, part, (((0,), (0,)), ((), ())), preferred_element_type=F32)
    gram_ref[...] = total * (1.0 / features)


def last_kernel(plan, rows_ref, tiles_ref, own_ref, other_ref, mine_ref, inverse_ref, basis_ref, factors_ref, all_ref):
    me = plan.me()
    documents, block, _ = tiles_ref.shape
    half = own_ref.shape[0]
    slots = tiles_ref.shape[2] // block
    inverse = inverse_ref[...]
    basis_ref[...] = dot_t3(mine_ref[...], inverse)
    all_ref[:half, :] = own_ref[...]
    all_ref[half:, :] = other_ref[...]
    for d in range(documents):
        picked = []
        for s in range(slots):
            for p in range(plan.pieces):
                at = pl.ds(plan.start(me, rows_ref[d, s], p), plan.piece)
                picked.append(all_ref[at, :])
        product = jnp.dot(tiles_ref[d], jnp.concatenate(picked, axis=0), preferred_element_type=F32)
        factors_ref[d * block : (d + 1) * block, :] = dot_t3(product, inverse).astype(BF16)


def body(plan, blocks, rows, counts, sketch, weights):
    documents, slots, block, _ = blocks.shape
    columns = sketch.shape[1]
    features = weights.shape[0]
    half = features // 2
    flat, plane, rest = plan.flat, plan.plane, plan.rest
    params = pltpu.CompilerParams(vmem_limit_bytes=VMEM_BYTES)
    shape = jax.ShapeDtypeStruct

    keep, send = pl.pallas_call(
        functools.partial(sum_kernel, plan),
        out_shape=(shape((half, columns), F32), shape((half, columns), BF16)),
        in_specs=[scalars(), scalars(), whole(), whole()],
        out_specs=(whole(), whole()),
        scratch_shapes=[pltpu.VMEM((features, columns), F32)],
        compiler_params=params,
        name="local_sum",
    )(rows, counts, blocks, sketch)

    got = plan.swap(send, 1)
    keep = keep.reshape(plane, rest * flat, columns)
    got = got.reshape(plane, rest * flat, columns)
    sent = [plan.swap((keep[p] + got[p].astype(F32)).astype(BF16), p << 1) for p in range(1, plane)]
    held = keep[0] + got[0].astype(F32)
    for part in sent:
        held = held + part.astype(F32)
    held = held.reshape(rest, flat, columns)
    step = 1 + plan.plane_bits
    sent = [plan.swap(held[q].astype(BF16), q << step) for q in range(1, rest)]
    mine = held[0]
    for part in sent:
        mine = mine + part.astype(F32)
    mine = mine * lax.dynamic_slice_in_dim(weights, plan.me() * flat, flat)[:, None]

    tiles = pl.pallas_call(
        tiles_kernel,
        out_shape=shape((documents, block, slots * block), BF16),
        in_specs=[scalars(), scalars(), whole(), whole()],
        out_specs=whole(),
        compiler_params=params,
        name="tiles",
    )(rows, counts, blocks, weights.reshape(features // block, block))

    rounded = mine.astype(BF16)
    near = jnp.concatenate([rounded] + [plan.swap(rounded, q << step) for q in range(1, rest)], axis=0)
    own = jnp.concatenate([near] + [plan.swap(near, p << 1) for p in range(1, plane)], axis=0)
    other = plan.swap(own, 1)

    gram = pl.pallas_call(
        functools.partial(gram_kernel, features=features),
        out_shape=shape((columns, columns), F32),
        in_specs=[whole(), whole()],
        out_specs=whole(),
        compiler_params=params,
        name="gram",
    )(own, other)
    factor = jnp.linalg.cholesky(gram, symmetrize_input=False)
    inverse = jax.scipy.linalg.solve_triangular(factor, jnp.eye(columns, dtype=F32), lower=True)
    return pl.pallas_call(
        functools.partial(last_kernel, plan),
        out_shape=(shape((flat, columns), F32), shape((documents * block, columns), BF16)),
        in_specs=[scalars()] + [whole()] * 5,
        out_specs=(whole(), whole()),
        scratch_shapes=[pltpu.VMEM((features, columns), BF16)],
        compiler_params=params,
        name="factors",
    )(rows, tiles, own, other, mine, inverse)


def solution(mesh):
    placed = (
        P(AXES, None, None, None),
        P(AXES, None),
        P(AXES),
        P(AXES, None),
        P(),
    )

    def run(blocks, rows, counts, sketch, weights):
        plan = Plan(mesh.shape["row"], mesh.shape["col"], weights.shape[0], blocks.shape[2])
        return jax.shard_map(
            functools.partial(body, plan),
            mesh=mesh,
            in_specs=placed,
            out_specs=(P(AXES, None), P(AXES, None)),
            check_vma=False,
        )(blocks, rows, counts, sketch, weights)

    return run
```

```python
import functools

import jax
import jax.numpy as jnp
from jax import lax
from jax.experimental import pallas as pl
from jax.experimental.pallas import tpu as pltpu
from jax.sharding import PartitionSpec as P

F32 = jnp.float32
BF16 = jnp.bfloat16
AXES = ("row", "col")
VMEM_BYTES = 48 * 1024 * 1024


def whole():
    return pl.BlockSpec(memory_space=pltpu.VMEM)


def scalars():
    return pl.BlockSpec(memory_space=pltpu.SMEM)


class Plan:
    def __init__(self, rows, cols, features, block):
        self.count = rows * cols
        self.cols = cols
        self.plane_bits = cols.bit_length() - 1
        self.plane = cols
        self.rest = self.count // 2 // cols
        assert self.plane * self.rest * 2 == self.count and self.count & (self.count - 1) == 0
        self.flat = features // self.count
        self.piece = min(self.flat, block)
        self.pieces = block // self.piece
        self.per_slice = self.flat // self.piece

    def me(self):
        return lax.axis_index("row") * self.cols + lax.axis_index("col")

    def start(self, me, feature_block, piece):
        unit = feature_block * self.pieces + piece
        owner = unit // self.per_slice if self.per_slice > 1 else unit
        inside = unit - owner * self.per_slice
        apart = owner ^ me
        core = apart & 1
        plane = (apart >> 1) & (self.plane - 1)
        rest = apart >> (1 + self.plane_bits)
        at = (core * self.plane + plane) * self.rest + rest
        return pl.multiple_of(at * self.flat + inside * self.piece, self.piece)

    def swap(self, value, mask):
        return lax.ppermute(value, AXES, [(d, d ^ mask) for d in range(self.count)])


def sum_kernel(plan, rows_ref, counts_ref, blocks_ref, sketch_ref, total_ref, send_ref, tiles_ref, docs_ref, sems):
    me = plan.me()
    documents, slots, block, _ = tiles_ref.shape
    half = send_ref.shape[0]
    parts = sems.shape[0]
    per = documents // parts
    copies = []
    for c in range(parts):
        tiles_at = pl.ds(c * per, per)
        docs_at = pl.ds(c * per * block, per * block)
        pair = (
            pltpu.make_async_copy(blocks_ref.at[tiles_at], tiles_ref.at[tiles_at], sems.at[c, 0]),
            pltpu.make_async_copy(sketch_ref.at[docs_at], docs_ref.at[docs_at], sems.at[c, 1]),
        )
        for copy in pair:
            copy.start()
        copies.append(pair)
    total_ref[...] = jnp.zeros_like(total_ref)
    for c in range(parts):
        for copy in copies[c]:
            copy.wait()
        for d in range(c * per, (c + 1) * per):
            docs = docs_ref[d * block : (d + 1) * block, :]
            terms = jnp.dot(tiles_ref[d].reshape(slots * block, block), docs, preferred_element_type=F32)
            for s in range(slots):
                term = jnp.where(s < counts_ref[d], terms[s * block : (s + 1) * block], 0.0)
                for p in range(plan.pieces):
                    at = pl.ds(plan.start(me, rows_ref[s, d], p), plan.piece)
                    total_ref[at, :] += term[p * plan.piece : (p + 1) * plan.piece]
    send_ref[...] = total_ref[half:, :].astype(BF16)


def tiles_kernel(rows_ref, counts_ref, blocks_ref, weights_ref, high_ref, low_ref):
    documents, slots, block, _ = blocks_ref.shape
    for d in range(documents):
        for s in range(slots):
            scale = weights_ref[pl.ds(rows_ref[s, d], 1), :]
            scale = jnp.where(s < counts_ref[d], scale, 0.0)
            high, low = split(blocks_ref[d, s].T.astype(F32) * scale)
            high_ref[d, :, s * block : (s + 1) * block] = high
            low_ref[d, :, s * block : (s + 1) * block] = low


def split(value):
    high = value.astype(BF16)
    return high, (value - high.astype(F32)).astype(BF16)


def dot_t(a, b):
    return lax.dot_general(a, b, (((1,), (1,)), ((), ())), preferred_element_type=F32)


def dot_t3(a, b):
    a_high, a_low = split(a)
    b_high, b_low = split(b)
    return dot_t(a_high, b_high) + (dot_t(a_high, b_low) + dot_t(a_low, b_high))


def dot3(a, b):
    a_high, a_low = split(a)
    b_high, b_low = split(b)
    return dot(a_high, b_high) + (dot(a_high, b_low) + dot(a_low, b_high))


def dot(a, b):
    return jnp.dot(a, b, preferred_element_type=F32)


def dot1(a, b):
    return dot(a.astype(BF16), b.astype(BF16))


def dot_t1(a, b):
    return dot_t(a.astype(BF16), b.astype(BF16))


def eliminate(gram_ref, inverse_ref):
    size = gram_ref.shape[0]
    lane = lax.broadcasted_iota(jnp.int32, (size, size), 1)
    line = lax.broadcasted_iota(jnp.int32, (size, 1), 0)
    first = lax.broadcasted_iota(jnp.int32, (1, size), 1)
    inverse_ref[...] = jnp.where(lane == line, 1.0, 0.0)

    def step(j, carry):
        values = gram_ref[...]
        pivot_row = gram_ref[pl.ds(j, 1), :]
        pivot = jnp.sum(jnp.where(first == j, pivot_row, 0.0), axis=1, keepdims=True)
        scale = 1.0 / jnp.sqrt(pivot)
        column = jnp.sum(jnp.where(lane == j, values, 0.0), axis=1, keepdims=True)
        column = jnp.where(line > j, column * scale, 0.0)
        gram_ref[...] = values - column * (pivot_row * scale)
        own_row = inverse_ref[pl.ds(j, 1), :] * scale
        inverse_ref[...] = jnp.where(line == j, own_row, inverse_ref[...] - column * own_row)
        return carry

    lax.fori_loop(0, size, step, 0)


def invert_factor(gram, gram_ref, inverse_ref):
    size = gram.shape[0]
    line = lax.broadcasted_iota(jnp.int32, (size, size), 0)
    lane = lax.broadcasted_iota(jnp.int32, (size, size), 1)
    same = line == lane
    eye = jnp.where(same, 1.0, 0.0)
    take = jnp.where(line > lane, 1.0, jnp.where(same, 0.5, 0.0))
    diagonal = jnp.where(same, gram, 0.0)
    down = 1.0 / jnp.sqrt(jnp.sum(diagonal, axis=1, keepdims=True))
    across = 1.0 / jnp.sqrt(jnp.sum(diagonal, axis=0, keepdims=True))
    beyond = gram * down * across - eye
    factor = eye - take * beyond
    for product, product_t in ((dot1, dot_t1), (dot1, dot_t1), (dot3, dot_t3), (dot3, dot_t3)):
        left = factor - eye + product(factor, beyond)
        residual = factor.T - eye + product_t(left, factor)
        factor = factor - product(take * residual, factor)
    inverse_ref[...] = factor * across
    worst = jnp.max(jnp.sum(jnp.abs(residual), axis=1))

    @pl.when(jnp.logical_not(worst < 1e-3))
    def _():
        gram_ref[...] = gram
        eliminate(gram_ref, inverse_ref)


def last_kernel(
    plan, features, rows_ref, high_ref, low_ref, own_ref, other_ref, mine_ref, basis_ref, factors_ref, all_ref, gram_ref, inverse_ref
):
    me = plan.me()
    documents, block, _ = high_ref.shape
    half = own_ref.shape[0]
    slots = high_ref.shape[2] // block
    gram = jnp.zeros(gram_ref.shape, F32)
    step = min(1024, half)
    for base, ref in ((0, own_ref), (half, other_ref)):
        for at in range(0, half, step):
            part = ref[at : at + step, :]
            all_ref[base + at : base + at + step, :] = part
            gram += lax.dot_general(part, part, (((0,), (0,)), ((), ())), preferred_element_type=F32)
    invert_factor(gram * (1.0 / features), gram_ref, inverse_ref)
    inverse = inverse_ref[...]
    basis_ref[...] = dot_t3(mine_ref[...], inverse)
    for d in range(documents):
        picked = []
        for s in range(slots):
            for p in range(plan.pieces):
                at = pl.ds(plan.start(me, rows_ref[s, d], p), plan.piece)
                picked.append(all_ref[at, :])
        picked = jnp.concatenate(picked, axis=0)
        product = dot(high_ref[d], picked) + dot(low_ref[d], picked)
        factors_ref[d * block : (d + 1) * block, :] = dot_t3(product, inverse).astype(BF16)


def body(plan, blocks, rows, counts, sketch, weights):
    documents, slots, block, _ = blocks.shape
    columns = sketch.shape[1]
    features = weights.shape[0]
    half = features // 2
    flat, plane, rest = plan.flat, plan.plane, plan.rest
    params = pltpu.CompilerParams(vmem_limit_bytes=VMEM_BYTES)
    shape = jax.ShapeDtypeStruct

    rows = rows.T
    parts = min(4, documents)
    keep, send = pl.pallas_call(
        functools.partial(sum_kernel, plan),
        out_shape=(shape((features, columns), F32), shape((half, columns), BF16)),
        in_specs=[scalars(), scalars(), pl.BlockSpec(memory_space=pltpu.HBM), pl.BlockSpec(memory_space=pltpu.HBM)],
        out_specs=(whole(), whole()),
        scratch_shapes=[
            pltpu.VMEM(blocks.shape, BF16),
            pltpu.VMEM(sketch.shape, BF16),
            pltpu.SemaphoreType.DMA((parts, 2)),
        ],
        compiler_params=params,
        name="local_sum",
    )(rows, counts, blocks, sketch)
    keep = keep[:half]

    got = plan.swap(send, 1)
    keep = keep.reshape(plane, rest * flat, columns)
    got = got.reshape(plane, rest * flat, columns)
    sent = [plan.swap((keep[p] + got[p].astype(F32)).astype(BF16), p << 1) for p in range(1, plane)]
    held = keep[0] + got[0].astype(F32)
    for part in sent:
        held = held + part.astype(F32)
    held = held.reshape(rest, flat, columns)
    step = 1 + plan.plane_bits
    sent = [plan.swap(held[q].astype(BF16), q << step) for q in range(1, rest)]
    mine = held[0]
    for part in sent:
        mine = mine + part.astype(F32)
    mine = mine * lax.dynamic_slice_in_dim(weights, plan.me() * flat, flat)[:, None]

    tiles_shape = shape((documents, block, slots * block), BF16)
    high, low = pl.pallas_call(
        tiles_kernel,
        out_shape=(tiles_shape, tiles_shape),
        in_specs=[scalars(), scalars(), whole(), whole()],
        out_specs=(whole(), whole()),
        compiler_params=params,
        cost_estimate=pl.CostEstimate(flops=1 << 20, bytes_accessed=16 << 20, transcendentals=0),
        name="tiles",
    )(rows, counts, blocks, weights.reshape(features // block, block))

    rounded = mine.astype(BF16)
    near = jnp.concatenate([rounded] + [plan.swap(rounded, q << step) for q in range(1, rest)], axis=0)
    own = jnp.concatenate([near] + [plan.swap(near, p << 1) for p in range(1, plane)], axis=0)
    other = plan.swap(own, 1)

    return pl.pallas_call(
        functools.partial(last_kernel, plan, features),
        out_shape=(shape((flat, columns), F32), shape((documents * block, columns), BF16)),
        in_specs=[scalars()] + [whole()] * 5,
        out_specs=(whole(), whole()),
        scratch_shapes=[
            pltpu.VMEM((features, columns), BF16),
            pltpu.VMEM((columns, columns), F32),
            pltpu.VMEM((columns, columns), F32),
        ],
        compiler_params=params,
        name="factors",
    )(rows, high, low, own, other, mine)


def solution(mesh):
    placed = (
        P(AXES, None, None, None),
        P(AXES, None),
        P(AXES),
        P(AXES, None),
        P(),
    )

    def run(blocks, rows, counts, sketch, weights):
        plan = Plan(mesh.shape["row"], mesh.shape["col"], weights.shape[0], blocks.shape[2])
        return jax.shard_map(
            functools.partial(body, plan),
            mesh=mesh,
            in_specs=placed,
            out_specs=(P(AXES, None), P(AXES, None)),
            check_vma=False,
        )(blocks, rows, counts, sketch, weights)

    return run
```

```python
import functools

import jax
import jax.numpy as jnp
from jax import lax
from jax.experimental import pallas as pl
from jax.experimental.pallas import tpu as pltpu
from jax.sharding import PartitionSpec as P

F32 = jnp.float32
BF16 = jnp.bfloat16
AXES = ("row", "col")
VMEM_BYTES = 48 * 1024 * 1024


def whole():
    return pl.BlockSpec(memory_space=pltpu.VMEM)


def in_hbm(value):
    return pltpu.with_memory_space_constraint(value, pltpu.HBM)


def scalars():
    return pl.BlockSpec(memory_space=pltpu.SMEM)


class Plan:
    def __init__(self, rows, cols, features, block):
        self.count = rows * cols
        self.cols = cols
        self.steps = self.count.bit_length() - 2
        assert 1 << (self.steps + 1) == self.count and self.steps >= 2
        bits = list(range(1, self.steps + 1))
        self.order = (bits[:-2] + [bits[-1], bits[-2]], [bits[-2]] + bits[:-2] + [bits[-1]])
        self.flat = features // self.count
        self.piece = min(self.flat, block)
        self.pieces = block // self.piece
        per_slice = self.flat // self.piece
        self.slice_bits = per_slice.bit_length() - 1
        assert 1 << self.slice_bits == per_slice and self.piece * self.pieces == block

    def me(self):
        return lax.axis_index("row") * self.cols + lax.axis_index("col")

    def start(self, me, feature_block, piece):
        unit = feature_block * self.pieces + piece
        owner = unit >> self.slice_bits
        inside = unit & ((1 << self.slice_bits) - 1)
        apart = owner ^ me
        places = []
        for order in self.order:
            place = apart & 1
            for bit in order:
                place = (place << 1) | ((apart >> bit) & 1)
            places.append(place)
        place = jnp.where((owner & 1) == 0, places[0], places[1])
        return pl.multiple_of(place * self.flat + inside * self.piece, self.piece)

    def swap(self, value, step):
        return lax.ppermute(value, AXES, [(d, d ^ (1 << self.order[d & 1][step])) for d in range(self.count)])

    def swap_cores(self, value):
        return lax.ppermute(value, AXES, [(d, d ^ 1) for d in range(self.count)])


def sum_kernel(plan, rows_ref, counts_ref, blocks_ref, sketch_ref, keep_ref, send_ref, total_ref, tiles_ref, docs_ref, sems):
    me = plan.me()
    documents, slots, block, _ = tiles_ref.shape
    half = send_ref.shape[0]
    parts = sems.shape[0]
    per = documents // parts
    copies = []
    for c in range(parts):
        tiles_at = pl.ds(c * per, per)
        docs_at = pl.ds(c * per * block, per * block)
        pair = (
            pltpu.make_async_copy(blocks_ref.at[tiles_at], tiles_ref.at[tiles_at], sems.at[c, 0]),
            pltpu.make_async_copy(sketch_ref.at[docs_at], docs_ref.at[docs_at], sems.at[c, 1]),
        )
        for copy in pair:
            copy.start()
        copies.append(pair)
    total_ref[...] = jnp.zeros_like(total_ref)
    for c in range(parts):
        for copy in copies[c]:
            copy.wait()
        for d in range(c * per, (c + 1) * per):
            docs = docs_ref[d * block : (d + 1) * block, :]
            terms = jnp.dot(tiles_ref[d].reshape(slots * block, block), docs, preferred_element_type=F32)
            for s in range(slots):
                term = jnp.where(s < counts_ref[d], terms[s * block : (s + 1) * block], 0.0)
                for p in range(plan.pieces):
                    at = pl.ds(plan.start(me, rows_ref[s, d], p), plan.piece)
                    total_ref[at, :] += term[p * plan.piece : (p + 1) * plan.piece]
    keep_ref[...] = total_ref[:half, :]
    send_ref[...] = total_ref[half:, :].astype(BF16)


def tiles_kernel(rows_ref, counts_ref, blocks_ref, weights_ref, high_ref, low_ref):
    documents, slots, block, _ = blocks_ref.shape
    for d in range(documents):
        for s in range(slots):
            scale = weights_ref[pl.ds(rows_ref[s, d], 1), :]
            scale = jnp.where(s < counts_ref[d], scale, 0.0)
            high, low = split(blocks_ref[d, s].T.astype(F32) * scale)
            high_ref[d, :, s * block : (s + 1) * block] = high
            low_ref[d, :, s * block : (s + 1) * block] = low


def split(value):
    high = value.astype(BF16)
    return high, (value - high.astype(F32)).astype(BF16)


def dot_t(a, b):
    return lax.dot_general(a, b, (((1,), (1,)), ((), ())), preferred_element_type=F32)


def dot_t3(a, b):
    a_high, a_low = split(a)
    b_high, b_low = split(b)
    return dot_t(a_high, b_high) + (dot_t(a_high, b_low) + dot_t(a_low, b_high))


def dot3(a, b):
    a_high, a_low = split(a)
    b_high, b_low = split(b)
    return dot(a_high, b_high) + (dot(a_high, b_low) + dot(a_low, b_high))


def dot(a, b):
    return jnp.dot(a, b, preferred_element_type=F32)


def dot1(a, b):
    return dot(a.astype(BF16), b.astype(BF16))


def dot_t1(a, b):
    return dot_t(a.astype(BF16), b.astype(BF16))


def eliminate(gram_ref, inverse_ref):
    size = gram_ref.shape[0]
    lane = lax.broadcasted_iota(jnp.int32, (size, size), 1)
    line = lax.broadcasted_iota(jnp.int32, (size, 1), 0)
    first = lax.broadcasted_iota(jnp.int32, (1, size), 1)
    inverse_ref[...] = jnp.where(lane == line, 1.0, 0.0)

    def step(j, carry):
        values = gram_ref[...]
        pivot_row = gram_ref[pl.ds(j, 1), :]
        pivot = jnp.sum(jnp.where(first == j, pivot_row, 0.0), axis=1, keepdims=True)
        scale = 1.0 / jnp.sqrt(pivot)
        column = jnp.sum(jnp.where(lane == j, values, 0.0), axis=1, keepdims=True)
        column = jnp.where(line > j, column * scale, 0.0)
        gram_ref[...] = values - column * (pivot_row * scale)
        own_row = inverse_ref[pl.ds(j, 1), :] * scale
        inverse_ref[...] = jnp.where(line == j, own_row, inverse_ref[...] - column * own_row)
        return carry

    lax.fori_loop(0, size, step, 0)


def invert_factor(gram, gram_ref, inverse_ref):
    size = gram.shape[0]
    line = lax.broadcasted_iota(jnp.int32, (size, size), 0)
    lane = lax.broadcasted_iota(jnp.int32, (size, size), 1)
    same = line == lane
    eye = jnp.where(same, 1.0, 0.0)
    take = jnp.where(line > lane, 1.0, jnp.where(same, 0.5, 0.0))
    diagonal = jnp.where(same, gram, 0.0)
    down = 1.0 / jnp.sqrt(jnp.sum(diagonal, axis=1, keepdims=True))
    across = 1.0 / jnp.sqrt(jnp.sum(diagonal, axis=0, keepdims=True))
    beyond = gram * down * across - eye
    factor = eye - take * beyond
    for product, product_t in ((dot1, dot_t1), (dot1, dot_t1), (dot3, dot_t3), (dot3, dot_t3)):
        left = factor - eye + product(factor, beyond)
        residual = factor.T - eye + product_t(left, factor)
        factor = factor - product(take * residual, factor)
    inverse_ref[...] = factor * across
    worst = jnp.max(jnp.sum(jnp.abs(residual), axis=1))

    @pl.when(jnp.logical_not(worst < 1e-3))
    def _():
        gram_ref[...] = gram
        eliminate(gram_ref, inverse_ref)


def last_kernel(
    plan, features, rows_ref, high_ref, low_ref, own_ref, other_ref, mine_ref, basis_ref, factors_ref, all_ref, gram_ref, inverse_ref
):
    me = plan.me()
    documents, block, _ = high_ref.shape
    half = own_ref.shape[0]
    slots = high_ref.shape[2] // block
    gram = jnp.zeros(gram_ref.shape, F32)
    step = min(1024, half)
    for base, ref in ((0, own_ref), (half, other_ref)):
        for at in range(0, half, step):
            part = ref[at : at + step, :]
            all_ref[base + at : base + at + step, :] = part
            gram += lax.dot_general(part, part, (((0,), (0,)), ((), ())), preferred_element_type=F32)
    invert_factor(gram * (1.0 / features), gram_ref, inverse_ref)
    inverse = inverse_ref[...]
    basis_ref[...] = dot_t3(mine_ref[...], inverse)
    for d in range(documents):
        picked = []
        for s in range(slots):
            for p in range(plan.pieces):
                at = pl.ds(plan.start(me, rows_ref[s, d], p), plan.piece)
                picked.append(all_ref[at, :])
        picked = jnp.concatenate(picked, axis=0)
        product = dot(high_ref[d], picked) + dot(low_ref[d], picked)
        factors_ref[d * block : (d + 1) * block, :] = dot_t3(product, inverse).astype(BF16)


def body(plan, blocks, rows, counts, sketch, weights):
    documents, slots, block, _ = blocks.shape
    columns = sketch.shape[1]
    features = weights.shape[0]
    half = features // 2
    flat = plan.flat
    params = pltpu.CompilerParams(vmem_limit_bytes=VMEM_BYTES)
    shape = jax.ShapeDtypeStruct

    rows = rows.T
    parts = min(4, documents)
    keep, send = pl.pallas_call(
        functools.partial(sum_kernel, plan),
        out_shape=(pltpu.VMEM((half, columns), F32), pltpu.VMEM((half, columns), BF16)),
        in_specs=[scalars(), scalars(), pl.BlockSpec(memory_space=pltpu.HBM), pl.BlockSpec(memory_space=pltpu.HBM)],
        out_specs=(whole(), whole()),
        scratch_shapes=[
            pltpu.VMEM((features, columns), F32),
            pltpu.VMEM(blocks.shape, BF16),
            pltpu.VMEM(sketch.shape, BF16),
            pltpu.SemaphoreType.DMA((parts, 2)),
        ],
        compiler_params=pltpu.CompilerParams(vmem_limit_bytes=VMEM_BYTES),
        name="local_sum",
    )(in_hbm(rows), in_hbm(counts), in_hbm(blocks), in_hbm(sketch))
    got = plan.swap_cores(send)
    for k in range(plan.steps):
        held = keep + got.astype(F32)
        middle = held.shape[0] // 2
        keep = held[:middle]
        got = plan.swap(held[middle:].astype(BF16), k)
    mine = keep + got.astype(F32)
    mine = mine * lax.dynamic_slice_in_dim(weights, plan.me() * flat, flat)[:, None]

    tiles_shape = shape((documents, block, slots * block), BF16)
    high, low = pl.pallas_call(
        tiles_kernel,
        out_shape=(tiles_shape, tiles_shape),
        in_specs=[scalars(), scalars(), whole(), whole()],
        out_specs=(whole(), whole()),
        compiler_params=params,
        cost_estimate=pl.CostEstimate(flops=1 << 20, bytes_accessed=16 << 20, transcendentals=0),
        name="tiles",
    )(rows, counts, blocks, weights.reshape(features // block, block))

    own = mine.astype(BF16)
    for k in reversed(range(plan.steps)):
        own = jnp.concatenate([own, plan.swap(own, k)], axis=0)
    other = plan.swap_cores(own)

    return pl.pallas_call(
        functools.partial(last_kernel, plan, features),
        out_shape=(shape((flat, columns), F32), shape((documents * block, columns), BF16)),
        in_specs=[scalars()] + [whole()] * 5,
        out_specs=(whole(), whole()),
        scratch_shapes=[
            pltpu.VMEM((features, columns), BF16),
            pltpu.VMEM((columns, columns), F32),
            pltpu.VMEM((columns, columns), F32),
        ],
        compiler_params=params,
        name="factors",
    )(rows, high, low, own, other, mine)


def solution(mesh):
    placed = (
        P(AXES, None, None, None),
        P(AXES, None),
        P(AXES),
        P(AXES, None),
        P(),
    )

    def run(blocks, rows, counts, sketch, weights):
        plan = Plan(mesh.shape["row"], mesh.shape["col"], weights.shape[0], blocks.shape[2])
        return jax.shard_map(
            functools.partial(body, plan),
            mesh=mesh,
            in_specs=placed,
            out_specs=(P(AXES, None), P(AXES, None)),
            check_vma=False,
        )(blocks, rows, counts, sketch, weights)

    return run
```

```python
import functools

import jax
import jax.numpy as jnp
from jax import lax
from jax.experimental import pallas as pl
from jax.experimental.pallas import tpu as pltpu
from jax.sharding import PartitionSpec as P

F32 = jnp.float32
BF16 = jnp.bfloat16
AXES = ("row", "col")
VMEM_BYTES = 48 * 1024 * 1024


def whole():
    return pl.BlockSpec(memory_space=pltpu.VMEM)


def in_hbm(value):
    return pltpu.with_memory_space_constraint(value, pltpu.HBM)


def scalars():
    return pl.BlockSpec(memory_space=pltpu.SMEM)


class Plan:
    def __init__(self, rows, cols, features, block):
        self.count = rows * cols
        self.cols = cols
        self.plane = cols
        self.line = rows // 2
        self.plane_bits = cols.bit_length() - 1
        assert self.plane * self.line * 2 == self.count and self.count & (self.count - 1) == 0
        self.turned = (False, self.plane == self.line)
        self.flat = features // self.count
        self.piece = min(self.flat, block)
        self.pieces = block // self.piece
        per_slice = self.flat // self.piece
        self.slice_bits = per_slice.bit_length() - 1
        assert 1 << self.slice_bits == per_slice and self.piece * self.pieces == block
        planes, lines = [], []
        for core in (0, 1):
            first = [[(z * self.plane + p) * 2 + core for p in range(self.plane)] for z in range(self.line)]
            second = [[(z * self.plane + p) * 2 + core for z in range(self.line)] for p in range(self.plane)]
            if self.turned[core]:
                first, second = second, first
            planes += first
            lines += second
        self.groups = (planes, lines)

    def me(self):
        return lax.axis_index("row") * self.cols + lax.axis_index("col")

    def start(self, me, feature_block, piece):
        unit = feature_block * self.pieces + piece
        owner = unit >> self.slice_bits
        inside = unit & ((1 << self.slice_bits) - 1)
        plane = (owner >> 1) & (self.plane - 1)
        line = owner >> (1 + self.plane_bits)
        place = plane * self.line + line
        if self.turned[1]:
            place = jnp.where((owner & 1) == 0, place, line * self.plane + plane)
        place = place + ((owner ^ me) & 1) * (self.count // 2)
        return pl.multiple_of(place * self.flat + inside * self.piece, self.piece)

    def exchange(self, value, stage):
        return lax.all_to_all(value, AXES, 0, 0, axis_index_groups=self.groups[stage], tiled=True)

    def swap_cores(self, value):
        return lax.ppermute(value, AXES, [(d, d ^ 1) for d in range(self.count)])


def sum_kernel(plan, rows_ref, counts_ref, blocks_ref, sketch_ref, keep_ref, send_ref, total_ref, tiles_ref, docs_ref, sems):
    me = plan.me()
    documents, slots, block, _ = tiles_ref.shape
    half = send_ref.shape[0]
    parts = sems.shape[0]
    per = documents // parts
    copies = []
    for c in range(parts):
        tiles_at = pl.ds(c * per, per)
        docs_at = pl.ds(c * per * block, per * block)
        pair = (
            pltpu.make_async_copy(blocks_ref.at[tiles_at], tiles_ref.at[tiles_at], sems.at[c, 0]),
            pltpu.make_async_copy(sketch_ref.at[docs_at], docs_ref.at[docs_at], sems.at[c, 1]),
        )
        for copy in pair:
            copy.start()
        copies.append(pair)
    total_ref[...] = jnp.zeros_like(total_ref)
    for c in range(parts):
        for copy in copies[c]:
            copy.wait()
        for d in range(c * per, (c + 1) * per):
            docs = docs_ref[d * block : (d + 1) * block, :]
            terms = jnp.dot(tiles_ref[d].reshape(slots * block, block), docs, preferred_element_type=F32)
            for s in range(slots):
                term = jnp.where(s < counts_ref[d], terms[s * block : (s + 1) * block], 0.0)
                for p in range(plan.pieces):
                    at = pl.ds(plan.start(me, rows_ref[s, d], p), plan.piece)
                    total_ref[at, :] += term[p * plan.piece : (p + 1) * plan.piece]
    keep_ref[...] = total_ref[:half, :]
    send_ref[...] = total_ref[half:, :].astype(BF16)


def tiles_kernel(rows_ref, counts_ref, blocks_ref, weights_ref, high_ref, low_ref):
    documents, slots, block, _ = blocks_ref.shape
    for d in range(documents):
        for s in range(slots):
            scale = weights_ref[pl.ds(rows_ref[s, d], 1), :]
            scale = jnp.where(s < counts_ref[d], scale, 0.0)
            high, low = split(blocks_ref[d, s].T.astype(F32) * scale)
            high_ref[d, :, s * block : (s + 1) * block] = high
            low_ref[d, :, s * block : (s + 1) * block] = low


def split(value):
    high = value.astype(BF16)
    return high, (value - high.astype(F32)).astype(BF16)


def dot_t(a, b):
    return lax.dot_general(a, b, (((1,), (1,)), ((), ())), preferred_element_type=F32)


def dot_t3(a, b):
    a_high, a_low = split(a)
    b_high, b_low = split(b)
    return dot_t(a_high, b_high) + (dot_t(a_high, b_low) + dot_t(a_low, b_high))


def dot3(a, b):
    a_high, a_low = split(a)
    b_high, b_low = split(b)
    return dot(a_high, b_high) + (dot(a_high, b_low) + dot(a_low, b_high))


def dot(a, b):
    return jnp.dot(a, b, preferred_element_type=F32)


def dot1(a, b):
    return dot(a.astype(BF16), b.astype(BF16))


def dot_t1(a, b):
    return dot_t(a.astype(BF16), b.astype(BF16))


def eliminate(gram_ref, inverse_ref):
    size = gram_ref.shape[0]
    lane = lax.broadcasted_iota(jnp.int32, (size, size), 1)
    line = lax.broadcasted_iota(jnp.int32, (size, 1), 0)
    first = lax.broadcasted_iota(jnp.int32, (1, size), 1)
    inverse_ref[...] = jnp.where(lane == line, 1.0, 0.0)

    def step(j, carry):
        values = gram_ref[...]
        pivot_row = gram_ref[pl.ds(j, 1), :]
        pivot = jnp.sum(jnp.where(first == j, pivot_row, 0.0), axis=1, keepdims=True)
        scale = 1.0 / jnp.sqrt(pivot)
        column = jnp.sum(jnp.where(lane == j, values, 0.0), axis=1, keepdims=True)
        column = jnp.where(line > j, column * scale, 0.0)
        gram_ref[...] = values - column * (pivot_row * scale)
        own_row = inverse_ref[pl.ds(j, 1), :] * scale
        inverse_ref[...] = jnp.where(line == j, own_row, inverse_ref[...] - column * own_row)
        return carry

    lax.fori_loop(0, size, step, 0)


def invert_factor(gram, gram_ref, inverse_ref):
    size = gram.shape[0]
    line = lax.broadcasted_iota(jnp.int32, (size, size), 0)
    lane = lax.broadcasted_iota(jnp.int32, (size, size), 1)
    same = line == lane
    eye = jnp.where(same, 1.0, 0.0)
    take = jnp.where(line > lane, 1.0, jnp.where(same, 0.5, 0.0))
    diagonal = jnp.where(same, gram, 0.0)
    down = 1.0 / jnp.sqrt(jnp.sum(diagonal, axis=1, keepdims=True))
    across = 1.0 / jnp.sqrt(jnp.sum(diagonal, axis=0, keepdims=True))
    beyond = gram * down * across - eye
    factor = eye - take * beyond
    for product, product_t in ((dot1, dot_t1), (dot1, dot_t1), (dot3, dot_t3), (dot3, dot_t3)):
        left = factor - eye + product(factor, beyond)
        residual = factor.T - eye + product_t(left, factor)
        factor = factor - product(take * residual, factor)
    inverse_ref[...] = factor * across
    worst = jnp.max(jnp.sum(jnp.abs(residual), axis=1))

    @pl.when(jnp.logical_not(worst < 1e-3))
    def _():
        gram_ref[...] = gram
        eliminate(gram_ref, inverse_ref)


def last_kernel(
    plan, features, rows_ref, high_ref, low_ref, own_ref, other_ref, mine_ref, basis_ref, factors_ref, all_ref, gram_ref, inverse_ref
):
    me = plan.me()
    documents, block, _ = high_ref.shape
    half = own_ref.shape[0]
    slots = high_ref.shape[2] // block
    gram = jnp.zeros(gram_ref.shape, F32)
    step = min(1024, half)
    for base, ref in ((0, own_ref), (half, other_ref)):
        for at in range(0, half, step):
            part = ref[at : at + step, :]
            all_ref[base + at : base + at + step, :] = part
            gram += lax.dot_general(part, part, (((0,), (0,)), ((), ())), preferred_element_type=F32)
    invert_factor(gram * (1.0 / features), gram_ref, inverse_ref)
    inverse = inverse_ref[...]
    basis_ref[...] = dot_t3(mine_ref[...], inverse)
    for d in range(documents):
        picked = []
        for s in range(slots):
            for p in range(plan.pieces):
                at = pl.ds(plan.start(me, rows_ref[s, d], p), plan.piece)
                picked.append(all_ref[at, :])
        picked = jnp.concatenate(picked, axis=0)
        product = dot(high_ref[d], picked) + dot(low_ref[d], picked)
        factors_ref[d * block : (d + 1) * block, :] = dot_t3(product, inverse).astype(BF16)


def body(plan, blocks, rows, counts, sketch, weights):
    documents, slots, block, _ = blocks.shape
    columns = sketch.shape[1]
    features = weights.shape[0]
    half = features // 2
    flat = plan.flat
    params = pltpu.CompilerParams(vmem_limit_bytes=VMEM_BYTES)
    shape = jax.ShapeDtypeStruct

    rows = rows.T
    parts = min(4, documents)
    keep, send = pl.pallas_call(
        functools.partial(sum_kernel, plan),
        out_shape=(pltpu.VMEM((half, columns), F32), pltpu.VMEM((half, columns), BF16)),
        in_specs=[scalars(), scalars(), pl.BlockSpec(memory_space=pltpu.HBM), pl.BlockSpec(memory_space=pltpu.HBM)],
        out_specs=(whole(), whole()),
        scratch_shapes=[
            pltpu.VMEM((features, columns), F32),
            pltpu.VMEM(blocks.shape, BF16),
            pltpu.VMEM(sketch.shape, BF16),
            pltpu.SemaphoreType.DMA((parts, 2)),
        ],
        compiler_params=pltpu.CompilerParams(vmem_limit_bytes=VMEM_BYTES),
        name="local_sum",
    )(in_hbm(rows), in_hbm(counts), in_hbm(blocks), in_hbm(sketch))
    got = plan.swap_cores(send)
    mine = keep + got.astype(F32)
    for stage, members in ((0, plan.plane), (1, plan.line)):
        parts = plan.exchange(mine.astype(BF16).reshape(members, -1, columns), stage)
        mine = parts[0].astype(F32)
        for j in range(1, members):
            mine = mine + parts[j].astype(F32)
    mine = mine * lax.dynamic_slice_in_dim(weights, plan.me() * flat, flat)[:, None]

    tiles_shape = shape((documents, block, slots * block), BF16)
    high, low = pl.pallas_call(
        tiles_kernel,
        out_shape=(tiles_shape, tiles_shape),
        in_specs=[scalars(), scalars(), whole(), whole()],
        out_specs=(whole(), whole()),
        compiler_params=params,
        cost_estimate=pl.CostEstimate(flops=1 << 20, bytes_accessed=16 << 20, transcendentals=0),
        name="tiles",
    )(rows, counts, blocks, weights.reshape(features // block, block))

    own = mine.astype(BF16)
    for stage, members in ((1, plan.line), (0, plan.plane)):
        own = plan.exchange(jnp.broadcast_to(own, (members,) + own.shape), stage).reshape(-1, columns)
    other = plan.swap_cores(own)

    return pl.pallas_call(
        functools.partial(last_kernel, plan, features),
        out_shape=(shape((flat, columns), F32), shape((documents * block, columns), BF16)),
        in_specs=[scalars()] + [whole()] * 5,
        out_specs=(whole(), whole()),
        scratch_shapes=[
            pltpu.VMEM((features, columns), BF16),
            pltpu.VMEM((columns, columns), F32),
            pltpu.VMEM((columns, columns), F32),
        ],
        compiler_params=params,
        name="factors",
    )(rows, high, low, own, other, mine)


def solution(mesh):
    placed = (
        P(AXES, None, None, None),
        P(AXES, None),
        P(AXES),
        P(AXES, None),
        P(),
    )

    def run(blocks, rows, counts, sketch, weights):
        plan = Plan(mesh.shape["row"], mesh.shape["col"], weights.shape[0], blocks.shape[2])
        return jax.shard_map(
            functools.partial(body, plan),
            mesh=mesh,
            in_specs=placed,
            out_specs=(P(AXES, None), P(AXES, None)),
            check_vma=False,
        )(blocks, rows, counts, sketch, weights)

    return run
```

```python
import functools

import jax
import jax.numpy as jnp
from jax import lax
from jax.experimental import pallas as pl
from jax.experimental.pallas import tpu as pltpu
from jax.sharding import PartitionSpec as P

F32 = jnp.float32
BF16 = jnp.bfloat16
AXES = ("row", "col")
VMEM_BYTES = 48 * 1024 * 1024


def whole():
    return pl.BlockSpec(memory_space=pltpu.VMEM)


def in_hbm(value):
    return pltpu.with_memory_space_constraint(value, pltpu.HBM)


def scalars():
    return pl.BlockSpec(memory_space=pltpu.SMEM)


class Plan:
    def __init__(self, rows, cols, features, block):
        self.count = rows * cols
        self.cols = cols
        self.plane = cols
        self.line = rows // 2
        self.plane_bits = cols.bit_length() - 1
        assert self.plane * self.line * 2 == self.count and self.count & (self.count - 1) == 0
        self.flat = features // self.count
        self.piece = min(self.flat, block)
        self.pieces = block // self.piece
        per_slice = self.flat // self.piece
        self.slice_bits = per_slice.bit_length() - 1
        assert 1 << self.slice_bits == per_slice and self.piece * self.pieces == block

    def me(self):
        return lax.axis_index("row") * self.cols + lax.axis_index("col")

    def start(self, me, feature_block, piece):
        unit = feature_block * self.pieces + piece
        owner = unit >> self.slice_bits
        inside = unit & ((1 << self.slice_bits) - 1)
        apart = owner ^ me
        place = (apart & 1) * self.plane + ((apart >> 1) & (self.plane - 1))
        place = place * self.line + (apart >> (1 + self.plane_bits))
        return pl.multiple_of(place * self.flat + inside * self.piece, self.piece)

    def swap(self, value, mask):
        return lax.ppermute(value, AXES, [(d, d ^ mask) for d in range(self.count)])

    def swap_cores(self, value):
        return self.swap(value, 1)

    def swap_plane(self, value, member):
        return self.swap(value, member << 1)

    def swap_line(self, value, member):
        return self.swap(value, member << (1 + self.plane_bits))


def sum_kernel(plan, rows_ref, counts_ref, blocks_ref, sketch_ref, keep_ref, *rest):
    send_refs, (total_ref, tiles_ref, docs_ref, sems) = rest[: plan.plane], rest[plan.plane :]
    me = plan.me()
    documents, slots, block, _ = tiles_ref.shape
    half = keep_ref.shape[0]
    parts = sems.shape[0]
    per = documents // parts
    copies = []
    for c in range(parts):
        tiles_at = pl.ds(c * per, per)
        docs_at = pl.ds(c * per * block, per * block)
        pair = (
            pltpu.make_async_copy(blocks_ref.at[tiles_at], tiles_ref.at[tiles_at], sems.at[c, 0]),
            pltpu.make_async_copy(sketch_ref.at[docs_at], docs_ref.at[docs_at], sems.at[c, 1]),
        )
        for copy in pair:
            copy.start()
        copies.append(pair)
    total_ref[...] = jnp.zeros_like(total_ref)
    for c in range(parts):
        for copy in copies[c]:
            copy.wait()
        for d in range(c * per, (c + 1) * per):
            docs = docs_ref[d * block : (d + 1) * block, :]
            terms = jnp.dot(tiles_ref[d].reshape(slots * block, block), docs, preferred_element_type=F32)
            for s in range(slots):
                term = jnp.where(s < counts_ref[d], terms[s * block : (s + 1) * block], 0.0)
                for p in range(plan.pieces):
                    at = pl.ds(plan.start(me, rows_ref[s, d], p), plan.piece)
                    total_ref[at, :] += term[p * plan.piece : (p + 1) * plan.piece]
    keep_ref[...] = total_ref[:half, :]
    for p, send_ref in enumerate(send_refs):
        size = send_ref.shape[0]
        send_ref[...] = total_ref[half + p * size : half + (p + 1) * size, :].astype(BF16)


def tiles_kernel(rows_ref, counts_ref, blocks_ref, weights_ref, high_ref, low_ref):
    documents, slots, block, _ = blocks_ref.shape
    for d in range(documents):
        for s in range(slots):
            scale = weights_ref[pl.ds(rows_ref[s, d], 1), :]
            scale = jnp.where(s < counts_ref[d], scale, 0.0)
            high, low = split(blocks_ref[d, s].T.astype(F32) * scale)
            high_ref[d, :, s * block : (s + 1) * block] = high
            low_ref[d, :, s * block : (s + 1) * block] = low


def split(value):
    high = value.astype(BF16)
    return high, (value - high.astype(F32)).astype(BF16)


def dot_t(a, b):
    return lax.dot_general(a, b, (((1,), (1,)), ((), ())), preferred_element_type=F32)


def dot_t3(a, b):
    a_high, a_low = split(a)
    b_high, b_low = split(b)
    return dot_t(a_high, b_high) + (dot_t(a_high, b_low) + dot_t(a_low, b_high))


def dot3(a, b):
    a_high, a_low = split(a)
    b_high, b_low = split(b)
    return dot(a_high, b_high) + (dot(a_high, b_low) + dot(a_low, b_high))


def dot(a, b):
    return jnp.dot(a, b, preferred_element_type=F32)


def dot1(a, b):
    return dot(a.astype(BF16), b.astype(BF16))


def dot_t1(a, b):
    return dot_t(a.astype(BF16), b.astype(BF16))


def eliminate(gram_ref, inverse_ref):
    size = gram_ref.shape[0]
    lane = lax.broadcasted_iota(jnp.int32, (size, size), 1)
    line = lax.broadcasted_iota(jnp.int32, (size, 1), 0)
    first = lax.broadcasted_iota(jnp.int32, (1, size), 1)
    inverse_ref[...] = jnp.where(lane == line, 1.0, 0.0)

    def step(j, carry):
        values = gram_ref[...]
        pivot_row = gram_ref[pl.ds(j, 1), :]
        pivot = jnp.sum(jnp.where(first == j, pivot_row, 0.0), axis=1, keepdims=True)
        scale = 1.0 / jnp.sqrt(pivot)
        column = jnp.sum(jnp.where(lane == j, values, 0.0), axis=1, keepdims=True)
        column = jnp.where(line > j, column * scale, 0.0)
        gram_ref[...] = values - column * (pivot_row * scale)
        own_row = inverse_ref[pl.ds(j, 1), :] * scale
        inverse_ref[...] = jnp.where(line == j, own_row, inverse_ref[...] - column * own_row)
        return carry

    lax.fori_loop(0, size, step, 0)


def newton(gram, inverse_ref):
    size = gram.shape[0]
    line = lax.broadcasted_iota(jnp.int32, (size, size), 0)
    lane = lax.broadcasted_iota(jnp.int32, (size, size), 1)
    same = line == lane
    eye = jnp.where(same, 1.0, 0.0)
    take = jnp.where(line > lane, 1.0, jnp.where(same, 0.5, 0.0))
    diagonal = jnp.where(same, gram, 0.0)
    down = 1.0 / jnp.sqrt(jnp.sum(diagonal, axis=1, keepdims=True))
    across = 1.0 / jnp.sqrt(jnp.sum(diagonal, axis=0, keepdims=True))
    beyond = gram * down * across - eye
    factor = eye - take * beyond
    for product, product_t in ((dot1, dot_t1), (dot1, dot_t1), (dot3, dot_t3)):
        left = factor - eye + product(factor, beyond)
        residual = factor.T - eye + product_t(left, factor)
        factor = factor - product(take * residual, factor)
    inverse_ref[...] = factor * across
    return jnp.max(jnp.sum(jnp.abs(residual), axis=1))


def last_kernel(plan, features, rows_ref, high_ref, low_ref, mine_ref, *rest):
    parts, (basis_ref, factors_ref) = rest[: 2 * plan.plane], rest[2 * plan.plane : 2 * plan.plane + 2]
    all_ref, product_ref, gram_ref, inverse_ref = rest[2 * plan.plane + 2 :]
    me = plan.me()
    documents, block, _ = high_ref.shape
    slots = high_ref.shape[2] // block
    gram = jnp.zeros(gram_ref.shape, F32)
    for p, ref in enumerate(parts):
        size = ref.shape[0]
        part = ref[...]
        all_ref[p * size : (p + 1) * size, :] = part
        gram += lax.dot_general(part, part, (((0,), (0,)), ((), ())), preferred_element_type=F32)
    gram = gram * (1.0 / features)
    residual = newton(gram, inverse_ref)
    for d in range(documents):
        picked = []
        for s in range(slots):
            for p in range(plan.pieces):
                at = pl.ds(plan.start(me, rows_ref[s, d], p), plan.piece)
                picked.append(all_ref[at, :])
        picked = jnp.concatenate(picked, axis=0)
        product_ref[d * block : (d + 1) * block, :] = dot(high_ref[d], picked) + dot(low_ref[d], picked)

    @pl.when(jnp.logical_not(residual < 1.5e-2))
    def _():
        gram_ref[...] = gram
        eliminate(gram_ref, inverse_ref)

    inverse = inverse_ref[...]
    basis_ref[...] = dot_t3(mine_ref[...], inverse)
    size = min(512, documents * block)
    for at in range(0, documents * block, size):
        factors_ref[at : at + size, :] = dot_t3(product_ref[at : at + size, :], inverse).astype(BF16)


def body(plan, blocks, rows, counts, sketch, weights):
    documents, slots, block, _ = blocks.shape
    columns = sketch.shape[1]
    features = weights.shape[0]
    half = features // 2
    chunk = half // plan.plane
    flat = plan.flat
    params = pltpu.CompilerParams(vmem_limit_bytes=VMEM_BYTES)
    shape = jax.ShapeDtypeStruct
    rows = rows.T
    parts = min(4, documents)

    keep, *send = pl.pallas_call(
        functools.partial(sum_kernel, plan),
        out_shape=(pltpu.VMEM((half, columns), F32),) + (pltpu.VMEM((chunk, columns), BF16),) * plan.plane,
        in_specs=[scalars(), scalars(), pl.BlockSpec(memory_space=pltpu.HBM), pl.BlockSpec(memory_space=pltpu.HBM)],
        out_specs=(whole(),) * (1 + plan.plane),
        scratch_shapes=[
            pltpu.VMEM((features, columns), F32),
            pltpu.VMEM(blocks.shape, BF16),
            pltpu.VMEM(sketch.shape, BF16),
            pltpu.SemaphoreType.DMA((parts, 2)),
        ],
        compiler_params=params,
        name="local_sum",
    )(in_hbm(rows), in_hbm(counts), in_hbm(blocks), in_hbm(sketch))

    tiles_shape = shape((documents, block, slots * block), BF16)
    high, low = pl.pallas_call(
        tiles_kernel,
        out_shape=(tiles_shape, tiles_shape),
        in_specs=[scalars(), scalars(), whole(), whole()],
        out_specs=(whole(), whole()),
        compiler_params=params,
        cost_estimate=pl.CostEstimate(flops=1 << 20, bytes_accessed=4 << 20, transcendentals=0),
        name="tiles",
    )(rows, counts, blocks, weights.reshape(features // block, block))

    order = list(range(1, plan.plane)) + [0]
    got = {p: plan.swap_cores(send[p]) for p in order}
    chip = {p: keep[p * chunk : (p + 1) * chunk] + got[p].astype(F32) for p in order}
    sent = [plan.swap_plane(chip[p].astype(BF16), p) for p in order[:-1]]
    sent, high, low = lax.optimization_barrier((sent, high, low))
    held = chip[0]
    for part in sent:
        held = held + part.astype(F32)
    held = held.reshape(plan.line, flat, columns)
    far_first = sorted(range(1, plan.line), key=lambda q: (-(q & -2), q))
    mine = held[0]
    for part in [plan.swap_line(held[q].astype(BF16), q) for q in far_first]:
        mine = mine + part.astype(F32)
    mine = mine * lax.dynamic_slice_in_dim(weights, plan.me() * flat, flat)[:, None]

    rounded = mine.astype(BF16)
    line = {q: plan.swap_line(rounded, q) for q in far_first}
    near = jnp.concatenate([rounded] + [line[q] for q in range(1, plan.line)], axis=0)
    own = [near] + [plan.swap_plane(near, p) for p in range(1, plan.plane)]
    other = [plan.swap_cores(part) for part in own]

    return pl.pallas_call(
        functools.partial(last_kernel, plan, features),
        out_shape=(shape((flat, columns), F32), shape((documents * block, columns), BF16)),
        in_specs=[scalars()] + [whole()] * (3 + 2 * plan.plane),
        out_specs=(whole(), whole()),
        scratch_shapes=[
            pltpu.VMEM((features, columns), BF16),
            pltpu.VMEM((documents * block, columns), F32),
            pltpu.VMEM((columns, columns), F32),
            pltpu.VMEM((columns, columns), F32),
        ],
        compiler_params=params,
        name="factors",
    )(rows, high, low, mine, *own, *other)


def solution(mesh):
    placed = (
        P(AXES, None, None, None),
        P(AXES, None),
        P(AXES),
        P(AXES, None),
        P(),
    )

    def run(blocks, rows, counts, sketch, weights):
        plan = Plan(mesh.shape["row"], mesh.shape["col"], weights.shape[0], blocks.shape[2])
        return jax.shard_map(
            functools.partial(body, plan),
            mesh=mesh,
            in_specs=placed,
            out_specs=(P(AXES, None), P(AXES, None)),
            check_vma=False,
        )(blocks, rows, counts, sketch, weights)

    return run
```

```python
import functools

import jax
import jax.numpy as jnp
from jax import lax
from jax.experimental import pallas as pl
from jax.experimental.pallas import tpu as pltpu
from jax.sharding import PartitionSpec as P

F32 = jnp.float32
BF16 = jnp.bfloat16
AXES = ("row", "col")
VMEM_BYTES = 48 * 1024 * 1024


def whole():
    return pl.BlockSpec(memory_space=pltpu.VMEM)


def in_hbm(value):
    return pltpu.with_memory_space_constraint(value, pltpu.HBM)


def scalars():
    return pl.BlockSpec(memory_space=pltpu.SMEM)


class Plan:
    def __init__(self, rows, cols, features, block):
        self.count = rows * cols
        self.cols = cols
        self.plane = cols
        self.line = rows // 2
        self.plane_bits = cols.bit_length() - 1
        assert self.plane * self.line * 2 == self.count and self.count & (self.count - 1) == 0
        self.flat = features // self.count
        self.piece = min(self.flat, block)
        self.pieces = block // self.piece
        per_slice = self.flat // self.piece
        self.slice_bits = per_slice.bit_length() - 1
        assert 1 << self.slice_bits == per_slice and self.piece * self.pieces == block

    def me(self):
        return lax.axis_index("row") * self.cols + lax.axis_index("col")

    def start(self, me, feature_block, piece):
        unit = feature_block * self.pieces + piece
        owner = unit >> self.slice_bits
        inside = unit & ((1 << self.slice_bits) - 1)
        apart = owner ^ me
        place = (apart & 1) * self.plane + ((apart >> 1) & (self.plane - 1))
        place = place * self.line + (apart >> (1 + self.plane_bits))
        return pl.multiple_of(place * self.flat + inside * self.piece, self.piece)

    def core(self):
        return lax.axis_index("col") & 1

    def swap(self, value, mask, cores=(0, 1)):
        return lax.ppermute(value, AXES, [(d, d ^ mask) for d in range(self.count) if d & 1 in cores])

    def swap_plane(self, value, member, cores=(0, 1)):
        return self.swap(value, member << 1, cores)

    def swap_line(self, value, member):
        return self.swap(value, member << (1 + self.plane_bits))


def sum_kernel(plan, rows_ref, counts_ref, blocks_ref, sketch_ref, keep_ref, *rest):
    send_refs, (total_ref, tiles_ref, docs_ref, sems) = rest[: plan.plane], rest[plan.plane :]
    me = plan.me()
    documents, slots, block, _ = tiles_ref.shape
    half = keep_ref.shape[0]
    parts = sems.shape[0]
    per = documents // parts
    copies = []
    for c in range(parts):
        tiles_at = pl.ds(c * per, per)
        docs_at = pl.ds(c * per * block, per * block)
        pair = (
            pltpu.make_async_copy(blocks_ref.at[tiles_at], tiles_ref.at[tiles_at], sems.at[c, 0]),
            pltpu.make_async_copy(sketch_ref.at[docs_at], docs_ref.at[docs_at], sems.at[c, 1]),
        )
        for copy in pair:
            copy.start()
        copies.append(pair)
    total_ref[...] = jnp.zeros_like(total_ref)
    for c in range(parts):
        for copy in copies[c]:
            copy.wait()
        for d in range(c * per, (c + 1) * per):
            docs = docs_ref[d * block : (d + 1) * block, :]
            terms = jnp.dot(tiles_ref[d].reshape(slots * block, block), docs, preferred_element_type=F32)
            for s in range(slots):
                term = jnp.where(s < counts_ref[d], terms[s * block : (s + 1) * block], 0.0)
                for p in range(plan.pieces):
                    at = pl.ds(plan.start(me, rows_ref[s, d], p), plan.piece)
                    total_ref[at, :] += term[p * plan.piece : (p + 1) * plan.piece]
    keep_ref[...] = total_ref[:half, :]
    for p, send_ref in enumerate(send_refs):
        size = send_ref.shape[0]
        send_ref[...] = total_ref[half + p * size : half + (p + 1) * size, :].astype(BF16)


def tiles_kernel(plan, rows_ref, counts_ref, blocks_ref, weights_ref, high_ref, low_ref, scale_ref, turned_ref):
    documents, slots, block, _ = blocks_ref.shape
    for d in range(documents):
        for s in range(slots):
            scale = weights_ref[pl.ds(rows_ref[s, d], 1), :]
            scale = jnp.where(s < counts_ref[d], scale, 0.0)
            high, low = split(blocks_ref[d, s].T.astype(F32) * scale)
            high_ref[d, :, s * block : (s + 1) * block] = high
            low_ref[d, :, s * block : (s + 1) * block] = low
    unit = plan.me() << plan.slice_bits
    lines = max(1, plan.flat // block)
    first = unit if plan.pieces == 1 else unit // plan.pieces
    for i in range(lines):
        line = weights_ref[pl.ds(first + i, 1), :]
        turned_ref[i * block : (i + 1) * block, :] = jnp.broadcast_to(line, (block, block)).T
    inside = 0 if plan.pieces == 1 else lax.rem(unit, plan.pieces) * plan.piece
    scale_ref[...] = turned_ref[pl.ds(pl.multiple_of(inside, plan.piece), plan.flat), :]


def plane_kernel(plan, keep_ref, *rest):
    steps = plan.plane
    parts = (rest[:steps], rest[steps : 2 * steps])
    held_ref, *send_refs = rest[2 * steps :]
    flat = plan.flat
    for core, refs in enumerate(parts):

        @pl.when(plan.core() == core)
        def _(refs=refs):
            for q in range(plan.line):
                at = slice(q * flat, (q + 1) * flat)
                total = keep_ref[at, :]
                for ref in refs:
                    total = total + ref[at, :].astype(F32)
                if q == 0:
                    held_ref[...] = total
                else:
                    send_refs[q - 1][...] = total.astype(BF16)


def line_kernel(held_ref, scale_ref, *rest):
    parts, (mine_ref, rounded_ref) = rest[:-2], rest[-2:]
    total = held_ref[...]
    for ref in parts:
        total = total + ref[...].astype(F32)
    total = total * scale_ref[...]
    mine_ref[...] = total
    rounded_ref[...] = total.astype(BF16)


def split(value):
    high = value.astype(BF16)
    return high, (value - high.astype(F32)).astype(BF16)


def dot_t(a, b):
    return lax.dot_general(a, b, (((1,), (1,)), ((), ())), preferred_element_type=F32)


def dot_t3(a, b):
    a_high, a_low = split(a)
    b_high, b_low = split(b)
    return dot_t(a_high, b_high) + (dot_t(a_high, b_low) + dot_t(a_low, b_high))


def dot3(a, b):
    a_high, a_low = split(a)
    b_high, b_low = split(b)
    return dot(a_high, b_high) + (dot(a_high, b_low) + dot(a_low, b_high))


def dot(a, b):
    return jnp.dot(a, b, preferred_element_type=F32)


def dot1(a, b):
    return dot(a.astype(BF16), b.astype(BF16))


def dot_t1(a, b):
    return dot_t(a.astype(BF16), b.astype(BF16))


def eliminate(gram_ref, inverse_ref):
    size = gram_ref.shape[0]
    lane = lax.broadcasted_iota(jnp.int32, (size, size), 1)
    line = lax.broadcasted_iota(jnp.int32, (size, 1), 0)
    first = lax.broadcasted_iota(jnp.int32, (1, size), 1)
    inverse_ref[...] = jnp.where(lane == line, 1.0, 0.0)

    def step(j, carry):
        values = gram_ref[...]
        pivot_row = gram_ref[pl.ds(j, 1), :]
        pivot = jnp.sum(jnp.where(first == j, pivot_row, 0.0), axis=1, keepdims=True)
        scale = 1.0 / jnp.sqrt(pivot)
        column = jnp.sum(jnp.where(lane == j, values, 0.0), axis=1, keepdims=True)
        column = jnp.where(line > j, column * scale, 0.0)
        gram_ref[...] = values - column * (pivot_row * scale)
        own_row = inverse_ref[pl.ds(j, 1), :] * scale
        inverse_ref[...] = jnp.where(line == j, own_row, inverse_ref[...] - column * own_row)
        return carry

    lax.fori_loop(0, size, step, 0)


def newton(gram, inverse_ref):
    size = gram.shape[0]
    line = lax.broadcasted_iota(jnp.int32, (size, size), 0)
    lane = lax.broadcasted_iota(jnp.int32, (size, size), 1)
    same = line == lane
    eye = jnp.where(same, 1.0, 0.0)
    take = jnp.where(line > lane, 1.0, jnp.where(same, 0.5, 0.0))
    diagonal = jnp.where(same, gram, 0.0)
    down = 1.0 / jnp.sqrt(jnp.sum(diagonal, axis=1, keepdims=True))
    across = 1.0 / jnp.sqrt(jnp.sum(diagonal, axis=0, keepdims=True))
    beyond = gram * down * across - eye
    factor = eye - take * beyond
    for product, product_t in ((dot1, dot_t1), (dot1, dot_t1), (dot3, dot_t3)):
        left = factor - eye + product(factor, beyond)
        residual = factor.T - eye + product_t(left, factor)
        factor = factor - product(take * residual, factor)
    inverse_ref[...] = factor * across
    return jnp.max(jnp.sum(jnp.abs(residual), axis=1))


def last_kernel(plan, features, rows_ref, high_ref, low_ref, mine_ref, *rest):
    parts, (basis_ref, factors_ref) = rest[: 2 * plan.plane], rest[2 * plan.plane : 2 * plan.plane + 2]
    all_ref, product_ref, gram_ref, inverse_ref = rest[2 * plan.plane + 2 :]
    me = plan.me()
    documents, block, _ = high_ref.shape
    slots = high_ref.shape[2] // block
    gram = jnp.zeros(gram_ref.shape, F32)
    for p, ref in enumerate(parts):
        size = ref.shape[0]
        part = ref[...]
        all_ref[p * size : (p + 1) * size, :] = part
        gram += lax.dot_general(part, part, (((0,), (0,)), ((), ())), preferred_element_type=F32)
    gram = gram * (1.0 / features)
    residual = newton(gram, inverse_ref)
    for d in range(documents):
        picked = []
        for s in range(slots):
            for p in range(plan.pieces):
                at = pl.ds(plan.start(me, rows_ref[s, d], p), plan.piece)
                picked.append(all_ref[at, :])
        picked = jnp.concatenate(picked, axis=0)
        product_ref[d * block : (d + 1) * block, :] = dot(high_ref[d], picked) + dot(low_ref[d], picked)

    @pl.when(jnp.logical_not(residual < 1.5e-2))
    def _():
        gram_ref[...] = gram
        eliminate(gram_ref, inverse_ref)

    inverse = inverse_ref[...]
    basis_ref[...] = dot_t3(mine_ref[...], inverse)
    size = min(512, documents * block)
    for at in range(0, documents * block, size):
        factors_ref[at : at + size, :] = dot_t3(product_ref[at : at + size, :], inverse).astype(BF16)


def body(plan, blocks, rows, counts, sketch, weights):
    documents, slots, block, _ = blocks.shape
    columns = sketch.shape[1]
    features = weights.shape[0]
    half = features // 2
    chunk = half // plan.plane
    flat = plan.flat
    params = pltpu.CompilerParams(vmem_limit_bytes=VMEM_BYTES)
    shape = jax.ShapeDtypeStruct
    rows = rows.T
    parts = min(4, documents)

    keep, *send = pl.pallas_call(
        functools.partial(sum_kernel, plan),
        out_shape=(pltpu.VMEM((half, columns), F32),) + (pltpu.VMEM((chunk, columns), BF16),) * plan.plane,
        in_specs=[scalars(), scalars(), pl.BlockSpec(memory_space=pltpu.HBM), pl.BlockSpec(memory_space=pltpu.HBM)],
        out_specs=(whole(),) * (1 + plan.plane),
        scratch_shapes=[
            pltpu.VMEM((features, columns), F32),
            pltpu.VMEM(blocks.shape, BF16),
            pltpu.VMEM(sketch.shape, BF16),
            pltpu.SemaphoreType.DMA((parts, 2)),
        ],
        compiler_params=params,
        name="local_sum",
    )(in_hbm(rows), in_hbm(counts), in_hbm(blocks), in_hbm(sketch))

    tiles_shape = shape((documents, block, slots * block), BF16)
    high, low, scale = pl.pallas_call(
        functools.partial(tiles_kernel, plan),
        out_shape=(tiles_shape, tiles_shape, shape((flat, columns), F32)),
        in_specs=[scalars(), scalars(), whole(), whole()],
        out_specs=(whole(),) * 3,
        scratch_shapes=[pltpu.VMEM((max(flat, block), block), F32)],
        compiler_params=params,
        cost_estimate=pl.CostEstimate(flops=1 << 20, bytes_accessed=4 << 20, transcendentals=0),
        name="tiles",
    )(rows, counts, blocks, weights.reshape(features // block, block))

    order = list(range(1, plan.plane)) + [0]
    sums = []
    for core in (0, 1):
        got = {p: plan.swap(send[p], 1, (1 - core,)) for p in order}
        chip = [(keep[p * chunk : (p + 1) * chunk] + got[p].astype(F32)).astype(BF16) for p in order[:-1]]
        sent = [plan.swap_plane(chip[p - 1], p, (core,)) for p in order[:-1]]
        sums += [got[0]] + sent
        if core == 0:
            send, sent[0] = lax.optimization_barrier((send, sent[0]))
    sums, high, low, scale = lax.optimization_barrier((sums, high, low, scale))
    held, *far = pl.pallas_call(
        functools.partial(plane_kernel, plan),
        grid=(1,),
        out_shape=(shape((flat, columns), F32),) + (shape((flat, columns), BF16),) * (plan.line - 1),
        in_specs=[pl.BlockSpec((chunk, columns), lambda i: (0, 0))] + [whole()] * (2 * plan.plane),
        out_specs=(whole(),) * plan.line,
        compiler_params=params,
        name="plane_sum",
    )(keep, *sums)
    far_first = sorted(range(1, plan.line), key=lambda q: (-(q & -2), q))
    mine, rounded = pl.pallas_call(
        line_kernel,
        out_shape=(shape((flat, columns), F32), shape((flat, columns), BF16)),
        in_specs=[whole()] * (1 + plan.line),
        out_specs=(whole(), whole()),
        compiler_params=params,
        name="line_sum",
    )(held, scale, *[plan.swap_line(far[q - 1], q) for q in far_first])

    line = {q: plan.swap_line(rounded, q) for q in far_first}
    near = jnp.concatenate([rounded] + [line[q] for q in range(1, plan.line)], axis=0)
    own = [near] + [plan.swap_plane(near, p) for p in range(1, plan.plane)]
    other = [plan.swap(part, 1) for part in own]

    return pl.pallas_call(
        functools.partial(last_kernel, plan, features),
        out_shape=(shape((flat, columns), F32), shape((documents * block, columns), BF16)),
        in_specs=[scalars()] + [whole()] * (3 + 2 * plan.plane),
        out_specs=(whole(), whole()),
        scratch_shapes=[
            pltpu.VMEM((features, columns), BF16),
            pltpu.VMEM((documents * block, columns), F32),
            pltpu.VMEM((columns, columns), F32),
            pltpu.VMEM((columns, columns), F32),
        ],
        compiler_params=params,
        name="factors",
    )(rows, high, low, mine, *own, *other)


def solution(mesh):
    placed = (
        P(AXES, None, None, None),
        P(AXES, None),
        P(AXES),
        P(AXES, None),
        P(),
    )

    def run(blocks, rows, counts, sketch, weights):
        plan = Plan(mesh.shape["row"], mesh.shape["col"], weights.shape[0], blocks.shape[2])
        return jax.shard_map(
            functools.partial(body, plan),
            mesh=mesh,
            in_specs=placed,
            out_specs=(P(AXES, None), P(AXES, None)),
            check_vma=False,
        )(blocks, rows, counts, sketch, weights)

    return run
```

```python
import functools

import jax
import jax.numpy as jnp
from jax import lax
from jax.experimental import pallas as pl
from jax.experimental.pallas import tpu as pltpu
from jax.sharding import PartitionSpec as P

F32 = jnp.float32
BF16 = jnp.bfloat16
AXES = ("row", "col")
VMEM_BYTES = 48 * 1024 * 1024


def whole():
    return pl.BlockSpec(memory_space=pltpu.VMEM)


def in_hbm(value):
    return pltpu.with_memory_space_constraint(value, pltpu.HBM)


def scalars():
    return pl.BlockSpec(memory_space=pltpu.SMEM)


class Plan:
    def __init__(self, rows, cols, features, block):
        self.count = rows * cols
        self.cols = cols
        self.plane = cols
        self.line = rows // 2
        self.plane_bits = cols.bit_length() - 1
        assert self.plane * self.line * 2 == self.count and self.count & (self.count - 1) == 0
        self.flat = features // self.count
        self.piece = min(self.flat, block)
        self.pieces = block // self.piece
        per_slice = self.flat // self.piece
        self.slice_bits = per_slice.bit_length() - 1
        assert 1 << self.slice_bits == per_slice and self.piece * self.pieces == block

    def me(self):
        return lax.axis_index("row") * self.cols + lax.axis_index("col")

    def start(self, me, feature_block, piece):
        unit = feature_block * self.pieces + piece
        owner = unit >> self.slice_bits
        inside = unit & ((1 << self.slice_bits) - 1)
        apart = owner ^ me
        place = (apart & 1) * self.plane + ((apart >> 1) & (self.plane - 1))
        place = place * self.line + (apart >> (1 + self.plane_bits))
        return pl.multiple_of(place * self.flat + inside * self.piece, self.piece)

    def swap(self, value, mask):
        return lax.ppermute(value, AXES, [(d, d ^ mask) for d in range(self.count)])

    def swap_plane(self, value, member):
        return self.swap(value, member << 1)

    def swap_line(self, value, member):
        return self.swap(value, member << (1 + self.plane_bits))


def sum_kernel(plan, rows_ref, counts_ref, blocks_ref, sketch_ref, keep_ref, *rest):
    send_refs, (total_ref, tiles_ref, docs_ref, sems) = rest[: plan.plane], rest[plan.plane :]
    me = plan.me()
    documents, slots, block, _ = tiles_ref.shape
    half = keep_ref.shape[0]
    parts = sems.shape[0]
    per = documents // parts
    copies = []
    for c in range(parts):
        tiles_at = pl.ds(c * per, per)
        docs_at = pl.ds(c * per * block, per * block)
        pair = (
            pltpu.make_async_copy(blocks_ref.at[tiles_at], tiles_ref.at[tiles_at], sems.at[c, 0]),
            pltpu.make_async_copy(sketch_ref.at[docs_at], docs_ref.at[docs_at], sems.at[c, 1]),
        )
        for copy in pair:
            copy.start()
        copies.append(pair)
    total_ref[...] = jnp.zeros_like(total_ref)
    for c in range(parts):
        for copy in copies[c]:
            copy.wait()
        for d in range(c * per, (c + 1) * per):
            docs = docs_ref[d * block : (d + 1) * block, :]
            terms = jnp.dot(tiles_ref[d].reshape(slots * block, block), docs, preferred_element_type=F32)
            for s in range(slots):
                term = jnp.where(s < counts_ref[d], terms[s * block : (s + 1) * block], 0.0)
                for p in range(plan.pieces):
                    at = pl.ds(plan.start(me, rows_ref[s, d], p), plan.piece)
                    total_ref[at, :] += term[p * plan.piece : (p + 1) * plan.piece]
    keep_ref[...] = total_ref[:half, :]
    for p, send_ref in enumerate(send_refs):
        size = send_ref.shape[0]
        send_ref[...] = total_ref[half + p * size : half + (p + 1) * size, :].astype(BF16)


def tiles_kernel(plan, rows_ref, counts_ref, blocks_ref, weights_ref, high_ref, low_ref, scale_ref, turned_ref):
    documents, slots, block, _ = blocks_ref.shape
    for d in range(documents):
        for s in range(slots):
            scale = weights_ref[pl.ds(rows_ref[s, d], 1), :]
            scale = jnp.where(s < counts_ref[d], scale, 0.0)
            high, low = split(blocks_ref[d, s].T.astype(F32) * scale)
            high_ref[d, :, s * block : (s + 1) * block] = high
            low_ref[d, :, s * block : (s + 1) * block] = low
    unit = plan.me() << plan.slice_bits
    lines = max(1, plan.flat // block)
    first = unit if plan.pieces == 1 else unit // plan.pieces
    for i in range(lines):
        line = weights_ref[pl.ds(first + i, 1), :]
        turned_ref[i * block : (i + 1) * block, :] = jnp.broadcast_to(line, (block, block)).T
    inside = 0 if plan.pieces == 1 else lax.rem(unit, plan.pieces) * plan.piece
    scale_ref[...] = turned_ref[pl.ds(pl.multiple_of(inside, plan.piece), plan.flat), :]


def plane_kernel(flat, keep_ref, got_ref, *rest):
    count = keep_ref.shape[0] // flat
    parts, out_refs = (got_ref,) + rest[:-count], rest[-count:]
    for q, out_ref in enumerate(out_refs):
        at = slice(q * flat, (q + 1) * flat)
        total = keep_ref[at, :]
        for ref in parts:
            total = total + ref[at, :].astype(F32)
        out_ref[...] = total.astype(out_ref.dtype)


def line_kernel(held_ref, scale_ref, *rest):
    parts, (mine_ref, rounded_ref) = rest[:-2], rest[-2:]
    total = held_ref[...]
    for ref in parts:
        total = total + ref[...].astype(F32)
    total = total * scale_ref[...]
    mine_ref[...] = total
    rounded_ref[...] = total.astype(BF16)


def split(value):
    high = value.astype(BF16)
    return high, (value - high.astype(F32)).astype(BF16)


def dot_t(a, b):
    return lax.dot_general(a, b, (((1,), (1,)), ((), ())), preferred_element_type=F32)


def dot_t3(a, b):
    a_high, a_low = split(a)
    b_high, b_low = split(b)
    return dot_t(a_high, b_high) + (dot_t(a_high, b_low) + dot_t(a_low, b_high))


def dot3(a, b):
    a_high, a_low = split(a)
    b_high, b_low = split(b)
    return dot(a_high, b_high) + (dot(a_high, b_low) + dot(a_low, b_high))


def dot(a, b):
    return jnp.dot(a, b, preferred_element_type=F32)


def dot1(a, b):
    return dot(a.astype(BF16), b.astype(BF16))


def dot_t1(a, b):
    return dot_t(a.astype(BF16), b.astype(BF16))


def eliminate(gram_ref, inverse_ref):
    size = gram_ref.shape[0]
    lane = lax.broadcasted_iota(jnp.int32, (size, size), 1)
    line = lax.broadcasted_iota(jnp.int32, (size, 1), 0)
    first = lax.broadcasted_iota(jnp.int32, (1, size), 1)
    inverse_ref[...] = jnp.where(lane == line, 1.0, 0.0)

    def step(j, carry):
        values = gram_ref[...]
        pivot_row = gram_ref[pl.ds(j, 1), :]
        pivot = jnp.sum(jnp.where(first == j, pivot_row, 0.0), axis=1, keepdims=True)
        scale = 1.0 / jnp.sqrt(pivot)
        column = jnp.sum(jnp.where(lane == j, values, 0.0), axis=1, keepdims=True)
        column = jnp.where(line > j, column * scale, 0.0)
        gram_ref[...] = values - column * (pivot_row * scale)
        own_row = inverse_ref[pl.ds(j, 1), :] * scale
        inverse_ref[...] = jnp.where(line == j, own_row, inverse_ref[...] - column * own_row)
        return carry

    lax.fori_loop(0, size, step, 0)


def newton(gram, inverse_ref):
    size = gram.shape[0]
    line = lax.broadcasted_iota(jnp.int32, (size, size), 0)
    lane = lax.broadcasted_iota(jnp.int32, (size, size), 1)
    same = line == lane
    eye = jnp.where(same, 1.0, 0.0)
    take = jnp.where(line > lane, 1.0, jnp.where(same, 0.5, 0.0))
    diagonal = jnp.where(same, gram, 0.0)
    down = 1.0 / jnp.sqrt(jnp.sum(diagonal, axis=1, keepdims=True))
    across = 1.0 / jnp.sqrt(jnp.sum(diagonal, axis=0, keepdims=True))
    beyond = gram * down * across - eye
    factor = eye - take * beyond
    for product, product_t in ((dot1, dot_t1), (dot1, dot_t1), (dot3, dot_t3)):
        left = factor - eye + product(factor, beyond)
        residual = factor.T - eye + product_t(left, factor)
        factor = factor - product(take * residual, factor)
    inverse_ref[...] = factor * across
    return jnp.max(jnp.sum(jnp.abs(residual), axis=1))


def last_kernel(plan, features, rows_ref, high_ref, low_ref, mine_ref, *rest):
    parts, (basis_ref, factors_ref) = rest[: 4 * plan.plane], rest[4 * plan.plane : 4 * plan.plane + 2]
    all_ref, product_ref, gram_ref, inverse_ref = rest[4 * plan.plane + 2 :]
    me = plan.me()
    documents, block, _ = high_ref.shape
    slots = high_ref.shape[2] // block
    gram = jnp.zeros(gram_ref.shape, F32)
    for p, ref in enumerate(parts):
        size = ref.shape[0]
        part = ref[...]
        all_ref[p * size : (p + 1) * size, :] = part
        gram += lax.dot_general(part, part, (((0,), (0,)), ((), ())), preferred_element_type=F32)
    gram = gram * (1.0 / features)
    residual = newton(gram, inverse_ref)
    for d in range(documents):
        picked = []
        for s in range(slots):
            for p in range(plan.pieces):
                at = pl.ds(plan.start(me, rows_ref[s, d], p), plan.piece)
                picked.append(all_ref[at, :])
        picked = jnp.concatenate(picked, axis=0)
        product_ref[d * block : (d + 1) * block, :] = dot(high_ref[d], picked) + dot(low_ref[d], picked)

    @pl.when(jnp.logical_not(residual < 1.5e-2))
    def _():
        gram_ref[...] = gram
        eliminate(gram_ref, inverse_ref)

    inverse = inverse_ref[...]
    basis_ref[...] = dot_t3(mine_ref[...], inverse)
    size = min(512, documents * block)
    for at in range(0, documents * block, size):
        factors_ref[at : at + size, :] = dot_t3(product_ref[at : at + size, :], inverse).astype(BF16)


def body(plan, blocks, rows, counts, sketch, weights):
    documents, slots, block, _ = blocks.shape
    columns = sketch.shape[1]
    features = weights.shape[0]
    half = features // 2
    chunk = half // plan.plane
    flat = plan.flat
    params = pltpu.CompilerParams(vmem_limit_bytes=VMEM_BYTES)
    shape = jax.ShapeDtypeStruct
    rows = rows.T
    parts = min(4, documents)

    keep, *send = pl.pallas_call(
        functools.partial(sum_kernel, plan),
        out_shape=(pltpu.VMEM((half, columns), F32),) + (pltpu.VMEM((chunk, columns), BF16),) * plan.plane,
        in_specs=[scalars(), scalars(), pl.BlockSpec(memory_space=pltpu.HBM), pl.BlockSpec(memory_space=pltpu.HBM)],
        out_specs=(whole(),) * (1 + plan.plane),
        scratch_shapes=[
            pltpu.VMEM((features, columns), F32),
            pltpu.VMEM(blocks.shape, BF16),
            pltpu.VMEM(sketch.shape, BF16),
            pltpu.SemaphoreType.DMA((parts, 2)),
        ],
        compiler_params=params,
        name="local_sum",
    )(in_hbm(rows), in_hbm(counts), in_hbm(blocks), in_hbm(sketch))

    tiles_shape = shape((documents, block, slots * block), BF16)
    high, low, scale = pl.pallas_call(
        functools.partial(tiles_kernel, plan),
        out_shape=(tiles_shape, tiles_shape, shape((flat, columns), F32)),
        in_specs=[scalars(), scalars(), whole(), whole()],
        out_specs=(whole(),) * 3,
        scratch_shapes=[pltpu.VMEM((max(flat, block), block), F32)],
        compiler_params=params,
        cost_estimate=pl.CostEstimate(flops=1 << 20, bytes_accessed=4 << 20, transcendentals=0),
        name="tiles",
    )(rows, counts, blocks, weights.reshape(features // block, block))

    middle = chunk // 2
    others = range(1, plan.plane)
    got = {p: plan.swap(send[p], 1) for p in (*others, 0)}
    chip = [(keep[p * chunk : (p + 1) * chunk] + got[p].astype(F32)).astype(BF16) for p in others]
    far_sent = [plan.swap_plane(chip[p - 1][middle:], p) for p in others]
    near_sent = [plan.swap_plane(chip[p - 1][:middle], p) for p in others]
    near_sent, high, low, scale = lax.optimization_barrier((near_sent, high, low, scale))

    def plane_sum(sent, at, dtypes):
        return pl.pallas_call(
            functools.partial(plane_kernel, flat),
            grid=(1,),
            out_shape=[shape((flat, columns), dtype) for dtype in dtypes],
            in_specs=[pl.BlockSpec((middle, columns), lambda i: (at, 0))] * 2 + [whole()] * len(sent),
            out_specs=[whole()] * len(dtypes),
            compiler_params=params,
            name="plane_sum",
        )(keep, got[0], *sent)

    split_at = plan.line // 2
    far = plane_sum(far_sent, 1, [BF16] * split_at)
    far = [plan.swap_line(part, split_at + q) for q, part in enumerate(far)]
    held, *near = plane_sum(near_sent, 0, [F32] + [BF16] * (split_at - 1))
    near = [plan.swap_line(part, 1 + q) for q, part in enumerate(near)]
    mine, rounded = pl.pallas_call(
        line_kernel,
        out_shape=(shape((flat, columns), F32), shape((flat, columns), BF16)),
        in_specs=[whole()] * (1 + plan.line),
        out_specs=(whole(), whole()),
        compiler_params=params,
        name="line_sum",
    )(held, scale, *near, *far)

    line = [rounded] + [plan.swap_line(rounded, q) for q in range(1, plan.line)]
    near, far = jnp.concatenate(line[:split_at], axis=0), jnp.concatenate(line[split_at:], axis=0)
    own = [near, far]
    near = [plan.swap_plane(near, p) for p in others]
    far = [plan.swap_plane(far, p) for p in others]
    for pair in zip(near, far):
        own += pair
    other = [plan.swap(part, 1) for part in own]

    return pl.pallas_call(
        functools.partial(last_kernel, plan, features),
        out_shape=(shape((flat, columns), F32), shape((documents * block, columns), BF16)),
        in_specs=[scalars()] + [whole()] * (3 + 4 * plan.plane),
        out_specs=(whole(), whole()),
        scratch_shapes=[
            pltpu.VMEM((features, columns), BF16),
            pltpu.VMEM((documents * block, columns), F32),
            pltpu.VMEM((columns, columns), F32),
            pltpu.VMEM((columns, columns), F32),
        ],
        compiler_params=params,
        name="factors",
    )(rows, high, low, mine, *own, *other)


def solution(mesh):
    placed = (
        P(AXES, None, None, None),
        P(AXES, None),
        P(AXES),
        P(AXES, None),
        P(),
    )

    def run(blocks, rows, counts, sketch, weights):
        plan = Plan(mesh.shape["row"], mesh.shape["col"], weights.shape[0], blocks.shape[2])
        return jax.shard_map(
            functools.partial(body, plan),
            mesh=mesh,
            in_specs=placed,
            out_specs=(P(AXES, None), P(AXES, None)),
            check_vma=False,
        )(blocks, rows, counts, sketch, weights)

    return run
```

```python
import functools

import jax
import jax.numpy as jnp
from jax import lax
from jax.experimental import pallas as pl
from jax.experimental.pallas import tpu as pltpu
from jax.sharding import PartitionSpec as P

F32 = jnp.float32
BF16 = jnp.bfloat16
AXES = ("row", "col")
VMEM_BYTES = 48 * 1024 * 1024


def whole():
    return pl.BlockSpec(memory_space=pltpu.VMEM)


def in_hbm(value):
    return pltpu.with_memory_space_constraint(value, pltpu.HBM)


def scalars():
    return pl.BlockSpec(memory_space=pltpu.SMEM)


class Plan:
    def __init__(self, rows, cols, features, block):
        self.count = rows * cols
        self.cols = cols
        self.plane = cols
        self.line = rows // 2
        self.plane_bits = cols.bit_length() - 1
        assert self.plane * self.line * 2 == self.count and self.count & (self.count - 1) == 0
        self.flat = features // self.count
        self.piece = min(self.flat, block)
        self.pieces = block // self.piece
        per_slice = self.flat // self.piece
        self.slice_bits = per_slice.bit_length() - 1
        assert 1 << self.slice_bits == per_slice and self.piece * self.pieces == block

    def me(self):
        return lax.axis_index("row") * self.cols + lax.axis_index("col")

    def start(self, me, feature_block, piece):
        unit = feature_block * self.pieces + piece
        owner = unit >> self.slice_bits
        inside = unit & ((1 << self.slice_bits) - 1)
        apart = owner ^ me
        place = (apart & 1) * self.plane + ((apart >> 1) & (self.plane - 1))
        place = place * self.line + (apart >> (1 + self.plane_bits))
        return pl.multiple_of(place * self.flat + inside * self.piece, self.piece)

    def swap(self, value, mask):
        return lax.ppermute(value, AXES, [(d, d ^ mask) for d in range(self.count)])

    def swap_plane(self, value, member):
        return self.swap(value, member << 1)

    def swap_line(self, value, member):
        return self.swap(value, member << (1 + self.plane_bits))


def sum_kernel(plan, rows_ref, counts_ref, blocks_ref, sketch_ref, keep_ref, *rest):
    send_refs, (total_ref, tiles_ref, docs_ref, sems) = rest[: plan.plane], rest[plan.plane :]
    me = plan.me()
    documents, slots, block, _ = tiles_ref.shape
    half = keep_ref.shape[0]
    parts = sems.shape[0]
    per = documents // parts
    copies = []
    for c in range(parts):
        tiles_at = pl.ds(c * per, per)
        docs_at = pl.ds(c * per * block, per * block)
        pair = (
            pltpu.make_async_copy(blocks_ref.at[tiles_at], tiles_ref.at[tiles_at], sems.at[c, 0]),
            pltpu.make_async_copy(sketch_ref.at[docs_at], docs_ref.at[docs_at], sems.at[c, 1]),
        )
        for copy in pair:
            copy.start()
        copies.append(pair)
    total_ref[...] = jnp.zeros_like(total_ref)
    for c in range(parts):
        for copy in copies[c]:
            copy.wait()
        for d in range(c * per, (c + 1) * per):
            docs = docs_ref[d * block : (d + 1) * block, :]
            terms = jnp.dot(tiles_ref[d].reshape(slots * block, block), docs, preferred_element_type=F32)
            for s in range(slots):
                term = jnp.where(s < counts_ref[d], terms[s * block : (s + 1) * block], 0.0)
                for p in range(plan.pieces):
                    at = pl.ds(plan.start(me, rows_ref[s, d], p), plan.piece)
                    total_ref[at, :] += term[p * plan.piece : (p + 1) * plan.piece]
    keep_ref[...] = total_ref[:half, :]
    for p, send_ref in enumerate(send_refs):
        size = send_ref.shape[0]
        send_ref[...] = total_ref[half + p * size : half + (p + 1) * size, :].astype(BF16)


def tiles_kernel(rows_ref, counts_ref, blocks_ref, weights_ref, high_ref, low_ref):
    documents, slots, block, _ = blocks_ref.shape
    for d in range(documents):
        for s in range(slots):
            scale = weights_ref[pl.ds(rows_ref[s, d], 1), :]
            scale = jnp.where(s < counts_ref[d], scale, 0.0)
            high, low = split(blocks_ref[d, s].T.astype(F32) * scale)
            high_ref[d, :, s * block : (s + 1) * block] = high
            low_ref[d, :, s * block : (s + 1) * block] = low


def scale_kernel(plan, weights_ref, scale_ref, turned_ref):
    block = weights_ref.shape[1]
    unit = plan.me() << plan.slice_bits
    lines = max(1, plan.flat // block)
    first = unit if plan.pieces == 1 else unit // plan.pieces
    for i in range(lines):
        line = weights_ref[pl.ds(first + i, 1), :]
        turned_ref[i * block : (i + 1) * block, :] = jnp.broadcast_to(line, (block, block)).T
    inside = 0 if plan.pieces == 1 else lax.rem(unit, plan.pieces) * plan.piece
    scale_ref[...] = turned_ref[pl.ds(pl.multiple_of(inside, plan.piece), plan.flat), :]


def plane_kernel(flat, keep_ref, got_ref, *rest):
    count = keep_ref.shape[0] // flat
    parts, out_refs = (got_ref,) + rest[:-count], rest[-count:]
    for q, out_ref in enumerate(out_refs):
        at = slice(q * flat, (q + 1) * flat)
        total = keep_ref[at, :]
        for ref in parts:
            total = total + ref[at, :].astype(F32)
        out_ref[...] = total.astype(out_ref.dtype)


def line_kernel(held_ref, scale_ref, *rest):
    parts, (mine_ref, rounded_ref) = rest[:-2], rest[-2:]
    total = held_ref[...]
    for ref in parts:
        total = total + ref[...].astype(F32)
    total = total * scale_ref[...]
    mine_ref[...] = total
    rounded_ref[...] = total.astype(BF16)


def split(value):
    high = value.astype(BF16)
    return high, (value - high.astype(F32)).astype(BF16)


def dot_t(a, b):
    return lax.dot_general(a, b, (((1,), (1,)), ((), ())), preferred_element_type=F32)


def dot_t3(a, b):
    a_high, a_low = split(a)
    b_high, b_low = split(b)
    return dot_t(a_high, b_high) + (dot_t(a_high, b_low) + dot_t(a_low, b_high))


def dot3(a, b):
    a_high, a_low = split(a)
    b_high, b_low = split(b)
    return dot(a_high, b_high) + (dot(a_high, b_low) + dot(a_low, b_high))


def dot(a, b):
    return jnp.dot(a, b, preferred_element_type=F32)


def dot1(a, b):
    return dot(a.astype(BF16), b.astype(BF16))


def dot_t1(a, b):
    return dot_t(a.astype(BF16), b.astype(BF16))


def eliminate(gram_ref, inverse_ref):
    size = gram_ref.shape[0]
    lane = lax.broadcasted_iota(jnp.int32, (size, size), 1)
    line = lax.broadcasted_iota(jnp.int32, (size, 1), 0)
    first = lax.broadcasted_iota(jnp.int32, (1, size), 1)
    inverse_ref[...] = jnp.where(lane == line, 1.0, 0.0)

    def step(j, carry):
        values = gram_ref[...]
        pivot_row = gram_ref[pl.ds(j, 1), :]
        pivot = jnp.sum(jnp.where(first == j, pivot_row, 0.0), axis=1, keepdims=True)
        scale = 1.0 / jnp.sqrt(pivot)
        column = jnp.sum(jnp.where(lane == j, values, 0.0), axis=1, keepdims=True)
        column = jnp.where(line > j, column * scale, 0.0)
        gram_ref[...] = values - column * (pivot_row * scale)
        own_row = inverse_ref[pl.ds(j, 1), :] * scale
        inverse_ref[...] = jnp.where(line == j, own_row, inverse_ref[...] - column * own_row)
        return carry

    lax.fori_loop(0, size, step, 0)


def newton(gram, inverse_ref):
    size = gram.shape[0]
    line = lax.broadcasted_iota(jnp.int32, (size, size), 0)
    lane = lax.broadcasted_iota(jnp.int32, (size, size), 1)
    same = line == lane
    eye = jnp.where(same, 1.0, 0.0)
    take = jnp.where(line > lane, 1.0, jnp.where(same, 0.5, 0.0))
    diagonal = jnp.where(same, gram, 0.0)
    down = 1.0 / jnp.sqrt(jnp.sum(diagonal, axis=1, keepdims=True))
    across = 1.0 / jnp.sqrt(jnp.sum(diagonal, axis=0, keepdims=True))
    beyond = gram * down * across - eye
    factor = eye - take * beyond
    for product, product_t in ((dot1, dot_t1), (dot1, dot_t1), (dot3, dot_t3)):
        left = factor - eye + product(factor, beyond)
        residual = factor.T - eye + product_t(left, factor)
        factor = factor - product(take * residual, factor)
    inverse_ref[...] = factor * across
    return jnp.max(jnp.sum(jnp.abs(residual), axis=1))


def last_kernel(plan, features, rows_ref, high_ref, low_ref, mine_ref, *rest):
    parts, (basis_ref, factors_ref) = rest[: 4 * plan.plane], rest[4 * plan.plane : 4 * plan.plane + 2]
    all_ref, product_ref, gram_ref, inverse_ref = rest[4 * plan.plane + 2 :]
    me = plan.me()
    documents, block, _ = high_ref.shape
    slots = high_ref.shape[2] // block
    gram = jnp.zeros(gram_ref.shape, F32)
    for i, ref in enumerate(parts):
        size = ref.shape[0]
        core, later = divmod(i, 2 * plan.plane)
        near, member = divmod(later, plan.plane)
        base = ((core * plan.plane + member) * 2 + 1 - near) * size
        part = ref[...]
        all_ref[base : base + size, :] = part
        gram += lax.dot_general(part, part, (((0,), (0,)), ((), ())), preferred_element_type=F32)
    gram = gram * (1.0 / features)
    residual = newton(gram, inverse_ref)
    for d in range(documents):
        picked = []
        for s in range(slots):
            for p in range(plan.pieces):
                at = pl.ds(plan.start(me, rows_ref[s, d], p), plan.piece)
                picked.append(all_ref[at, :])
        picked = jnp.concatenate(picked, axis=0)
        product_ref[d * block : (d + 1) * block, :] = dot(high_ref[d], picked) + dot(low_ref[d], picked)

    @pl.when(jnp.logical_not(residual < 1.5e-2))
    def _():
        gram_ref[...] = gram
        eliminate(gram_ref, inverse_ref)

    inverse = inverse_ref[...]
    basis_ref[...] = dot_t3(mine_ref[...], inverse)
    size = min(512, documents * block)
    for at in range(0, documents * block, size):
        factors_ref[at : at + size, :] = dot_t3(product_ref[at : at + size, :], inverse).astype(BF16)


def body(plan, blocks, rows, counts, sketch, weights):
    documents, slots, block, _ = blocks.shape
    columns = sketch.shape[1]
    features = weights.shape[0]
    half = features // 2
    chunk = half // plan.plane
    flat = plan.flat
    params = pltpu.CompilerParams(vmem_limit_bytes=VMEM_BYTES)
    shape = jax.ShapeDtypeStruct
    rows = rows.T
    parts = min(4, documents)

    keep, *send = pl.pallas_call(
        functools.partial(sum_kernel, plan),
        out_shape=(pltpu.VMEM((half, columns), F32),) + (pltpu.VMEM((chunk, columns), BF16),) * plan.plane,
        in_specs=[scalars(), scalars(), pl.BlockSpec(memory_space=pltpu.HBM), pl.BlockSpec(memory_space=pltpu.HBM)],
        out_specs=(whole(),) * (1 + plan.plane),
        scratch_shapes=[
            pltpu.VMEM((features, columns), F32),
            pltpu.VMEM(blocks.shape, BF16),
            pltpu.VMEM(sketch.shape, BF16),
            pltpu.SemaphoreType.DMA((parts, 2)),
        ],
        compiler_params=params,
        name="local_sum",
    )(in_hbm(rows), in_hbm(counts), in_hbm(blocks), in_hbm(sketch))

    tiles_shape = shape((documents, block, slots * block), BF16)
    lines = weights.reshape(features // block, block)
    high, low = pl.pallas_call(
        tiles_kernel,
        out_shape=(tiles_shape, tiles_shape),
        in_specs=[scalars(), scalars(), whole(), whole()],
        out_specs=(whole(), whole()),
        compiler_params=params,
        cost_estimate=pl.CostEstimate(flops=1 << 20, bytes_accessed=4 << 20, transcendentals=0),
        name="tiles",
    )(rows, counts, blocks, lines)
    scale = pl.pallas_call(
        functools.partial(scale_kernel, plan),
        out_shape=shape((flat, columns), F32),
        in_specs=[whole()],
        out_specs=whole(),
        scratch_shapes=[pltpu.VMEM((max(flat, block), block), F32)],
        compiler_params=params,
        name="scale",
    )(lines)

    middle = chunk // 2
    others = range(1, plan.plane)
    got = {p: plan.swap(send[p], 1) for p in (*others, 0)}
    chip = [(keep[p * chunk : (p + 1) * chunk] + got[p].astype(F32)).astype(BF16) for p in others]
    chip, got[0] = lax.optimization_barrier((chip, got[0]))
    far_sent = [plan.swap_plane(chip[p - 1][middle:], p) for p in others]
    near_sent = [plan.swap_plane(chip[p - 1][:middle], p) for p in others]
    near_sent, scale = lax.optimization_barrier((near_sent, scale))

    def plane_sum(sent, at, dtypes):
        return pl.pallas_call(
            functools.partial(plane_kernel, flat),
            grid=(1,),
            out_shape=[shape((flat, columns), dtype) for dtype in dtypes],
            in_specs=[pl.BlockSpec((middle, columns), lambda i: (at, 0))] * 2 + [whole()] * len(sent),
            out_specs=[whole()] * len(dtypes),
            compiler_params=params,
            name="plane_sum",
        )(keep, got[0], *sent)

    split_at = plan.line // 2
    far = plane_sum(far_sent, 1, [BF16] * split_at)
    far = [plan.swap_line(part, split_at + q) for q, part in enumerate(far)]
    held, *near = plane_sum(near_sent, 0, [F32] + [BF16] * (split_at - 1))
    near = [plan.swap_line(part, 1 + q) for q, part in enumerate(near)]
    near, far, high, low = lax.optimization_barrier((near, far, high, low))
    mine, rounded = pl.pallas_call(
        line_kernel,
        out_shape=(shape((flat, columns), F32), shape((flat, columns), BF16)),
        in_specs=[whole()] * (1 + plan.line),
        out_specs=(whole(), whole()),
        compiler_params=params,
        name="line_sum",
    )(held, scale, *near, *far)

    line = [rounded] + [plan.swap_line(rounded, q) for q in range(1, plan.line)]
    near, far = jnp.concatenate(line[:split_at], axis=0), jnp.concatenate(line[split_at:], axis=0)
    near = [near] + [plan.swap_plane(near, p) for p in others]
    far = [far] + [plan.swap_plane(far, p) for p in others]
    own = far + near
    other = [plan.swap(part, 1) for part in own]

    return pl.pallas_call(
        functools.partial(last_kernel, plan, features),
        out_shape=(shape((flat, columns), F32), shape((documents * block, columns), BF16)),
        in_specs=[scalars()] + [whole()] * (3 + 4 * plan.plane),
        out_specs=(whole(), whole()),
        scratch_shapes=[
            pltpu.VMEM((features, columns), BF16),
            pltpu.VMEM((documents * block, columns), F32),
            pltpu.VMEM((columns, columns), F32),
            pltpu.VMEM((columns, columns), F32),
        ],
        compiler_params=params,
        name="factors",
    )(rows, high, low, mine, *own, *other)


def solution(mesh):
    placed = (
        P(AXES, None, None, None),
        P(AXES, None),
        P(AXES),
        P(AXES, None),
        P(),
    )

    def run(blocks, rows, counts, sketch, weights):
        plan = Plan(mesh.shape["row"], mesh.shape["col"], weights.shape[0], blocks.shape[2])
        return jax.shard_map(
            functools.partial(body, plan),
            mesh=mesh,
            in_specs=placed,
            out_specs=(P(AXES, None), P(AXES, None)),
            check_vma=False,
        )(blocks, rows, counts, sketch, weights)

    return run
```

```python
import functools

import jax
import jax.numpy as jnp
from jax import lax
from jax.experimental import pallas as pl
from jax.experimental.pallas import tpu as pltpu
from jax.sharding import PartitionSpec as P

F32 = jnp.float32
BF16 = jnp.bfloat16
AXES = ("row", "col")
VMEM_BYTES = 48 * 1024 * 1024


def whole():
    return pl.BlockSpec(memory_space=pltpu.VMEM)


def in_hbm(value):
    return pltpu.with_memory_space_constraint(value, pltpu.HBM)


def scalars():
    return pl.BlockSpec(memory_space=pltpu.SMEM)


class Plan:
    def __init__(self, rows, cols, features, block):
        self.count = rows * cols
        self.cols = cols
        self.plane = cols
        self.line = rows // 2
        self.plane_bits = cols.bit_length() - 1
        assert self.plane * self.line * 2 == self.count and self.count & (self.count - 1) == 0
        self.flat = features // self.count
        self.piece = min(self.flat, block)
        self.pieces = block // self.piece
        per_slice = self.flat // self.piece
        self.slice_bits = per_slice.bit_length() - 1
        assert 1 << self.slice_bits == per_slice and self.piece * self.pieces == block

    def me(self):
        return lax.axis_index("row") * self.cols + lax.axis_index("col")

    def start(self, me, feature_block, piece):
        unit = feature_block * self.pieces + piece
        owner = unit >> self.slice_bits
        inside = unit & ((1 << self.slice_bits) - 1)
        apart = owner ^ me
        place = (apart & 1) * self.plane + ((apart >> 1) & (self.plane - 1))
        place = place * self.line + (apart >> (1 + self.plane_bits))
        return pl.multiple_of(place * self.flat + inside * self.piece, self.piece)

    def swap(self, value, mask):
        return lax.ppermute(value, AXES, [(d, d ^ mask) for d in range(self.count)])

    def swap_plane(self, value, member):
        return self.swap(value, member << 1)

    def swap_line(self, value, member):
        return self.swap(value, member << (1 + self.plane_bits))


def sum_kernel(plan, rows_ref, counts_ref, blocks_ref, sketch_ref, total_ref, *rest):
    send_refs, (tiles_ref, docs_ref, sems) = rest[: plan.plane], rest[plan.plane :]
    me = plan.me()
    documents, slots, block, _ = tiles_ref.shape
    half = total_ref.shape[0] // 2
    parts = sems.shape[0]
    per = documents // parts
    copies = []
    for c in range(parts):
        tiles_at = pl.ds(c * per, per)
        docs_at = pl.ds(c * per * block, per * block)
        pair = (
            pltpu.make_async_copy(blocks_ref.at[tiles_at], tiles_ref.at[tiles_at], sems.at[c, 0]),
            pltpu.make_async_copy(sketch_ref.at[docs_at], docs_ref.at[docs_at], sems.at[c, 1]),
        )
        for copy in pair:
            copy.start()
        copies.append(pair)
    total_ref[...] = jnp.zeros_like(total_ref)
    for c in range(parts):
        for copy in copies[c]:
            copy.wait()
        for d in range(c * per, (c + 1) * per):
            docs = docs_ref[d * block : (d + 1) * block, :]
            terms = jnp.dot(tiles_ref[d].reshape(slots * block, block), docs, preferred_element_type=F32)
            for s in range(slots):
                term = jnp.where(s < counts_ref[d], terms[s * block : (s + 1) * block], 0.0)
                for p in range(plan.pieces):
                    at = pl.ds(plan.start(me, rows_ref[s, d], p), plan.piece)
                    total_ref[at, :] += term[p * plan.piece : (p + 1) * plan.piece]
    for p, send_ref in enumerate(send_refs):
        size = send_ref.shape[0]
        send_ref[...] = total_ref[half + p * size : half + (p + 1) * size, :].astype(BF16)


def tiles_kernel(rows_ref, counts_ref, blocks_ref, weights_ref, high_ref, low_ref):
    documents, slots, block, _ = blocks_ref.shape
    for d in range(documents):
        for s in range(slots):
            scale = weights_ref[pl.ds(rows_ref[s, d], 1), :]
            scale = jnp.where(s < counts_ref[d], scale, 0.0)
            high, low = split(blocks_ref[d, s].T.astype(F32) * scale)
            high_ref[d, :, s * block : (s + 1) * block] = high
            low_ref[d, :, s * block : (s + 1) * block] = low


def scale_kernel(plan, weights_ref, scale_ref, turned_ref):
    block = weights_ref.shape[1]
    unit = plan.me() << plan.slice_bits
    lines = max(1, plan.flat // block)
    first = unit if plan.pieces == 1 else unit // plan.pieces
    for i in range(lines):
        line = weights_ref[pl.ds(first + i, 1), :]
        turned_ref[i * block : (i + 1) * block, :] = jnp.broadcast_to(line, (block, block)).T
    inside = 0 if plan.pieces == 1 else lax.rem(unit, plan.pieces) * plan.piece
    scale_ref[...] = turned_ref[pl.ds(pl.multiple_of(inside, plan.piece), plan.flat), :]


def chip_kernel(start, total_ref, got_ref, far_ref, near_ref):
    middle = near_ref.shape[0]
    for ref, at in ((far_ref, middle), (near_ref, 0)):
        held = total_ref[start + at : start + at + middle, :]
        ref[...] = (held + got_ref[at : at + middle, :].astype(F32)).astype(BF16)


def plane_kernel(flat, start, total_ref, got_ref, *rest):
    count = rest[0].shape[0] // flat
    parts, out_refs = rest[:-count], rest[-count:]
    for q, out_ref in enumerate(out_refs):
        at = slice(start + q * flat, start + (q + 1) * flat)
        total = total_ref[at, :] + got_ref[at, :].astype(F32)
        for ref in parts:
            total = total + ref[q * flat : (q + 1) * flat, :].astype(F32)
        out_ref[...] = total.astype(out_ref.dtype)


def line_kernel(held_ref, scale_ref, *rest):
    parts, (mine_ref, rounded_ref) = rest[:-2], rest[-2:]
    total = held_ref[...]
    for ref in parts:
        total = total + ref[...].astype(F32)
    total = total * scale_ref[...]
    mine_ref[...] = total
    rounded_ref[...] = total.astype(BF16)


def split(value):
    high = value.astype(BF16)
    return high, (value - high.astype(F32)).astype(BF16)


def dot_t(a, b):
    return lax.dot_general(a, b, (((1,), (1,)), ((), ())), preferred_element_type=F32)


def dot_t3(a, b):
    a_high, a_low = split(a)
    b_high, b_low = split(b)
    return dot_t(a_high, b_high) + (dot_t(a_high, b_low) + dot_t(a_low, b_high))


def dot3(a, b):
    a_high, a_low = split(a)
    b_high, b_low = split(b)
    return dot(a_high, b_high) + (dot(a_high, b_low) + dot(a_low, b_high))


def dot(a, b):
    return jnp.dot(a, b, preferred_element_type=F32)


def dot1(a, b):
    return dot(a.astype(BF16), b.astype(BF16))


def dot_t1(a, b):
    return dot_t(a.astype(BF16), b.astype(BF16))


def eliminate(gram_ref, inverse_ref):
    size = gram_ref.shape[0]
    lane = lax.broadcasted_iota(jnp.int32, (size, size), 1)
    line = lax.broadcasted_iota(jnp.int32, (size, 1), 0)
    first = lax.broadcasted_iota(jnp.int32, (1, size), 1)
    inverse_ref[...] = jnp.where(lane == line, 1.0, 0.0)

    def step(j, carry):
        values = gram_ref[...]
        pivot_row = gram_ref[pl.ds(j, 1), :]
        pivot = jnp.sum(jnp.where(first == j, pivot_row, 0.0), axis=1, keepdims=True)
        scale = 1.0 / jnp.sqrt(pivot)
        column = jnp.sum(jnp.where(lane == j, values, 0.0), axis=1, keepdims=True)
        column = jnp.where(line > j, column * scale, 0.0)
        gram_ref[...] = values - column * (pivot_row * scale)
        own_row = inverse_ref[pl.ds(j, 1), :] * scale
        inverse_ref[...] = jnp.where(line == j, own_row, inverse_ref[...] - column * own_row)
        return carry

    lax.fori_loop(0, size, step, 0)


def newton(gram, inverse_ref):
    size = gram.shape[0]
    line = lax.broadcasted_iota(jnp.int32, (size, size), 0)
    lane = lax.broadcasted_iota(jnp.int32, (size, size), 1)
    same = line == lane
    eye = jnp.where(same, 1.0, 0.0)
    take = jnp.where(line > lane, 1.0, jnp.where(same, 0.5, 0.0))
    diagonal = jnp.where(same, gram, 0.0)
    down = 1.0 / jnp.sqrt(jnp.sum(diagonal, axis=1, keepdims=True))
    across = 1.0 / jnp.sqrt(jnp.sum(diagonal, axis=0, keepdims=True))
    beyond = gram * down * across - eye
    factor = eye - take * beyond
    for product, product_t in ((dot1, dot_t1), (dot1, dot_t1), (dot3, dot_t3)):
        left = factor - eye + product(factor, beyond)
        residual = factor.T - eye + product_t(left, factor)
        factor = factor - product(take * residual, factor)
    inverse_ref[...] = factor * across
    return jnp.max(jnp.sum(jnp.abs(residual), axis=1))


def last_kernel(plan, features, rows_ref, high_ref, low_ref, mine_ref, *rest):
    parts, (basis_ref, factors_ref) = rest[: 4 * plan.plane], rest[4 * plan.plane : 4 * plan.plane + 2]
    all_ref, product_ref, gram_ref, inverse_ref = rest[4 * plan.plane + 2 :]
    me = plan.me()
    documents, block, _ = high_ref.shape
    slots = high_ref.shape[2] // block
    gram = jnp.zeros(gram_ref.shape, F32)
    for i, ref in enumerate(parts):
        size = ref.shape[0]
        core, later = divmod(i, 2 * plan.plane)
        near, member = divmod(later, plan.plane)
        base = ((core * plan.plane + member) * 2 + 1 - near) * size
        part = ref[...]
        all_ref[base : base + size, :] = part
        gram += lax.dot_general(part, part, (((0,), (0,)), ((), ())), preferred_element_type=F32)
    gram = gram * (1.0 / features)
    residual = newton(gram, inverse_ref)
    for d in range(documents):
        picked = []
        for s in range(slots):
            for p in range(plan.pieces):
                at = pl.ds(plan.start(me, rows_ref[s, d], p), plan.piece)
                picked.append(all_ref[at, :])
        picked = jnp.concatenate(picked, axis=0)
        product_ref[d * block : (d + 1) * block, :] = dot(high_ref[d], picked) + dot(low_ref[d], picked)

    @pl.when(jnp.logical_not(residual < 1.5e-2))
    def _():
        gram_ref[...] = gram
        eliminate(gram_ref, inverse_ref)

    inverse = inverse_ref[...]
    basis_ref[...] = dot_t3(mine_ref[...], inverse)
    size = min(512, documents * block)
    for at in range(0, documents * block, size):
        factors_ref[at : at + size, :] = dot_t3(product_ref[at : at + size, :], inverse).astype(BF16)


def body(plan, blocks, rows, counts, sketch, weights):
    documents, slots, block, _ = blocks.shape
    columns = sketch.shape[1]
    features = weights.shape[0]
    half = features // 2
    chunk = half // plan.plane
    flat = plan.flat
    params = pltpu.CompilerParams(vmem_limit_bytes=VMEM_BYTES)
    shape = jax.ShapeDtypeStruct
    rows = rows.T
    parts = min(4, documents)

    total, *send = pl.pallas_call(
        functools.partial(sum_kernel, plan),
        out_shape=(pltpu.VMEM((features, columns), F32),) + (pltpu.VMEM((chunk, columns), BF16),) * plan.plane,
        in_specs=[scalars(), scalars(), pl.BlockSpec(memory_space=pltpu.HBM), pl.BlockSpec(memory_space=pltpu.HBM)],
        out_specs=(whole(),) * (1 + plan.plane),
        scratch_shapes=[
            pltpu.VMEM(blocks.shape, BF16),
            pltpu.VMEM(sketch.shape, BF16),
            pltpu.SemaphoreType.DMA((parts, 2)),
        ],
        compiler_params=params,
        name="local_sum",
    )(in_hbm(rows), in_hbm(counts), in_hbm(blocks), in_hbm(sketch))

    tiles_shape = shape((documents, block, slots * block), BF16)
    lines = weights.reshape(features // block, block)
    high, low = pl.pallas_call(
        tiles_kernel,
        out_shape=(tiles_shape, tiles_shape),
        in_specs=[scalars(), scalars(), whole(), whole()],
        out_specs=(whole(), whole()),
        compiler_params=params,
        cost_estimate=pl.CostEstimate(flops=1 << 20, bytes_accessed=4 << 20, transcendentals=0),
        name="tiles",
    )(rows, counts, blocks, lines)
    scale = pl.pallas_call(
        functools.partial(scale_kernel, plan),
        out_shape=shape((flat, columns), F32),
        in_specs=[whole()],
        out_specs=whole(),
        scratch_shapes=[pltpu.VMEM((max(flat, block), block), F32)],
        compiler_params=params,
        name="scale",
    )(lines)

    middle = chunk // 2
    others = range(1, plan.plane)
    got = {p: plan.swap(send[p], 1) for p in (*others, 0)}
    got[1], got[0] = lax.optimization_barrier((got[1], got[0]))
    chip = {
        p: pl.pallas_call(
            functools.partial(chip_kernel, p * chunk),
            out_shape=[shape((middle, columns), BF16)] * 2,
            in_specs=[whole(), whole()],
            out_specs=[whole()] * 2,
            compiler_params=params,
            name="chip_sum",
        )(total, got[p])
        for p in others
    }
    far_sent = [plan.swap_plane(chip[p][0], p) for p in reversed(others)]
    near_sent = [plan.swap_plane(chip[p][1], p) for p in reversed(others)]
    far_sent, scale = lax.optimization_barrier((far_sent, scale))

    def plane_sum(sent, start, dtypes):
        return pl.pallas_call(
            functools.partial(plane_kernel, flat, start),
            out_shape=[shape((flat, columns), dtype) for dtype in dtypes],
            in_specs=[whole()] * (2 + len(sent)),
            out_specs=[whole()] * len(dtypes),
            compiler_params=params,
            name="plane_sum",
        )(total, got[0], *sent)

    split_at = plan.line // 2
    far = plane_sum(far_sent, middle, [BF16] * split_at)
    far = [plan.swap_line(part, split_at + q) for q, part in enumerate(far)]
    held, *near = plane_sum(near_sent, 0, [F32] + [BF16] * (split_at - 1))
    near = [plan.swap_line(part, 1 + q) for q, part in enumerate(near)]
    near, far, high, low = lax.optimization_barrier((near, far, high, low))
    mine, rounded = pl.pallas_call(
        line_kernel,
        out_shape=(shape((flat, columns), F32), shape((flat, columns), BF16)),
        in_specs=[whole()] * (1 + plan.line),
        out_specs=(whole(), whole()),
        compiler_params=params,
        name="line_sum",
    )(held, scale, *near, *far)

    line = [rounded] + [plan.swap_line(rounded, q) for q in range(1, plan.line)]
    near, far = jnp.concatenate(line[:split_at], axis=0), jnp.concatenate(line[split_at:], axis=0)
    near = [near] + [plan.swap_plane(near, p) for p in others]
    far = [far] + [plan.swap_plane(far, p) for p in others]
    own = far + near
    other = [plan.swap(part, 1) for part in own]

    return pl.pallas_call(
        functools.partial(last_kernel, plan, features),
        out_shape=(shape((flat, columns), F32), shape((documents * block, columns), BF16)),
        in_specs=[scalars()] + [whole()] * (3 + 4 * plan.plane),
        out_specs=(whole(), whole()),
        scratch_shapes=[
            pltpu.VMEM((features, columns), BF16),
            pltpu.VMEM((documents * block, columns), F32),
            pltpu.VMEM((columns, columns), F32),
            pltpu.VMEM((columns, columns), F32),
        ],
        compiler_params=params,
        name="factors",
    )(rows, high, low, mine, *own, *other)


def solution(mesh):
    placed = (
        P(AXES, None, None, None),
        P(AXES, None),
        P(AXES),
        P(AXES, None),
        P(),
    )

    def run(blocks, rows, counts, sketch, weights):
        plan = Plan(mesh.shape["row"], mesh.shape["col"], weights.shape[0], blocks.shape[2])
        return jax.shard_map(
            functools.partial(body, plan),
            mesh=mesh,
            in_specs=placed,
            out_specs=(P(AXES, None), P(AXES, None)),
            check_vma=False,
        )(blocks, rows, counts, sketch, weights)

    return run
```

```python
import functools

import jax
import jax.numpy as jnp
from jax import lax
from jax.experimental import pallas as pl
from jax.experimental.pallas import tpu as pltpu
from jax.sharding import PartitionSpec as P

F32 = jnp.float32
BF16 = jnp.bfloat16
AXES = ("row", "col")
VMEM_BYTES = 48 * 1024 * 1024


def whole():
    return pl.BlockSpec(memory_space=pltpu.VMEM)


def in_hbm(value):
    return pltpu.with_memory_space_constraint(value, pltpu.HBM)


def scalars():
    return pl.BlockSpec(memory_space=pltpu.SMEM)


class Plan:
    def __init__(self, rows, cols, features, block):
        self.count = rows * cols
        self.cols = cols
        self.plane = cols
        self.line = rows // 2
        self.plane_bits = cols.bit_length() - 1
        assert self.plane * self.line * 2 == self.count and self.count & (self.count - 1) == 0
        self.flat = features // self.count
        self.piece = min(self.flat, block)
        self.pieces = block // self.piece
        per_slice = self.flat // self.piece
        self.slice_bits = per_slice.bit_length() - 1
        assert 1 << self.slice_bits == per_slice and self.piece * self.pieces == block

    def me(self):
        return lax.axis_index("row") * self.cols + lax.axis_index("col")

    def start(self, me, feature_block, piece):
        unit = feature_block * self.pieces + piece
        owner = unit >> self.slice_bits
        inside = unit & ((1 << self.slice_bits) - 1)
        apart = owner ^ me
        place = (apart & 1) * self.plane + ((apart >> 1) & (self.plane - 1))
        place = place * self.line + (apart >> (1 + self.plane_bits))
        return pl.multiple_of(place * self.flat + inside * self.piece, self.piece)

    def swap(self, value, mask):
        return lax.ppermute(value, AXES, [(d, d ^ mask) for d in range(self.count)])

    def swap_plane(self, value, member):
        return self.swap(value, member << 1)

    def swap_line(self, value, member):
        return self.swap(value, member << (1 + self.plane_bits))


def sum_kernel(plan, rows_ref, counts_ref, blocks_ref, sketch_ref, total_ref, *rest):
    send_refs, (tiles_ref, docs_ref, sems) = rest[: plan.plane], rest[plan.plane :]
    me = plan.me()
    documents, slots, block, _ = tiles_ref.shape
    half = total_ref.shape[0] // 2
    parts = sems.shape[0]
    per = documents // parts
    copies = []
    for c in range(parts):
        tiles_at = pl.ds(c * per, per)
        docs_at = pl.ds(c * per * block, per * block)
        pair = (
            pltpu.make_async_copy(blocks_ref.at[tiles_at], tiles_ref.at[tiles_at], sems.at[c, 0]),
            pltpu.make_async_copy(sketch_ref.at[docs_at], docs_ref.at[docs_at], sems.at[c, 1]),
        )
        for copy in pair:
            copy.start()
        copies.append(pair)
    total_ref[...] = jnp.zeros_like(total_ref)
    for c in range(parts):
        for copy in copies[c]:
            copy.wait()
        for d in range(c * per, (c + 1) * per):
            docs = docs_ref[d * block : (d + 1) * block, :]
            terms = jnp.dot(tiles_ref[d].reshape(slots * block, block), docs, preferred_element_type=F32)
            for s in range(slots):
                term = jnp.where(s < counts_ref[d], terms[s * block : (s + 1) * block], 0.0)
                for p in range(plan.pieces):
                    at = pl.ds(plan.start(me, rows_ref[s, d], p), plan.piece)
                    total_ref[at, :] += term[p * plan.piece : (p + 1) * plan.piece]
    for p, send_ref in enumerate(send_refs):
        size = send_ref.shape[0]
        send_ref[...] = total_ref[half + p * size : half + (p + 1) * size, :].astype(BF16)


def tiles_kernel(rows_ref, counts_ref, blocks_ref, weights_ref, out_ref):
    documents, slots, block, _ = blocks_ref.shape
    for d in range(documents):
        for s in range(slots):
            scale = weights_ref[pl.ds(rows_ref[s, d], 1), :]
            scale = jnp.where(s < counts_ref[d], scale, 0.0)
            high, low = split(blocks_ref[d, s].T.astype(F32) * scale)
            out_ref[d, :block, s * block : (s + 1) * block] = high
            out_ref[d, block:, s * block : (s + 1) * block] = low


def scale_kernel(plan, weights_ref, scale_ref, turned_ref):
    block = weights_ref.shape[1]
    unit = plan.me() << plan.slice_bits
    lines = max(1, plan.flat // block)
    first = unit if plan.pieces == 1 else unit // plan.pieces
    for i in range(lines):
        line = weights_ref[pl.ds(first + i, 1), :]
        turned_ref[i * block : (i + 1) * block, :] = jnp.broadcast_to(line, (block, block)).T
    inside = 0 if plan.pieces == 1 else lax.rem(unit, plan.pieces) * plan.piece
    scale_ref[...] = turned_ref[pl.ds(pl.multiple_of(inside, plan.piece), plan.flat), :]


def chip_kernel(start, total_ref, got_ref, far_ref, near_ref):
    middle = near_ref.shape[0]
    for ref, at in ((far_ref, middle), (near_ref, 0)):
        held = total_ref[start + at : start + at + middle, :]
        ref[...] = (held + got_ref[at : at + middle, :].astype(F32)).astype(BF16)


def plane_kernel(flat, start, total_ref, got_ref, *rest):
    count = rest[0].shape[0] // flat
    parts, out_refs = rest[:-count], rest[-count:]
    for q, out_ref in enumerate(out_refs):
        at = slice(start + q * flat, start + (q + 1) * flat)
        total = total_ref[at, :] + got_ref[at, :].astype(F32)
        for ref in parts:
            total = total + ref[q * flat : (q + 1) * flat, :].astype(F32)
        out_ref[...] = total.astype(out_ref.dtype)


def line_kernel(held_ref, scale_ref, *rest):
    parts, (mine_ref, rounded_ref) = rest[:-2], rest[-2:]
    total = held_ref[...]
    for ref in parts:
        total = total + ref[...].astype(F32)
    total = total * scale_ref[...]
    mine_ref[...] = total
    rounded_ref[...] = total.astype(BF16)


def split(value):
    high = value.astype(BF16)
    return high, (value - high.astype(F32)).astype(BF16)


def dot_t(a, b):
    return lax.dot_general(a, b, (((1,), (1,)), ((), ())), preferred_element_type=F32)


def both(total):
    size = total.shape[1] // 2
    return total[:, :size] + total[:, size:]


def dot_t3(a, b):
    b_high, b_low = split(b)
    top = jnp.concatenate([b_high, b_high], axis=1)
    low = jnp.concatenate([b_low, jnp.zeros_like(b_low)], axis=1)
    return both(dot_t(jnp.concatenate(split(a), axis=1), jnp.concatenate([top, low], axis=0)))


def dot3(a, b):
    b_high, b_low = split(b)
    top = jnp.concatenate([b_high, b_low], axis=1)
    low = jnp.concatenate([b_high, jnp.zeros_like(b_low)], axis=1)
    return both(dot(jnp.concatenate(split(a), axis=1), jnp.concatenate([top, low], axis=0)))


def dot(a, b):
    return jnp.dot(a, b, preferred_element_type=F32)


def dot1(a, b):
    return dot(a.astype(BF16), b.astype(BF16))


def dot_t1(a, b):
    return dot_t(a.astype(BF16), b.astype(BF16))


def eliminate(gram_ref, inverse_ref):
    size = gram_ref.shape[0]
    lane = lax.broadcasted_iota(jnp.int32, (size, size), 1)
    line = lax.broadcasted_iota(jnp.int32, (size, 1), 0)
    first = lax.broadcasted_iota(jnp.int32, (1, size), 1)
    inverse_ref[...] = jnp.where(lane == line, 1.0, 0.0)

    def step(j, carry):
        values = gram_ref[...]
        pivot_row = gram_ref[pl.ds(j, 1), :]
        pivot = jnp.sum(jnp.where(first == j, pivot_row, 0.0), axis=1, keepdims=True)
        scale = 1.0 / jnp.sqrt(pivot)
        column = jnp.sum(jnp.where(lane == j, values, 0.0), axis=1, keepdims=True)
        column = jnp.where(line > j, column * scale, 0.0)
        gram_ref[...] = values - column * (pivot_row * scale)
        own_row = inverse_ref[pl.ds(j, 1), :] * scale
        inverse_ref[...] = jnp.where(line == j, own_row, inverse_ref[...] - column * own_row)
        return carry

    lax.fori_loop(0, size, step, 0)


def newton(gram, inverse_ref):
    size = gram.shape[0]
    line = lax.broadcasted_iota(jnp.int32, (size, size), 0)
    lane = lax.broadcasted_iota(jnp.int32, (size, size), 1)
    same = line == lane
    eye = jnp.where(same, 1.0, 0.0)
    take = jnp.where(line > lane, 1.0, jnp.where(same, 0.5, 0.0))
    diagonal = jnp.where(same, gram, 0.0)
    down = 1.0 / jnp.sqrt(jnp.sum(diagonal, axis=1, keepdims=True))
    across = 1.0 / jnp.sqrt(jnp.sum(diagonal, axis=0, keepdims=True))
    beyond = gram * down * across - eye
    factor = eye - take * beyond
    for product, product_t in ((dot1, dot_t1), (dot1, dot_t1), (dot3, dot_t3)):
        left = factor - eye + product(factor, beyond)
        residual = factor.T - eye + product_t(left, factor)
        factor = factor - product(take * residual, factor)
    inverse_ref[...] = factor * across
    return jnp.max(jnp.sum(jnp.abs(residual), axis=1))


def gram_kernel(*refs):
    gram = jnp.zeros(refs[-1].shape, F32)
    for ref in refs[:-1]:
        part = ref[...]
        gram += lax.dot_general(part, part, (((0,), (0,)), ((), ())), preferred_element_type=F32)
    refs[-1][...] = gram


def last_kernel(plan, features, late, rows_ref, tiles_ref, mine_ref, early_ref, *rest):
    parts, (basis_ref, factors_ref) = rest[: 4 * plan.plane], rest[4 * plan.plane : 4 * plan.plane + 2]
    all_ref, product_ref, gram_ref, inverse_ref = rest[4 * plan.plane + 2 :]
    me = plan.me()
    documents = tiles_ref.shape[0]
    block = tiles_ref.shape[1] // 2
    slots = tiles_ref.shape[2] // block
    gram = early_ref[...]
    for i, ref in enumerate(parts):
        size = ref.shape[0]
        core, later = divmod(i, 2 * plan.plane)
        near, member = divmod(later, plan.plane)
        base = ((core * plan.plane + member) * 2 + 1 - near) * size
        part = ref[...]
        all_ref[base : base + size, :] = part
        if i in late:
            gram += lax.dot_general(part, part, (((0,), (0,)), ((), ())), preferred_element_type=F32)
    gram = gram * (1.0 / features)
    residual = newton(gram, inverse_ref)
    for d in range(documents):
        picked = []
        for s in range(slots):
            for p in range(plan.pieces):
                at = pl.ds(plan.start(me, rows_ref[s, d], p), plan.piece)
                picked.append(all_ref[at, :])
        terms = dot(tiles_ref[d], jnp.concatenate(picked, axis=0))
        product_ref[d * block : (d + 1) * block, :] = terms[:block] + terms[block:]

    @pl.when(jnp.logical_not(residual < 1.5e-2))
    def _():
        gram_ref[...] = gram
        eliminate(gram_ref, inverse_ref)

    inverse = inverse_ref[...]
    basis_ref[...] = dot_t3(mine_ref[...], inverse)
    size = min(512, documents * block)
    for at in range(0, documents * block, size):
        factors_ref[at : at + size, :] = dot_t3(product_ref[at : at + size, :], inverse).astype(BF16)


def body(plan, blocks, rows, counts, sketch, weights):
    documents, slots, block, _ = blocks.shape
    columns = sketch.shape[1]
    features = weights.shape[0]
    half = features // 2
    chunk = half // plan.plane
    flat = plan.flat
    params = pltpu.CompilerParams(vmem_limit_bytes=VMEM_BYTES)
    shape = jax.ShapeDtypeStruct
    rows = rows.T
    parts = min(4, documents)

    total, *send = pl.pallas_call(
        functools.partial(sum_kernel, plan),
        out_shape=(pltpu.VMEM((features, columns), F32),) + (pltpu.VMEM((chunk, columns), BF16),) * plan.plane,
        in_specs=[scalars(), scalars(), pl.BlockSpec(memory_space=pltpu.HBM), pl.BlockSpec(memory_space=pltpu.HBM)],
        out_specs=(whole(),) * (1 + plan.plane),
        scratch_shapes=[
            pltpu.VMEM(blocks.shape, BF16),
            pltpu.VMEM(sketch.shape, BF16),
            pltpu.SemaphoreType.DMA((parts, 2)),
        ],
        compiler_params=params,
        name="local_sum",
    )(in_hbm(rows), in_hbm(counts), in_hbm(blocks), in_hbm(sketch))

    lines = weights.reshape(features // block, block)
    tiles = pl.pallas_call(
        tiles_kernel,
        out_shape=shape((documents, 2 * block, slots * block), BF16),
        in_specs=[scalars(), scalars(), whole(), whole()],
        out_specs=whole(),
        compiler_params=params,
        cost_estimate=pl.CostEstimate(flops=1 << 20, bytes_accessed=4 << 20, transcendentals=0),
        name="tiles",
    )(rows, counts, blocks, lines)
    scale = pl.pallas_call(
        functools.partial(scale_kernel, plan),
        out_shape=shape((flat, columns), F32),
        in_specs=[whole()],
        out_specs=whole(),
        scratch_shapes=[pltpu.VMEM((max(flat, block), block), F32)],
        compiler_params=params,
        name="scale",
    )(lines)

    middle = chunk // 2
    others = range(1, plan.plane)
    got = {p: plan.swap(send[p], 1) for p in (*others, 0)}
    got[1], got[0] = lax.optimization_barrier((got[1], got[0]))
    chip = {
        p: pl.pallas_call(
            functools.partial(chip_kernel, p * chunk),
            out_shape=[shape((middle, columns), BF16)] * 2,
            in_specs=[whole(), whole()],
            out_specs=[whole()] * 2,
            compiler_params=params,
            name="chip_sum",
        )(total, got[p])
        for p in others
    }
    far_sent = [plan.swap_plane(chip[p][0], p) for p in reversed(others)]
    near_sent = [plan.swap_plane(chip[p][1], p) for p in reversed(others)]
    far_sent, scale = lax.optimization_barrier((far_sent, scale))

    def plane_sum(sent, start, dtypes):
        return pl.pallas_call(
            functools.partial(plane_kernel, flat, start),
            out_shape=[shape((flat, columns), dtype) for dtype in dtypes],
            in_specs=[whole()] * (2 + len(sent)),
            out_specs=[whole()] * len(dtypes),
            compiler_params=params,
            name="plane_sum",
        )(total, got[0], *sent)

    split_at = plan.line // 2
    far = plane_sum(far_sent, middle, [BF16] * split_at)
    far = [plan.swap_line(part, split_at + q) for q, part in enumerate(far)]
    held, *near = plane_sum(near_sent, 0, [F32] + [BF16] * (split_at - 1))
    near = [plan.swap_line(part, 1 + q) for q, part in enumerate(near)]
    near, far, tiles = lax.optimization_barrier((near, far, tiles))
    mine, rounded = pl.pallas_call(
        line_kernel,
        out_shape=(shape((flat, columns), F32), shape((flat, columns), BF16)),
        in_specs=[whole()] * (1 + plan.line),
        out_specs=(whole(), whole()),
        compiler_params=params,
        name="line_sum",
    )(held, scale, *near, *far)

    line = [rounded] + [plan.swap_line(rounded, q) for q in range(1, plan.line)]
    near, far = jnp.concatenate(line[:split_at], axis=0), jnp.concatenate(line[split_at:], axis=0)
    near = [near] + [plan.swap_plane(near, p) for p in others]
    far = [far] + [plan.swap_plane(far, p) for p in others]
    own = far + near
    other = [plan.swap(part, 1) for part in own]

    pieces = own + other
    late = range(len(own) + 1, len(own) + plan.plane)
    gram = pl.pallas_call(
        gram_kernel,
        out_shape=shape((columns, columns), F32),
        in_specs=[whole()] * (len(pieces) - len(late)),
        out_specs=whole(),
        compiler_params=params,
        cost_estimate=pl.CostEstimate(flops=2 * features * columns * columns, bytes_accessed=4 << 20, transcendentals=0),
        name="gram",
    )(*[piece for i, piece in enumerate(pieces) if i not in late])
    return pl.pallas_call(
        functools.partial(last_kernel, plan, features, late),
        out_shape=(shape((flat, columns), F32), shape((documents * block, columns), BF16)),
        in_specs=[scalars()] + [whole()] * (3 + len(pieces)),
        out_specs=(whole(), whole()),
        scratch_shapes=[
            pltpu.VMEM((features, columns), BF16),
            pltpu.VMEM((documents * block, columns), F32),
            pltpu.VMEM((columns, columns), F32),
            pltpu.VMEM((columns, columns), F32),
        ],
        compiler_params=params,
        name="factors",
    )(rows, tiles, mine, gram, *pieces)


def solution(mesh):
    placed = (
        P(AXES, None, None, None),
        P(AXES, None),
        P(AXES),
        P(AXES, None),
        P(),
    )

    def run(blocks, rows, counts, sketch, weights):
        plan = Plan(mesh.shape["row"], mesh.shape["col"], weights.shape[0], blocks.shape[2])
        return jax.shard_map(
            functools.partial(body, plan),
            mesh=mesh,
            in_specs=placed,
            out_specs=(P(AXES, None), P(AXES, None)),
            check_vma=False,
        )(blocks, rows, counts, sketch, weights)

    return run
```

```python
import functools

import jax
import jax.numpy as jnp
from jax import lax
from jax.experimental import pallas as pl
from jax.experimental.pallas import tpu as pltpu
from jax.sharding import PartitionSpec as P

F32 = jnp.float32
BF16 = jnp.bfloat16
AXES = ("row", "col")
VMEM_BYTES = 48 * 1024 * 1024


def whole():
    return pl.BlockSpec(memory_space=pltpu.VMEM)


def in_hbm(value):
    return pltpu.with_memory_space_constraint(value, pltpu.HBM)


def scalars():
    return pl.BlockSpec(memory_space=pltpu.SMEM)


class Plan:
    def __init__(self, rows, cols, features, block):
        self.count = rows * cols
        self.cols = cols
        self.plane = cols
        self.line = rows // 2
        self.plane_bits = cols.bit_length() - 1
        assert self.plane * self.line * 2 == self.count and self.count & (self.count - 1) == 0
        self.flat = features // self.count
        self.piece = min(self.flat, block)
        self.pieces = block // self.piece
        per_slice = self.flat // self.piece
        self.slice_bits = per_slice.bit_length() - 1
        assert 1 << self.slice_bits == per_slice and self.piece * self.pieces == block

    def me(self):
        return lax.axis_index("row") * self.cols + lax.axis_index("col")

    def start(self, me, feature_block, piece):
        unit = feature_block * self.pieces + piece
        owner = unit >> self.slice_bits
        inside = unit & ((1 << self.slice_bits) - 1)
        apart = owner ^ me
        place = (apart & 1) * self.plane + ((apart >> 1) & (self.plane - 1))
        place = place * self.line + (apart >> (1 + self.plane_bits))
        return pl.multiple_of(place * self.flat + inside * self.piece, self.piece)

    def swap(self, value, mask):
        return lax.ppermute(value, AXES, [(d, d ^ mask) for d in range(self.count)])

    def swap_plane(self, value, member):
        return self.swap(value, member << 1)

    def swap_line(self, value, member):
        return self.swap(value, member << (1 + self.plane_bits))


def sum_kernel(plan, rows_hbm, counts_hbm, blocks_ref, sketch_ref, total_ref, *rest):
    send_refs, (tiles_ref, docs_ref, rows_ref, counts_ref, sems, small_sems) = rest[: plan.plane], rest[plan.plane :]
    me = plan.me()
    documents, slots, block, _ = tiles_ref.shape
    half = total_ref.shape[0] // 2
    parts = sems.shape[0]
    per = documents // parts
    small = (
        pltpu.make_async_copy(rows_hbm, rows_ref, small_sems.at[0]),
        pltpu.make_async_copy(counts_hbm, counts_ref, small_sems.at[1]),
    )
    for copy in small:
        copy.start()
    copies = []
    for c in range(parts):
        tiles_at = pl.ds(c * per, per)
        docs_at = pl.ds(c * per * block, per * block)
        pair = (
            pltpu.make_async_copy(blocks_ref.at[tiles_at], tiles_ref.at[tiles_at], sems.at[c, 0]),
            pltpu.make_async_copy(sketch_ref.at[docs_at], docs_ref.at[docs_at], sems.at[c, 1]),
        )
        for copy in pair:
            copy.start()
        copies.append(pair)
    total_ref[...] = jnp.zeros_like(total_ref)
    for copy in small:
        copy.wait()
    for c in range(parts):
        for copy in copies[c]:
            copy.wait()
        for d in range(c * per, (c + 1) * per):
            docs = docs_ref[d * block : (d + 1) * block, :]
            terms = jnp.dot(tiles_ref[d].reshape(slots * block, block), docs, preferred_element_type=F32)
            for s in range(slots):
                term = jnp.where(s < counts_ref[d], terms[s * block : (s + 1) * block], 0.0)
                for p in range(plan.pieces):
                    at = pl.ds(plan.start(me, rows_ref[s, d], p), plan.piece)
                    total_ref[at, :] += term[p * plan.piece : (p + 1) * plan.piece]
    for p, send_ref in enumerate(send_refs):
        size = send_ref.shape[0]
        send_ref[...] = total_ref[half + p * size : half + (p + 1) * size, :].astype(BF16)


def tiles_kernel(rows_ref, counts_ref, blocks_ref, weights_ref, out_ref):
    documents, slots, block, _ = blocks_ref.shape
    for d in range(documents):
        for s in range(slots):
            scale = weights_ref[pl.ds(rows_ref[s, d], 1), :]
            scale = jnp.where(s < counts_ref[d], scale, 0.0)
            high, low = split(blocks_ref[d, s].T.astype(F32) * scale)
            out_ref[d, :block, s * block : (s + 1) * block] = high
            out_ref[d, block:, s * block : (s + 1) * block] = low


def scale_kernel(plan, weights_ref, scale_ref, turned_ref):
    block = weights_ref.shape[1]
    unit = plan.me() << plan.slice_bits
    lines = max(1, plan.flat // block)
    first = unit if plan.pieces == 1 else unit // plan.pieces
    for i in range(lines):
        line = weights_ref[pl.ds(first + i, 1), :]
        turned_ref[i * block : (i + 1) * block, :] = jnp.broadcast_to(line, (block, block)).T
    inside = 0 if plan.pieces == 1 else lax.rem(unit, plan.pieces) * plan.piece
    scale_ref[...] = turned_ref[pl.ds(pl.multiple_of(inside, plan.piece), plan.flat), :]


def chip_kernel(start, total_ref, got_ref, far_ref, near_ref):
    middle = near_ref.shape[0]
    for ref, at in ((far_ref, middle), (near_ref, 0)):
        held = total_ref[start + at : start + at + middle, :]
        ref[...] = (held + got_ref[at : at + middle, :].astype(F32)).astype(BF16)


def plane_kernel(flat, start, total_ref, got_ref, *rest):
    count = rest[0].shape[0] // flat
    parts, out_refs = rest[:-count], rest[-count:]
    for q, out_ref in enumerate(out_refs):
        at = slice(start + q * flat, start + (q + 1) * flat)
        total = total_ref[at, :] + got_ref[at, :].astype(F32)
        for ref in parts:
            total = total + ref[q * flat : (q + 1) * flat, :].astype(F32)
        out_ref[...] = total.astype(out_ref.dtype)


def line_kernel(held_ref, scale_ref, *rest):
    parts, (mine_ref, rounded_ref) = rest[:-2], rest[-2:]
    total = held_ref[...]
    for ref in parts:
        total = total + ref[...].astype(F32)
    total = total * scale_ref[...]
    mine_ref[...] = total
    rounded_ref[...] = total.astype(BF16)


def split(value):
    high = value.astype(BF16)
    return high, (value - high.astype(F32)).astype(BF16)


def dot_t(a, b):
    return lax.dot_general(a, b, (((1,), (1,)), ((), ())), preferred_element_type=F32)


def both(total):
    size = total.shape[1] // 2
    return total[:, :size] + total[:, size:]


def dot_t3(a, b):
    b_high, b_low = split(b)
    top = jnp.concatenate([b_high, b_high], axis=1)
    low = jnp.concatenate([b_low, jnp.zeros_like(b_low)], axis=1)
    return both(dot_t(jnp.concatenate(split(a), axis=1), jnp.concatenate([top, low], axis=0)))


def dot3(a, b):
    b_high, b_low = split(b)
    top = jnp.concatenate([b_high, b_low], axis=1)
    low = jnp.concatenate([b_high, jnp.zeros_like(b_low)], axis=1)
    return both(dot(jnp.concatenate(split(a), axis=1), jnp.concatenate([top, low], axis=0)))


def dot(a, b):
    return jnp.dot(a, b, preferred_element_type=F32)


def dot1(a, b):
    return dot(a.astype(BF16), b.astype(BF16))


def dot_t1(a, b):
    return dot_t(a.astype(BF16), b.astype(BF16))


def eliminate(gram_ref, inverse_ref):
    size = gram_ref.shape[0]
    lane = lax.broadcasted_iota(jnp.int32, (size, size), 1)
    line = lax.broadcasted_iota(jnp.int32, (size, 1), 0)
    first = lax.broadcasted_iota(jnp.int32, (1, size), 1)
    inverse_ref[...] = jnp.where(lane == line, 1.0, 0.0)

    def step(j, carry):
        values = gram_ref[...]
        pivot_row = gram_ref[pl.ds(j, 1), :]
        pivot = jnp.sum(jnp.where(first == j, pivot_row, 0.0), axis=1, keepdims=True)
        scale = 1.0 / jnp.sqrt(pivot)
        column = jnp.sum(jnp.where(lane == j, values, 0.0), axis=1, keepdims=True)
        column = jnp.where(line > j, column * scale, 0.0)
        gram_ref[...] = values - column * (pivot_row * scale)
        own_row = inverse_ref[pl.ds(j, 1), :] * scale
        inverse_ref[...] = jnp.where(line == j, own_row, inverse_ref[...] - column * own_row)
        return carry

    lax.fori_loop(0, size, step, 0)


def newton(gram, inverse_ref):
    size = gram.shape[0]
    line = lax.broadcasted_iota(jnp.int32, (size, size), 0)
    lane = lax.broadcasted_iota(jnp.int32, (size, size), 1)
    same = line == lane
    eye = jnp.where(same, 1.0, 0.0)
    take = jnp.where(line > lane, 1.0, jnp.where(same, 0.5, 0.0))
    diagonal = jnp.where(same, gram, 0.0)
    down = 1.0 / jnp.sqrt(jnp.sum(diagonal, axis=1, keepdims=True))
    across = 1.0 / jnp.sqrt(jnp.sum(diagonal, axis=0, keepdims=True))
    beyond = gram * down * across - eye
    factor = eye - take * beyond
    for product, product_t in ((dot1, dot_t1), (dot3, dot_t3)):
        left = factor - eye + product(factor, beyond)
        residual = factor.T - eye + product_t(left, factor)
        factor = factor - product(take * residual, factor)
    inverse_ref[...] = factor * across
    return jnp.sum(residual * residual)


def gram_kernel(*refs):
    gram = jnp.zeros(refs[-1].shape, F32)
    for ref in refs[:-1]:
        part = ref[...]
        gram += lax.dot_general(part, part, (((0,), (0,)), ((), ())), preferred_element_type=F32)
    refs[-1][...] = gram


def last_kernel(plan, features, late, rows_ref, tiles_ref, mine_ref, early_ref, *rest):
    parts, (basis_ref, factors_ref) = rest[: 4 * plan.plane], rest[4 * plan.plane : 4 * plan.plane + 2]
    all_ref, product_ref, gram_ref, inverse_ref = rest[4 * plan.plane + 2 :]
    me = plan.me()
    documents = tiles_ref.shape[0]
    block = tiles_ref.shape[1] // 2
    slots = tiles_ref.shape[2] // block
    gram = early_ref[...]
    for i, ref in enumerate(parts):
        size = ref.shape[0]
        core, later = divmod(i, 2 * plan.plane)
        near, member = divmod(later, plan.plane)
        base = ((core * plan.plane + member) * 2 + 1 - near) * size
        part = ref[...]
        all_ref[base : base + size, :] = part
        if i in late:
            gram += lax.dot_general(part, part, (((0,), (0,)), ((), ())), preferred_element_type=F32)
    gram = gram * (1.0 / features)
    residual = newton(gram, inverse_ref)
    for d in range(documents):
        picked = []
        for s in range(slots):
            for p in range(plan.pieces):
                at = pl.ds(plan.start(me, rows_ref[s, d], p), plan.piece)
                picked.append(all_ref[at, :])
        terms = dot(tiles_ref[d], jnp.concatenate(picked, axis=0))
        product_ref[d * block : (d + 1) * block, :] = terms[:block] + terms[block:]

    @pl.when(jnp.logical_not(residual < 1e-3))
    def _():
        gram_ref[...] = gram
        eliminate(gram_ref, inverse_ref)

    inverse = inverse_ref[...]
    basis_ref[...] = dot_t3(mine_ref[...], inverse)
    size = min(512, documents * block)
    for at in range(0, documents * block, size):
        factors_ref[at : at + size, :] = dot_t3(product_ref[at : at + size, :], inverse).astype(BF16)


def body(plan, blocks, rows, counts, sketch, weights):
    documents, slots, block, _ = blocks.shape
    columns = sketch.shape[1]
    features = weights.shape[0]
    half = features // 2
    chunk = half // plan.plane
    flat = plan.flat
    params = pltpu.CompilerParams(vmem_limit_bytes=VMEM_BYTES)
    shape = jax.ShapeDtypeStruct
    rows = rows.T
    parts = min(4, documents)

    total, *send = pl.pallas_call(
        functools.partial(sum_kernel, plan),
        out_shape=(pltpu.VMEM((features, columns), F32),) + (pltpu.VMEM((chunk, columns), BF16),) * plan.plane,
        in_specs=[pl.BlockSpec(memory_space=pltpu.HBM)] * 4,
        out_specs=(whole(),) * (1 + plan.plane),
        scratch_shapes=[
            pltpu.VMEM(blocks.shape, BF16),
            pltpu.VMEM(sketch.shape, BF16),
            pltpu.SMEM(rows.shape, jnp.int32),
            pltpu.SMEM(counts.shape, jnp.int32),
            pltpu.SemaphoreType.DMA((parts, 2)),
            pltpu.SemaphoreType.DMA((2,)),
        ],
        compiler_params=params,
        name="local_sum",
    )(in_hbm(rows), in_hbm(counts), in_hbm(blocks), in_hbm(sketch))

    lines = weights.reshape(features // block, block)
    tiles = pl.pallas_call(
        tiles_kernel,
        out_shape=shape((documents, 2 * block, slots * block), BF16),
        in_specs=[scalars(), scalars(), whole(), whole()],
        out_specs=whole(),
        compiler_params=params,
        cost_estimate=pl.CostEstimate(flops=1 << 20, bytes_accessed=4 << 20, transcendentals=0),
        name="tiles",
    )(rows, counts, blocks, lines)
    scale = pl.pallas_call(
        functools.partial(scale_kernel, plan),
        out_shape=shape((flat, columns), F32),
        in_specs=[whole()],
        out_specs=whole(),
        scratch_shapes=[pltpu.VMEM((max(flat, block), block), F32)],
        compiler_params=params,
        name="scale",
    )(lines)

    middle = chunk // 2
    others = range(1, plan.plane)
    got = {p: plan.swap(send[p], 1) for p in (*others, 0)}
    got[1], got[0] = lax.optimization_barrier((got[1], got[0]))
    chip = {}
    for p in others:
        chip[p] = pl.pallas_call(
            functools.partial(chip_kernel, p * chunk),
            out_shape=[shape((middle, columns), BF16)] * 2,
            in_specs=[whole(), whole()],
            out_specs=[whole()] * 2,
            compiler_params=params,
            name="chip_sum",
        )(total, got[p])
    far_sent = [plan.swap_plane(chip[p][0], p) for p in reversed(others)]
    near_sent = [plan.swap_plane(chip[p][1], p) for p in reversed(others)]
    far_sent, scale = lax.optimization_barrier((far_sent, scale))

    def plane_sum(sent, start, dtypes):
        return pl.pallas_call(
            functools.partial(plane_kernel, flat, start),
            out_shape=[shape((flat, columns), dtype) for dtype in dtypes],
            in_specs=[whole()] * (2 + len(sent)),
            out_specs=[whole()] * len(dtypes),
            compiler_params=params,
            name="plane_sum",
        )(total, got[0], *sent)

    split_at = plan.line // 2
    far = plane_sum(far_sent, middle, [BF16] * split_at)
    far = [plan.swap_line(part, split_at + q) for q, part in enumerate(far)]
    held, *near = plane_sum(near_sent, 0, [F32] + [BF16] * (split_at - 1))
    near = [plan.swap_line(part, 1 + q) for q, part in enumerate(near)]
    near, far, tiles = lax.optimization_barrier((near, far, tiles))
    mine, rounded = pl.pallas_call(
        line_kernel,
        out_shape=(shape((flat, columns), F32), shape((flat, columns), BF16)),
        in_specs=[whole()] * (1 + plan.line),
        out_specs=(whole(), whole()),
        compiler_params=params,
        name="line_sum",
    )(held, scale, *near, *far)

    line = [rounded] + [plan.swap_line(rounded, q) for q in range(1, plan.line)]
    near, far = jnp.concatenate(line[:split_at], axis=0), jnp.concatenate(line[split_at:], axis=0)
    near = [near] + [plan.swap_plane(near, p) for p in others]
    far = [far] + [plan.swap_plane(far, p) for p in others]
    own = far + near
    other = [plan.swap(part, 1) for part in own]

    pieces = own + other
    late = range(len(own) + 1, len(own) + plan.plane)
    gram = pl.pallas_call(
        gram_kernel,
        out_shape=shape((columns, columns), F32),
        in_specs=[whole()] * (len(pieces) - len(late)),
        out_specs=whole(),
        compiler_params=params,
        cost_estimate=pl.CostEstimate(flops=2 * features * columns * columns, bytes_accessed=4 << 20, transcendentals=0),
        name="gram",
    )(*[piece for i, piece in enumerate(pieces) if i not in late])
    return pl.pallas_call(
        functools.partial(last_kernel, plan, features, late),
        out_shape=(shape((flat, columns), F32), shape((documents * block, columns), BF16)),
        in_specs=[scalars()] + [whole()] * (3 + len(pieces)),
        out_specs=(whole(), whole()),
        scratch_shapes=[
            pltpu.VMEM((features, columns), BF16),
            pltpu.VMEM((documents * block, columns), F32),
            pltpu.VMEM((columns, columns), F32),
            pltpu.VMEM((columns, columns), F32),
        ],
        compiler_params=params,
        name="factors",
    )(rows, tiles, mine, gram, *pieces)


def solution(mesh):
    placed = (
        P(AXES, None, None, None),
        P(AXES, None),
        P(AXES),
        P(AXES, None),
        P(),
    )

    def run(blocks, rows, counts, sketch, weights):
        plan = Plan(mesh.shape["row"], mesh.shape["col"], weights.shape[0], blocks.shape[2])
        return jax.shard_map(
            functools.partial(body, plan),
            mesh=mesh,
            in_specs=placed,
            out_specs=(P(AXES, None), P(AXES, None)),
            check_vma=False,
        )(blocks, rows, counts, sketch, weights)

    return run
```

```python
import functools

import jax
import jax.numpy as jnp
from jax import lax
from jax.experimental import pallas as pl
from jax.experimental.pallas import tpu as pltpu
from jax.sharding import PartitionSpec as P

F32 = jnp.float32
BF16 = jnp.bfloat16
AXES = ("row", "col")
VMEM_BYTES = 48 * 1024 * 1024


def whole():
    return pl.BlockSpec(memory_space=pltpu.VMEM)


def in_hbm(value):
    return pltpu.with_memory_space_constraint(value, pltpu.HBM)


def scalars():
    return pl.BlockSpec(memory_space=pltpu.SMEM)


class Plan:
    def __init__(self, rows, cols, features, block):
        self.count = rows * cols
        self.cols = cols
        self.plane = cols
        self.line = rows // 2
        self.plane_bits = cols.bit_length() - 1
        assert self.plane * self.line * 2 == self.count and self.count & (self.count - 1) == 0
        self.flat = features // self.count
        self.piece = min(self.flat, block)
        self.pieces = block // self.piece
        per_slice = self.flat // self.piece
        self.slice_bits = per_slice.bit_length() - 1
        assert 1 << self.slice_bits == per_slice and self.piece * self.pieces == block

    def me(self):
        return lax.axis_index("row") * self.cols + lax.axis_index("col")

    def start(self, me, feature_block, piece):
        unit = feature_block * self.pieces + piece
        owner = unit >> self.slice_bits
        inside = unit & ((1 << self.slice_bits) - 1)
        apart = owner ^ me
        place = (apart & 1) * self.plane + ((apart >> 1) & (self.plane - 1))
        place = place * self.line + (apart >> (1 + self.plane_bits))
        return pl.multiple_of(place * self.flat + inside * self.piece, self.piece)

    def swap(self, value, mask):
        return lax.ppermute(value, AXES, [(d, d ^ mask) for d in range(self.count)])

    def swap_plane(self, value, member):
        return self.swap(value, member << 1)

    def swap_line(self, value, member):
        return self.swap(value, member << (1 + self.plane_bits))


def sum_kernel(plan, rows_hbm, counts_hbm, blocks_ref, sketch_ref, total_ref, *rest):
    send_refs, (tiles_ref, docs_ref, rows_ref, counts_ref, sems, small_sems) = rest[: plan.plane], rest[plan.plane :]
    me = plan.me()
    documents, slots, block, _ = tiles_ref.shape
    half = total_ref.shape[0] // 2
    parts = sems.shape[0]
    per = documents // parts
    small = (
        pltpu.make_async_copy(rows_hbm, rows_ref, small_sems.at[0]),
        pltpu.make_async_copy(counts_hbm, counts_ref, small_sems.at[1]),
    )
    for copy in small:
        copy.start()
    copies = []
    for c in range(parts):
        tiles_at = pl.ds(c * per, per)
        docs_at = pl.ds(c * per * block, per * block)
        pair = (
            pltpu.make_async_copy(blocks_ref.at[tiles_at], tiles_ref.at[tiles_at], sems.at[c, 0]),
            pltpu.make_async_copy(sketch_ref.at[docs_at], docs_ref.at[docs_at], sems.at[c, 1]),
        )
        for copy in pair:
            copy.start()
        copies.append(pair)
    total_ref[...] = jnp.zeros_like(total_ref)
    for copy in small:
        copy.wait()
    for c in range(parts):
        for copy in copies[c]:
            copy.wait()
        for d in range(c * per, (c + 1) * per):
            docs = docs_ref[d * block : (d + 1) * block, :]
            terms = jnp.dot(tiles_ref[d].reshape(slots * block, block), docs, preferred_element_type=F32)
            for s in range(slots):
                term = jnp.where(s < counts_ref[d], terms[s * block : (s + 1) * block], 0.0)
                for p in range(plan.pieces):
                    at = pl.ds(plan.start(me, rows_ref[s, d], p), plan.piece)
                    total_ref[at, :] += term[p * plan.piece : (p + 1) * plan.piece]
    for p, send_ref in enumerate(send_refs):
        size = send_ref.shape[0]
        send_ref[...] = total_ref[half + p * size : half + (p + 1) * size, :].astype(BF16)


def tiles_kernel(rows_ref, counts_ref, blocks_ref, weights_ref, out_ref):
    documents, slots, block, _ = blocks_ref.shape
    for d in range(documents):
        for s in range(slots):
            scale = weights_ref[pl.ds(rows_ref[s, d], 1), :]
            scale = jnp.where(s < counts_ref[d], scale, 0.0)
            high, low = split(blocks_ref[d, s].T.astype(F32) * scale)
            out_ref[d, :block, s * block : (s + 1) * block] = high
            out_ref[d, block:, s * block : (s + 1) * block] = low


def scale_kernel(plan, weights_ref, scale_ref, turned_ref):
    block = weights_ref.shape[1]
    unit = plan.me() << plan.slice_bits
    lines = max(1, plan.flat // block)
    first = unit if plan.pieces == 1 else unit // plan.pieces
    for i in range(lines):
        line = weights_ref[pl.ds(first + i, 1), :]
        turned_ref[i * block : (i + 1) * block, :] = jnp.broadcast_to(line, (block, block)).T
    inside = 0 if plan.pieces == 1 else lax.rem(unit, plan.pieces) * plan.piece
    scale_ref[...] = turned_ref[pl.ds(pl.multiple_of(inside, plan.piece), plan.flat), :]


def chip_kernel(start, total_ref, got_ref, far_ref, near_ref):
    middle = near_ref.shape[0]
    for ref, at in ((far_ref, middle), (near_ref, 0)):
        held = total_ref[start + at : start + at + middle, :]
        ref[...] = (held + got_ref[at : at + middle, :].astype(F32)).astype(BF16)


def plane_kernel(flat, start, total_ref, got_ref, *rest):
    count = rest[0].shape[0] // flat
    parts, out_refs = rest[:-count], rest[-count:]
    for q, out_ref in enumerate(out_refs):
        at = slice(start + q * flat, start + (q + 1) * flat)
        total = total_ref[at, :] + got_ref[at, :].astype(F32)
        for ref in parts:
            total = total + ref[q * flat : (q + 1) * flat, :].astype(F32)
        out_ref[...] = total.astype(out_ref.dtype)


def line_kernel(held_ref, scale_ref, *rest):
    parts, (mine_ref, rounded_ref) = rest[:-2], rest[-2:]
    total = held_ref[...]
    for ref in parts:
        total = total + ref[...].astype(F32)
    total = total * scale_ref[...]
    mine_ref[...] = total
    rounded_ref[...] = total.astype(BF16)


def split(value):
    high = value.astype(BF16)
    return high, (value - high.astype(F32)).astype(BF16)


def dot_t(a, b):
    return lax.dot_general(a, b, (((1,), (1,)), ((), ())), preferred_element_type=F32)


def both(total):
    size = total.shape[1] // 2
    return total[:, :size] + total[:, size:]


def dot_t3(a, b):
    b_high, b_low = split(b)
    top = jnp.concatenate([b_high, b_high], axis=1)
    low = jnp.concatenate([b_low, jnp.zeros_like(b_low)], axis=1)
    return both(dot_t(jnp.concatenate(split(a), axis=1), jnp.concatenate([top, low], axis=0)))


def dot3(a, b):
    b_high, b_low = split(b)
    top = jnp.concatenate([b_high, b_low], axis=1)
    low = jnp.concatenate([b_high, jnp.zeros_like(b_low)], axis=1)
    return both(dot(jnp.concatenate(split(a), axis=1), jnp.concatenate([top, low], axis=0)))


def dot(a, b):
    return jnp.dot(a, b, preferred_element_type=F32)


def dot1(a, b):
    return dot(a.astype(BF16), b.astype(BF16))


def dot_t1(a, b):
    return dot_t(a.astype(BF16), b.astype(BF16))


def eliminate(gram_ref, inverse_ref):
    size = gram_ref.shape[0]
    lane = lax.broadcasted_iota(jnp.int32, (size, size), 1)
    line = lax.broadcasted_iota(jnp.int32, (size, 1), 0)
    first = lax.broadcasted_iota(jnp.int32, (1, size), 1)
    inverse_ref[...] = jnp.where(lane == line, 1.0, 0.0)

    def step(j, carry):
        values = gram_ref[...]
        pivot_row = gram_ref[pl.ds(j, 1), :]
        pivot = jnp.sum(jnp.where(first == j, pivot_row, 0.0), axis=1, keepdims=True)
        scale = 1.0 / jnp.sqrt(pivot)
        column = jnp.sum(jnp.where(lane == j, values, 0.0), axis=1, keepdims=True)
        column = jnp.where(line > j, column * scale, 0.0)
        gram_ref[...] = values - column * (pivot_row * scale)
        own_row = inverse_ref[pl.ds(j, 1), :] * scale
        inverse_ref[...] = jnp.where(line == j, own_row, inverse_ref[...] - column * own_row)
        return carry

    lax.fori_loop(0, size, step, 0)


def newton(gram, inverse_ref):
    size = gram.shape[0]
    line = lax.broadcasted_iota(jnp.int32, (size, size), 0)
    lane = lax.broadcasted_iota(jnp.int32, (size, size), 1)
    same = line == lane
    eye = jnp.where(same, 1.0, 0.0)
    take = jnp.where(line > lane, 1.0, jnp.where(same, 0.5, 0.0))
    diagonal = jnp.where(same, gram, 0.0)
    down = 1.0 / jnp.sqrt(jnp.sum(diagonal, axis=1, keepdims=True))
    across = 1.0 / jnp.sqrt(jnp.sum(diagonal, axis=0, keepdims=True))
    beyond = gram * down * across - eye
    factor = eye - take * beyond
    for product, product_t in ((dot1, dot_t1), (dot3, dot_t3)):
        left = factor - eye + product(factor, beyond)
        residual = factor.T - eye + product_t(left, factor)
        factor = factor - product(take * residual, factor)
    inverse_ref[...] = factor * across
    return jnp.sum(residual * residual)


def gram_kernel(*refs):
    gram = jnp.zeros(refs[-1].shape, F32)
    for ref in refs[:-1]:
        part = ref[...]
        gram += lax.dot_general(part, part, (((0,), (0,)), ((), ())), preferred_element_type=F32)
    refs[-1][...] = gram


def last_kernel(plan, features, late, rows_ref, tiles_ref, mine_ref, early_ref, *rest):
    parts, (basis_ref, factors_ref) = rest[: 4 * plan.plane], rest[4 * plan.plane : 4 * plan.plane + 2]
    all_ref, product_ref, gram_ref, inverse_ref = rest[4 * plan.plane + 2 :]
    me = plan.me()
    documents = tiles_ref.shape[0]
    block = tiles_ref.shape[1] // 2
    slots = tiles_ref.shape[2] // block
    gram = early_ref[...]
    for i, ref in enumerate(parts):
        size = ref.shape[0]
        core, later = divmod(i, 2 * plan.plane)
        near, member = divmod(later, plan.plane)
        if near and member:
            member = plan.plane - member
        base = ((core * plan.plane + member) * 2 + 1 - near) * size
        part = ref[...]
        all_ref[base : base + size, :] = part
        if i in late:
            gram += lax.dot_general(part, part, (((0,), (0,)), ((), ())), preferred_element_type=F32)
    gram = gram * (1.0 / features)
    residual = newton(gram, inverse_ref)
    for d in range(documents):
        picked = []
        for s in range(slots):
            for p in range(plan.pieces):
                at = pl.ds(plan.start(me, rows_ref[s, d], p), plan.piece)
                picked.append(all_ref[at, :])
        terms = dot(tiles_ref[d], jnp.concatenate(picked, axis=0))
        product_ref[d * block : (d + 1) * block, :] = terms[:block] + terms[block:]

    @pl.when(jnp.logical_not(residual < 1e-3))
    def _():
        gram_ref[...] = gram
        eliminate(gram_ref, inverse_ref)

    inverse = inverse_ref[...]
    basis_ref[...] = dot_t3(mine_ref[...], inverse)
    size = min(512, documents * block)
    for at in range(0, documents * block, size):
        factors_ref[at : at + size, :] = dot_t3(product_ref[at : at + size, :], inverse).astype(BF16)


def body(plan, blocks, rows, counts, sketch, weights):
    documents, slots, block, _ = blocks.shape
    columns = sketch.shape[1]
    features = weights.shape[0]
    half = features // 2
    chunk = half // plan.plane
    flat = plan.flat
    params = pltpu.CompilerParams(vmem_limit_bytes=VMEM_BYTES)
    shape = jax.ShapeDtypeStruct
    rows = rows.T
    parts = min(4, documents)

    total, *send = pl.pallas_call(
        functools.partial(sum_kernel, plan),
        out_shape=(pltpu.VMEM((features, columns), F32),) + (pltpu.VMEM((chunk, columns), BF16),) * plan.plane,
        in_specs=[pl.BlockSpec(memory_space=pltpu.HBM)] * 4,
        out_specs=(whole(),) * (1 + plan.plane),
        scratch_shapes=[
            pltpu.VMEM(blocks.shape, BF16),
            pltpu.VMEM(sketch.shape, BF16),
            pltpu.SMEM(rows.shape, jnp.int32),
            pltpu.SMEM(counts.shape, jnp.int32),
            pltpu.SemaphoreType.DMA((parts, 2)),
            pltpu.SemaphoreType.DMA((2,)),
        ],
        compiler_params=params,
        name="local_sum",
    )(in_hbm(rows), in_hbm(counts), in_hbm(blocks), in_hbm(sketch))

    lines = weights.reshape(features // block, block)
    tiles = pl.pallas_call(
        tiles_kernel,
        out_shape=shape((documents, 2 * block, slots * block), BF16),
        in_specs=[scalars(), scalars(), whole(), whole()],
        out_specs=whole(),
        compiler_params=params,
        cost_estimate=pl.CostEstimate(flops=1 << 20, bytes_accessed=4 << 20, transcendentals=0),
        name="tiles",
    )(rows, counts, blocks, lines)
    scale = pl.pallas_call(
        functools.partial(scale_kernel, plan),
        out_shape=shape((flat, columns), F32),
        in_specs=[whole()],
        out_specs=whole(),
        scratch_shapes=[pltpu.VMEM((max(flat, block), block), F32)],
        compiler_params=params,
        name="scale",
    )(lines)

    middle = chunk // 2
    others = range(1, plan.plane)
    got = {p: plan.swap(send[p], 1) for p in (*others, 0)}
    got[plan.plane - 1], got[0] = lax.optimization_barrier((got[plan.plane - 1], got[0]))
    chip = {}
    for p in others:
        chip[p] = pl.pallas_call(
            functools.partial(chip_kernel, p * chunk),
            out_shape=[shape((middle, columns), BF16)] * 2,
            in_specs=[whole(), whole()],
            out_specs=[whole()] * 2,
            compiler_params=params,
            name="chip_sum",
        )(total, got[p])
    far_sent = [plan.swap_plane(chip[p][0], p) for p in others]
    near_sent = [plan.swap_plane(chip[p][1], p) for p in others]
    far_sent, scale = lax.optimization_barrier((far_sent, scale))

    def plane_sum(sent, start, dtypes):
        return pl.pallas_call(
            functools.partial(plane_kernel, flat, start),
            out_shape=[shape((flat, columns), dtype) for dtype in dtypes],
            in_specs=[whole()] * (2 + len(sent)),
            out_specs=[whole()] * len(dtypes),
            compiler_params=params,
            name="plane_sum",
        )(total, got[0], *sent)

    split_at = plan.line // 2
    far = plane_sum(far_sent, middle, [BF16] * split_at)
    far = [plan.swap_line(part, split_at + q) for q, part in enumerate(far)]
    held, *near = plane_sum(near_sent, 0, [F32] + [BF16] * (split_at - 1))
    near = [plan.swap_line(part, 1 + q) for q, part in enumerate(near)]
    near, far, tiles = lax.optimization_barrier((near, far, tiles))
    mine, rounded = pl.pallas_call(
        line_kernel,
        out_shape=(shape((flat, columns), F32), shape((flat, columns), BF16)),
        in_specs=[whole()] * (1 + plan.line),
        out_specs=(whole(), whole()),
        compiler_params=params,
        name="line_sum",
    )(held, scale, *near, *far)

    line = [rounded] + [plan.swap_line(rounded, q) for q in range(1, plan.line)]
    near, far = jnp.concatenate(line[:split_at], axis=0), jnp.concatenate(line[split_at:], axis=0)
    near = [near] + [plan.swap_plane(near, p) for p in reversed(others)]
    far = [far] + [plan.swap_plane(far, p) for p in others]
    own = far + near
    other = [plan.swap(part, 1) for part in own]

    pieces = own + other
    late = range(len(own) + 1, len(own) + plan.plane)
    gram = pl.pallas_call(
        gram_kernel,
        out_shape=shape((columns, columns), F32),
        in_specs=[whole()] * (len(pieces) - len(late)),
        out_specs=whole(),
        compiler_params=params,
        cost_estimate=pl.CostEstimate(flops=2 * features * columns * columns, bytes_accessed=4 << 20, transcendentals=0),
        name="gram",
    )(*[piece for i, piece in enumerate(pieces) if i not in late])
    return pl.pallas_call(
        functools.partial(last_kernel, plan, features, late),
        out_shape=(shape((flat, columns), F32), shape((documents * block, columns), BF16)),
        in_specs=[scalars()] + [whole()] * (3 + len(pieces)),
        out_specs=(whole(), whole()),
        scratch_shapes=[
            pltpu.VMEM((features, columns), BF16),
            pltpu.VMEM((documents * block, columns), F32),
            pltpu.VMEM((columns, columns), F32),
            pltpu.VMEM((columns, columns), F32),
        ],
        compiler_params=params,
        name="factors",
    )(rows, tiles, mine, gram, *pieces)


def solution(mesh):
    placed = (
        P(AXES, None, None, None),
        P(AXES, None),
        P(AXES),
        P(AXES, None),
        P(),
    )

    def run(blocks, rows, counts, sketch, weights):
        plan = Plan(mesh.shape["row"], mesh.shape["col"], weights.shape[0], blocks.shape[2])
        return jax.shard_map(
            functools.partial(body, plan),
            mesh=mesh,
            in_specs=placed,
            out_specs=(P(AXES, None), P(AXES, None)),
            check_vma=False,
        )(blocks, rows, counts, sketch, weights)

    return run
```

```python
import functools

import jax
import jax.numpy as jnp
from jax import lax
from jax.experimental import pallas as pl
from jax.experimental.pallas import tpu as pltpu
from jax.sharding import PartitionSpec as P

F32 = jnp.float32
BF16 = jnp.bfloat16
AXES = ("row", "col")
VMEM_BYTES = 48 * 1024 * 1024


def whole():
    return pl.BlockSpec(memory_space=pltpu.VMEM)


def in_hbm(value):
    return pltpu.with_memory_space_constraint(value, pltpu.HBM)


def scalars():
    return pl.BlockSpec(memory_space=pltpu.SMEM)


class Plan:
    def __init__(self, rows, cols, features, block):
        self.count = rows * cols
        self.cols = cols
        self.plane = cols
        self.line = rows // 2
        self.plane_bits = cols.bit_length() - 1
        assert self.plane * self.line * 2 == self.count and self.count & (self.count - 1) == 0
        self.flat = features // self.count
        self.piece = min(self.flat, block)
        self.pieces = block // self.piece
        per_slice = self.flat // self.piece
        self.slice_bits = per_slice.bit_length() - 1
        assert 1 << self.slice_bits == per_slice and self.piece * self.pieces == block

    def me(self):
        return lax.axis_index("row") * self.cols + lax.axis_index("col")

    def start(self, me, feature_block, piece):
        unit = feature_block * self.pieces + piece
        owner = unit >> self.slice_bits
        inside = unit & ((1 << self.slice_bits) - 1)
        apart = owner ^ me
        place = (apart & 1) * self.plane + ((apart >> 1) & (self.plane - 1))
        place = place * self.line + (apart >> (1 + self.plane_bits))
        return pl.multiple_of(place * self.flat + inside * self.piece, self.piece)

    def swap(self, value, mask):
        return lax.ppermute(value, AXES, [(d, d ^ mask) for d in range(self.count)])

    def swap_plane(self, value, member):
        return self.swap(value, member << 1)

    def swap_line(self, value, member):
        return self.swap(value, member << (1 + self.plane_bits))


def sum_kernel(plan, rows_hbm, counts_hbm, blocks_ref, sketch_ref, total_ref, *rest):
    first_ref, other_ref, tiles_ref, docs_ref, rows_ref, counts_ref, sems, small_sems = rest
    me = plan.me()
    documents, slots, block, _ = tiles_ref.shape
    half = total_ref.shape[0] // 2
    parts = sems.shape[0]
    per = documents // parts
    small = (
        pltpu.make_async_copy(rows_hbm, rows_ref, small_sems.at[0]),
        pltpu.make_async_copy(counts_hbm, counts_ref, small_sems.at[1]),
    )
    for copy in small:
        copy.start()
    copies = []
    for c in range(parts):
        tiles_at = pl.ds(c * per, per)
        docs_at = pl.ds(c * per * block, per * block)
        pair = (
            pltpu.make_async_copy(blocks_ref.at[tiles_at], tiles_ref.at[tiles_at], sems.at[c, 0]),
            pltpu.make_async_copy(sketch_ref.at[docs_at], docs_ref.at[docs_at], sems.at[c, 1]),
        )
        for copy in pair:
            copy.start()
        copies.append(pair)
    total_ref[...] = jnp.zeros_like(total_ref)
    for copy in small:
        copy.wait()
    for c in range(parts):
        for copy in copies[c]:
            copy.wait()
        for d in range(c * per, (c + 1) * per):
            docs = docs_ref[d * block : (d + 1) * block, :]
            terms = jnp.dot(tiles_ref[d].reshape(slots * block, block), docs, preferred_element_type=F32)
            for s in range(slots):
                term = jnp.where(s < counts_ref[d], terms[s * block : (s + 1) * block], 0.0)
                for p in range(plan.pieces):
                    at = pl.ds(plan.start(me, rows_ref[s, d], p), plan.piece)
                    total_ref[at, :] += term[p * plan.piece : (p + 1) * plan.piece]
    later = other_ref.shape[0]
    first_ref[...] = total_ref[half + later :, :].astype(BF16)
    other_ref[...] = total_ref[half : half + later, :].astype(BF16)


def tiles_kernel(rows_ref, counts_ref, blocks_ref, weights_ref, out_ref):
    documents, slots, block, _ = blocks_ref.shape
    for d in range(documents):
        for s in range(slots):
            scale = weights_ref[pl.ds(rows_ref[s, d], 1), :]
            scale = jnp.where(s < counts_ref[d], scale, 0.0)
            high, low = split(blocks_ref[d, s].T.astype(F32) * scale)
            out_ref[d, :block, s * block : (s + 1) * block] = high
            out_ref[d, block:, s * block : (s + 1) * block] = low


def scale_kernel(plan, weights_ref, scale_ref, turned_ref):
    block = weights_ref.shape[1]
    unit = plan.me() << plan.slice_bits
    lines = max(1, plan.flat // block)
    first = unit if plan.pieces == 1 else unit // plan.pieces
    for i in range(lines):
        line = weights_ref[pl.ds(first + i, 1), :]
        turned_ref[i * block : (i + 1) * block, :] = jnp.broadcast_to(line, (block, block)).T
    inside = 0 if plan.pieces == 1 else lax.rem(unit, plan.pieces) * plan.piece
    scale_ref[...] = turned_ref[pl.ds(pl.multiple_of(inside, plan.piece), plan.flat), :]


def chip_kernel(start, got_start, total_ref, got_ref, far_ref, near_ref):
    middle = near_ref.shape[0]
    for ref, at in ((far_ref, middle), (near_ref, 0)):
        held = total_ref[start + at : start + at + middle, :]
        got = got_ref[got_start + at : got_start + at + middle, :]
        ref[...] = (held + got.astype(F32)).astype(BF16)


def plane_kernel(flat, start, total_ref, got_ref, *rest):
    count = rest[0].shape[0] // flat
    parts, out_refs = rest[:-count], rest[-count:]
    for q, out_ref in enumerate(out_refs):
        at = slice(start + q * flat, start + (q + 1) * flat)
        total = total_ref[at, :] + got_ref[at, :].astype(F32)
        for ref in parts:
            total = total + ref[q * flat : (q + 1) * flat, :].astype(F32)
        out_ref[...] = total.astype(out_ref.dtype)


def line_kernel(held_ref, scale_ref, *rest):
    parts, (mine_ref, rounded_ref) = rest[:-2], rest[-2:]
    total = held_ref[...]
    for ref in parts:
        total = total + ref[...].astype(F32)
    total = total * scale_ref[...]
    mine_ref[...] = total
    rounded_ref[...] = total.astype(BF16)


def split(value):
    high = value.astype(BF16)
    return high, (value - high.astype(F32)).astype(BF16)


def dot_t(a, b):
    return lax.dot_general(a, b, (((1,), (1,)), ((), ())), preferred_element_type=F32)


def both(total):
    size = total.shape[1] // 2
    return total[:, :size] + total[:, size:]


def dot_t3(a, b):
    b_high, b_low = split(b)
    top = jnp.concatenate([b_high, b_high], axis=1)
    low = jnp.concatenate([b_low, jnp.zeros_like(b_low)], axis=1)
    return both(dot_t(jnp.concatenate(split(a), axis=1), jnp.concatenate([top, low], axis=0)))


def dot3(a, b):
    b_high, b_low = split(b)
    top = jnp.concatenate([b_high, b_low], axis=1)
    low = jnp.concatenate([b_high, jnp.zeros_like(b_low)], axis=1)
    return both(dot(jnp.concatenate(split(a), axis=1), jnp.concatenate([top, low], axis=0)))


def dot(a, b):
    return jnp.dot(a, b, preferred_element_type=F32)


def dot1(a, b):
    return dot(a.astype(BF16), b.astype(BF16))


def dot_t1(a, b):
    return dot_t(a.astype(BF16), b.astype(BF16))


def eliminate(gram_ref, inverse_ref):
    size = gram_ref.shape[0]
    lane = lax.broadcasted_iota(jnp.int32, (size, size), 1)
    line = lax.broadcasted_iota(jnp.int32, (size, 1), 0)
    first = lax.broadcasted_iota(jnp.int32, (1, size), 1)
    inverse_ref[...] = jnp.where(lane == line, 1.0, 0.0)

    def step(j, carry):
        values = gram_ref[...]
        pivot_row = gram_ref[pl.ds(j, 1), :]
        pivot = jnp.sum(jnp.where(first == j, pivot_row, 0.0), axis=1, keepdims=True)
        scale = 1.0 / jnp.sqrt(pivot)
        column = jnp.sum(jnp.where(lane == j, values, 0.0), axis=1, keepdims=True)
        column = jnp.where(line > j, column * scale, 0.0)
        gram_ref[...] = values - column * (pivot_row * scale)
        own_row = inverse_ref[pl.ds(j, 1), :] * scale
        inverse_ref[...] = jnp.where(line == j, own_row, inverse_ref[...] - column * own_row)
        return carry

    lax.fori_loop(0, size, step, 0)


def newton(gram, inverse_ref):
    size = gram.shape[0]
    line = lax.broadcasted_iota(jnp.int32, (size, size), 0)
    lane = lax.broadcasted_iota(jnp.int32, (size, size), 1)
    same = line == lane
    eye = jnp.where(same, 1.0, 0.0)
    take = jnp.where(line > lane, 1.0, jnp.where(same, 0.5, 0.0))
    diagonal = jnp.where(same, gram, 0.0)
    down = 1.0 / jnp.sqrt(jnp.sum(diagonal, axis=1, keepdims=True))
    across = 1.0 / jnp.sqrt(jnp.sum(diagonal, axis=0, keepdims=True))
    beyond = gram * down * across - eye
    factor = eye - take * beyond
    for product, product_t in ((dot1, dot_t1), (dot3, dot_t3)):
        left = factor - eye + product(factor, beyond)
        residual = factor.T - eye + product_t(left, factor)
        factor = factor - product(take * residual, factor)
    inverse_ref[...] = factor * across
    return jnp.sum(residual * residual)


def place(plan, index, size):
    core, later = divmod(index, 2 * plan.plane)
    near, member = divmod(later, plan.plane)
    if near and member:
        member = plan.plane - member
    return ((core * plan.plane + member) * 2 + 1 - near) * size


def take(plan, indices, refs, all_ref, gram):
    for index, ref in zip(indices, refs):
        size = ref.shape[0]
        base = place(plan, index, size)
        part = ref[...]
        all_ref[base : base + size, :] = part
        gram += lax.dot_general(part, part, (((0,), (0,)), ((), ())), preferred_element_type=F32)
    return gram


def gather_kernel(plan, indices, before, *refs):
    parts, (all_ref, gram_ref) = refs[-2 - len(indices) : -2], refs[-2:]
    gram = refs[1][...] if before else jnp.zeros(gram_ref.shape, F32)
    gram_ref[...] = take(plan, indices, parts, all_ref, gram)


def last_kernel(plan, features, late, rows_ref, tiles_ref, mine_ref, _, early_ref, *rest):
    parts = rest[: len(late)]
    basis_ref, factors_ref, all_ref, product_ref, gram_ref, inverse_ref = rest[len(late) :]
    me = plan.me()
    documents = tiles_ref.shape[0]
    block = tiles_ref.shape[1] // 2
    slots = tiles_ref.shape[2] // block
    gram = take(plan, late, parts, all_ref, early_ref[...])
    gram = gram * (1.0 / features)
    residual = newton(gram, inverse_ref)
    for d in range(documents):
        picked = []
        for s in range(slots):
            for p in range(plan.pieces):
                at = pl.ds(plan.start(me, rows_ref[s, d], p), plan.piece)
                picked.append(all_ref[at, :])
        terms = dot(tiles_ref[d], jnp.concatenate(picked, axis=0))
        product_ref[d * block : (d + 1) * block, :] = terms[:block] + terms[block:]

    @pl.when(jnp.logical_not(residual < 1e-3))
    def _():
        gram_ref[...] = gram
        eliminate(gram_ref, inverse_ref)

    inverse = inverse_ref[...]
    basis_ref[...] = dot_t3(mine_ref[...], inverse)
    size = min(512, documents * block)
    for at in range(0, documents * block, size):
        factors_ref[at : at + size, :] = dot_t3(product_ref[at : at + size, :], inverse).astype(BF16)


def body(plan, blocks, rows, counts, sketch, weights):
    documents, slots, block, _ = blocks.shape
    columns = sketch.shape[1]
    features = weights.shape[0]
    half = features // 2
    chunk = half // plan.plane
    flat = plan.flat
    params = pltpu.CompilerParams(vmem_limit_bytes=VMEM_BYTES)
    shape = jax.ShapeDtypeStruct
    rows = rows.T
    parts = min(4, documents)

    total, first, later = pl.pallas_call(
        functools.partial(sum_kernel, plan),
        out_shape=(
            pltpu.VMEM((features, columns), F32),
            pltpu.VMEM((chunk, columns), BF16),
            pltpu.VMEM((half - chunk, columns), BF16),
        ),
        in_specs=[pl.BlockSpec(memory_space=pltpu.HBM)] * 4,
        out_specs=(whole(),) * 3,
        scratch_shapes=[
            pltpu.VMEM(blocks.shape, BF16),
            pltpu.VMEM(sketch.shape, BF16),
            pltpu.SMEM(rows.shape, jnp.int32),
            pltpu.SMEM(counts.shape, jnp.int32),
            pltpu.SemaphoreType.DMA((parts, 2)),
            pltpu.SemaphoreType.DMA((2,)),
        ],
        compiler_params=params,
        name="local_sum",
    )(in_hbm(rows), in_hbm(counts), in_hbm(blocks), in_hbm(sketch))

    lines = weights.reshape(features // block, block)
    tiles = pl.pallas_call(
        tiles_kernel,
        out_shape=shape((documents, 2 * block, slots * block), BF16),
        in_specs=[scalars(), scalars(), whole(), whole()],
        out_specs=whole(),
        compiler_params=params,
        cost_estimate=pl.CostEstimate(flops=1 << 20, bytes_accessed=4 << 20, transcendentals=0),
        name="tiles",
    )(rows, counts, blocks, lines)
    scale = pl.pallas_call(
        functools.partial(scale_kernel, plan),
        out_shape=shape((flat, columns), F32),
        in_specs=[whole()],
        out_specs=whole(),
        scratch_shapes=[pltpu.VMEM((max(flat, block), block), F32)],
        compiler_params=params,
        name="scale",
    )(lines)

    middle = chunk // 2
    others = range(1, plan.plane)
    first, later = plan.swap(first, 1), plan.swap(later, 1)
    chip = {}
    for p in others:
        last = p == plan.plane - 1
        chip[p] = pl.pallas_call(
            functools.partial(chip_kernel, p * chunk, 0 if last else p * chunk),
            out_shape=[shape((middle, columns), BF16)] * 2,
            in_specs=[whole(), whole()],
            out_specs=[whole()] * 2,
            compiler_params=params,
            name="chip_sum",
        )(total, first if last else later)
    far_sent = [plan.swap_plane(chip[p][0], p) for p in others]
    near_sent = [plan.swap_plane(chip[p][1], p) for p in others]
    far_sent, scale = lax.optimization_barrier((far_sent, scale))

    def plane_sum(sent, start, dtypes):
        return pl.pallas_call(
            functools.partial(plane_kernel, flat, start),
            out_shape=[shape((flat, columns), dtype) for dtype in dtypes],
            in_specs=[whole()] * (2 + len(sent)),
            out_specs=[whole()] * len(dtypes),
            compiler_params=params,
            name="plane_sum",
        )(total, later, *sent)

    split_at = plan.line // 2
    far = plane_sum(far_sent, middle, [BF16] * split_at)
    far = [plan.swap_line(part, split_at + q) for q, part in enumerate(far)]
    held, *near = plane_sum(near_sent, 0, [F32] + [BF16] * (split_at - 1))
    near = [plan.swap_line(part, 1 + q) for q, part in enumerate(near)]
    far, near, tiles = lax.optimization_barrier((far, near, tiles))
    mine, rounded = pl.pallas_call(
        line_kernel,
        out_shape=(shape((flat, columns), F32), shape((flat, columns), BF16)),
        in_specs=[whole()] * (1 + plan.line),
        out_specs=(whole(), whole()),
        compiler_params=params,
        name="line_sum",
    )(held, scale, *near, *far)

    line = [rounded] + [plan.swap_line(rounded, q) for q in range(1, plan.line)]
    near, far = jnp.concatenate(line[:split_at], axis=0), jnp.concatenate(line[split_at:], axis=0)
    near = [near] + [plan.swap_plane(near, p) for p in reversed(others)]
    far = [far] + [plan.swap_plane(far, p) for p in others]
    own = far + near
    other = [plan.swap(part, 1) for part in own]

    pieces = own + other
    count = len(own)
    gathered = (pltpu.VMEM((features, columns), BF16), pltpu.VMEM((columns, columns), F32))

    def gather(before, indices):
        return pl.pallas_call(
            functools.partial(gather_kernel, plan, indices, bool(before)),
            out_shape=gathered,
            in_specs=[whole()] * (len(before) + len(indices)),
            out_specs=(whole(), whole()),
            input_output_aliases={0: 0} if before else {},
            compiler_params=params,
            cost_estimate=pl.CostEstimate(
                flops=2 * middle * len(indices) * columns * columns, bytes_accessed=2 << 20, transcendentals=0
            ),
            name="gram",
        )(*before, *[pieces[i] for i in indices])

    late = list(range(count + 1, count + plan.plane))
    early = list(range(plan.plane, count)) + [0]
    between = [i for i in range(2 * count) if i not in late and i not in early]
    state = gather(gather((), early), between)
    basis, factors, _ = pl.pallas_call(
        functools.partial(last_kernel, plan, features, late),
        out_shape=(shape((flat, columns), F32), shape((documents * block, columns), BF16), gathered[0]),
        in_specs=[scalars()] + [whole()] * (4 + len(late)),
        out_specs=(whole(),) * 3,
        input_output_aliases={3: 2},
        scratch_shapes=[
            pltpu.VMEM((documents * block, columns), F32),
            pltpu.VMEM((columns, columns), F32),
            pltpu.VMEM((columns, columns), F32),
        ],
        compiler_params=params,
        name="factors",
    )(rows, tiles, mine, *state, *[pieces[i] for i in late])
    return basis, factors


def solution(mesh):
    placed = (
        P(AXES, None, None, None),
        P(AXES, None),
        P(AXES),
        P(AXES, None),
        P(),
    )

    def run(blocks, rows, counts, sketch, weights):
        plan = Plan(mesh.shape["row"], mesh.shape["col"], weights.shape[0], blocks.shape[2])
        return jax.shard_map(
            functools.partial(body, plan),
            mesh=mesh,
            in_specs=placed,
            out_specs=(P(AXES, None), P(AXES, None)),
            check_vma=False,
        )(blocks, rows, counts, sketch, weights)

    return run
```

```python
import functools

import jax
import jax.numpy as jnp
from jax import lax
from jax.experimental import pallas as pl
from jax.experimental.pallas import tpu as pltpu
from jax.sharding import PartitionSpec as P

F32 = jnp.float32
BF16 = jnp.bfloat16
AXES = ("row", "col")
VMEM_BYTES = 48 * 1024 * 1024


def whole():
    return pl.BlockSpec(memory_space=pltpu.VMEM)


def in_hbm(value):
    return pltpu.with_memory_space_constraint(value, pltpu.HBM)


def scalars():
    return pl.BlockSpec(memory_space=pltpu.SMEM)


class Plan:
    def __init__(self, rows, cols, features, block):
        self.count = rows * cols
        self.cols = cols
        self.plane = cols
        self.line = rows // 2
        self.plane_bits = cols.bit_length() - 1
        assert self.plane * self.line * 2 == self.count and self.count & (self.count - 1) == 0
        self.flat = features // self.count
        self.piece = min(self.flat, block)
        self.pieces = block // self.piece
        per_slice = self.flat // self.piece
        self.slice_bits = per_slice.bit_length() - 1
        assert 1 << self.slice_bits == per_slice and self.piece * self.pieces == block

    def me(self):
        return lax.axis_index("row") * self.cols + lax.axis_index("col")

    def start(self, me, feature_block, piece):
        unit = feature_block * self.pieces + piece
        owner = unit >> self.slice_bits
        inside = unit & ((1 << self.slice_bits) - 1)
        apart = owner ^ me
        place = (apart & 1) * self.plane + ((apart >> 1) & (self.plane - 1))
        place = place * self.line + (apart >> (1 + self.plane_bits))
        return pl.multiple_of(place * self.flat + inside * self.piece, self.piece)

    def swap(self, value, mask):
        return lax.ppermute(value, AXES, [(d, d ^ mask) for d in range(self.count)])

    def swap_plane(self, value, member):
        return self.swap(value, member << 1)

    def swap_line(self, value, member):
        return self.swap(value, member << (1 + self.plane_bits))


def sum_kernel(plan, rows_hbm, counts_hbm, blocks_ref, sketch_ref, total_ref, *rest):
    send_refs, (tiles_ref, docs_ref, rows_ref, counts_ref, sems, small_sems) = rest[: plan.plane], rest[plan.plane :]
    me = plan.me()
    documents, slots, block, _ = tiles_ref.shape
    half = total_ref.shape[0] // 2
    parts = sems.shape[0]
    per = documents // parts
    small = (
        pltpu.make_async_copy(rows_hbm, rows_ref, small_sems.at[0]),
        pltpu.make_async_copy(counts_hbm, counts_ref, small_sems.at[1]),
    )
    for copy in small:
        copy.start()
    copies = []
    for c in range(parts):
        tiles_at = pl.ds(c * per, per)
        docs_at = pl.ds(c * per * block, per * block)
        pair = (
            pltpu.make_async_copy(blocks_ref.at[tiles_at], tiles_ref.at[tiles_at], sems.at[c, 0]),
            pltpu.make_async_copy(sketch_ref.at[docs_at], docs_ref.at[docs_at], sems.at[c, 1]),
        )
        for copy in pair:
            copy.start()
        copies.append(pair)
    total_ref[...] = jnp.zeros_like(total_ref)
    for copy in small:
        copy.wait()
    for c in range(parts):
        for copy in copies[c]:
            copy.wait()
        for d in range(c * per, (c + 1) * per):
            docs = docs_ref[d * block : (d + 1) * block, :]
            terms = jnp.dot(tiles_ref[d].reshape(slots * block, block), docs, preferred_element_type=F32)
            for s in range(slots):
                term = jnp.where(s < counts_ref[d], terms[s * block : (s + 1) * block], 0.0)
                for p in range(plan.pieces):
                    at = pl.ds(plan.start(me, rows_ref[s, d], p), plan.piece)
                    total_ref[at, :] += term[p * plan.piece : (p + 1) * plan.piece]
    for p, send_ref in enumerate(send_refs):
        size = send_ref.shape[0]
        send_ref[...] = total_ref[half + p * size : half + (p + 1) * size, :].astype(BF16)


def tiles_kernel(rows_ref, counts_ref, blocks_ref, weights_ref, out_ref):
    documents, slots, block, _ = blocks_ref.shape
    for d in range(documents):
        for s in range(slots):
            scale = weights_ref[pl.ds(rows_ref[s, d], 1), :]
            scale = jnp.where(s < counts_ref[d], scale, 0.0)
            high, low = split(blocks_ref[d, s].T.astype(F32) * scale)
            out_ref[d, :block, s * block : (s + 1) * block] = high
            out_ref[d, block:, s * block : (s + 1) * block] = low


def scale_kernel(plan, weights_ref, scale_ref, turned_ref):
    block = weights_ref.shape[1]
    unit = plan.me() << plan.slice_bits
    lines = max(1, plan.flat // block)
    first = unit if plan.pieces == 1 else unit // plan.pieces
    for i in range(lines):
        line = weights_ref[pl.ds(first + i, 1), :]
        turned_ref[i * block : (i + 1) * block, :] = jnp.broadcast_to(line, (block, block)).T
    inside = 0 if plan.pieces == 1 else lax.rem(unit, plan.pieces) * plan.piece
    scale_ref[...] = turned_ref[pl.ds(pl.multiple_of(inside, plan.piece), plan.flat), :]


def chip_kernel(start, total_ref, got_ref, far_ref, near_ref):
    middle = near_ref.shape[0]
    for ref, at in ((far_ref, middle), (near_ref, 0)):
        held = total_ref[start + at : start + at + middle, :]
        ref[...] = (held + got_ref[at : at + middle, :].astype(F32)).astype(BF16)


def plane_kernel(flat, start, total_ref, got_ref, *rest):
    count = rest[0].shape[0] // flat
    parts, out_refs = rest[:-count], rest[-count:]
    for q, out_ref in enumerate(out_refs):
        at = slice(start + q * flat, start + (q + 1) * flat)
        total = total_ref[at, :] + got_ref[at, :].astype(F32)
        for ref in parts:
            total = total + ref[q * flat : (q + 1) * flat, :].astype(F32)
        out_ref[...] = total.astype(out_ref.dtype)


def line_kernel(held_ref, scale_ref, *rest):
    parts, (mine_ref, rounded_ref) = rest[:-2], rest[-2:]
    total = held_ref[...]
    for ref in parts:
        total = total + ref[...].astype(F32)
    total = total * scale_ref[...]
    mine_ref[...] = total
    rounded_ref[...] = total.astype(BF16)


def split(value):
    high = value.astype(BF16)
    return high, (value - high.astype(F32)).astype(BF16)


def dot_t(a, b):
    return lax.dot_general(a, b, (((1,), (1,)), ((), ())), preferred_element_type=F32)


def both(total):
    size = total.shape[1] // 2
    return total[:, :size] + total[:, size:]


def dot_t3(a, b):
    b_high, b_low = split(b)
    top = jnp.concatenate([b_high, b_high], axis=1)
    low = jnp.concatenate([b_low, jnp.zeros_like(b_low)], axis=1)
    return both(dot_t(jnp.concatenate(split(a), axis=1), jnp.concatenate([top, low], axis=0)))


def dot3(a, b):
    b_high, b_low = split(b)
    top = jnp.concatenate([b_high, b_low], axis=1)
    low = jnp.concatenate([b_high, jnp.zeros_like(b_low)], axis=1)
    return both(dot(jnp.concatenate(split(a), axis=1), jnp.concatenate([top, low], axis=0)))


def dot(a, b):
    return jnp.dot(a, b, preferred_element_type=F32)


def dot1(a, b):
    return dot(a.astype(BF16), b.astype(BF16))


def dot_t1(a, b):
    return dot_t(a.astype(BF16), b.astype(BF16))


def eliminate(gram_ref, inverse_ref):
    size = gram_ref.shape[0]
    lane = lax.broadcasted_iota(jnp.int32, (size, size), 1)
    line = lax.broadcasted_iota(jnp.int32, (size, 1), 0)
    first = lax.broadcasted_iota(jnp.int32, (1, size), 1)
    inverse_ref[...] = jnp.where(lane == line, 1.0, 0.0)

    def step(j, carry):
        values = gram_ref[...]
        pivot_row = gram_ref[pl.ds(j, 1), :]
        pivot = jnp.sum(jnp.where(first == j, pivot_row, 0.0), axis=1, keepdims=True)
        scale = 1.0 / jnp.sqrt(pivot)
        column = jnp.sum(jnp.where(lane == j, values, 0.0), axis=1, keepdims=True)
        column = jnp.where(line > j, column * scale, 0.0)
        gram_ref[...] = values - column * (pivot_row * scale)
        own_row = inverse_ref[pl.ds(j, 1), :] * scale
        inverse_ref[...] = jnp.where(line == j, own_row, inverse_ref[...] - column * own_row)
        return carry

    lax.fori_loop(0, size, step, 0)


def newton(gram, inverse_ref):
    size = gram.shape[0]
    line = lax.broadcasted_iota(jnp.int32, (size, size), 0)
    lane = lax.broadcasted_iota(jnp.int32, (size, size), 1)
    same = line == lane
    eye = jnp.where(same, 1.0, 0.0)
    take = jnp.where(line > lane, 1.0, jnp.where(same, 0.5, 0.0))
    diagonal = jnp.where(same, gram, 0.0)
    down = 1.0 / jnp.sqrt(jnp.sum(diagonal, axis=1, keepdims=True))
    across = 1.0 / jnp.sqrt(jnp.sum(diagonal, axis=0, keepdims=True))
    beyond = gram * down * across - eye
    factor = eye - take * beyond
    for product, product_t in ((dot1, dot_t1), (dot3, dot_t3)):
        left = factor - eye + product(factor, beyond)
        residual = factor.T - eye + product_t(left, factor)
        factor = factor - product(take * residual, factor)
    inverse_ref[...] = factor * across
    return jnp.sum(residual * residual)


def gram_kernel(*refs):
    gram = jnp.zeros(refs[-1].shape, F32)
    for ref in refs[:-1]:
        part = ref[...]
        gram += lax.dot_general(part, part, (((0,), (0,)), ((), ())), preferred_element_type=F32)
    refs[-1][...] = gram


def last_kernel(plan, features, late, rows_ref, tiles_ref, mine_ref, early_ref, *rest):
    parts, (basis_ref, factors_ref) = rest[: 4 * plan.plane], rest[4 * plan.plane : 4 * plan.plane + 2]
    all_ref, product_ref, gram_ref, inverse_ref, near_basis_ref, near_factors_ref, sems = rest[4 * plan.plane + 2 :]
    me = plan.me()
    documents = tiles_ref.shape[0]
    block = tiles_ref.shape[1] // 2
    slots = tiles_ref.shape[2] // block
    gram = early_ref[...]
    for i, ref in enumerate(parts):
        size = ref.shape[0]
        core, later = divmod(i, 2 * plan.plane)
        near, member = divmod(later, plan.plane)
        if near and member:
            member = plan.plane - member
        base = ((core * plan.plane + member) * 2 + 1 - near) * size
        part = ref[...]
        all_ref[base : base + size, :] = part
        if i in late:
            gram += lax.dot_general(part, part, (((0,), (0,)), ((), ())), preferred_element_type=F32)
    gram = gram * (1.0 / features)
    residual = newton(gram, inverse_ref)
    for d in range(documents):
        picked = []
        for s in range(slots):
            for p in range(plan.pieces):
                at = pl.ds(plan.start(me, rows_ref[s, d], p), plan.piece)
                picked.append(all_ref[at, :])
        terms = dot(tiles_ref[d], jnp.concatenate(picked, axis=0))
        product_ref[d * block : (d + 1) * block, :] = terms[:block] + terms[block:]

    @pl.when(jnp.logical_not(residual < 1e-3))
    def _():
        gram_ref[...] = gram
        eliminate(gram_ref, inverse_ref)

    inverse = inverse_ref[...]
    near_basis_ref[...] = dot_t3(mine_ref[...], inverse)
    copies = [pltpu.make_async_copy(near_basis_ref, basis_ref, sems.at[0])]
    copies[0].start()
    steps = sems.shape[0] - 1
    size = documents * block // steps
    for i in range(steps):
        at = pl.ds(i * size, size)
        near_factors_ref[at, :] = dot_t3(product_ref[at, :], inverse).astype(BF16)
        copies.append(pltpu.make_async_copy(near_factors_ref.at[at], factors_ref.at[at], sems.at[i + 1]))
        copies[-1].start()
    for copy in copies:
        copy.wait()


def body(plan, blocks, rows, counts, sketch, weights):
    documents, slots, block, _ = blocks.shape
    columns = sketch.shape[1]
    features = weights.shape[0]
    half = features // 2
    chunk = half // plan.plane
    flat = plan.flat
    params = pltpu.CompilerParams(vmem_limit_bytes=VMEM_BYTES)
    shape = jax.ShapeDtypeStruct
    rows = rows.T
    parts = min(4, documents)

    total, *send = pl.pallas_call(
        functools.partial(sum_kernel, plan),
        out_shape=(pltpu.VMEM((features, columns), F32),) + (pltpu.VMEM((chunk, columns), BF16),) * plan.plane,
        in_specs=[pl.BlockSpec(memory_space=pltpu.HBM)] * 4,
        out_specs=(whole(),) * (1 + plan.plane),
        scratch_shapes=[
            pltpu.VMEM(blocks.shape, BF16),
            pltpu.VMEM(sketch.shape, BF16),
            pltpu.SMEM(rows.shape, jnp.int32),
            pltpu.SMEM(counts.shape, jnp.int32),
            pltpu.SemaphoreType.DMA((parts, 2)),
            pltpu.SemaphoreType.DMA((2,)),
        ],
        compiler_params=params,
        name="local_sum",
    )(in_hbm(rows), in_hbm(counts), in_hbm(blocks), in_hbm(sketch))

    lines = weights.reshape(features // block, block)
    tiles = pl.pallas_call(
        tiles_kernel,
        out_shape=shape((documents, 2 * block, slots * block), BF16),
        in_specs=[scalars(), scalars(), whole(), whole()],
        out_specs=whole(),
        compiler_params=params,
        cost_estimate=pl.CostEstimate(flops=1 << 20, bytes_accessed=4 << 20, transcendentals=0),
        name="tiles",
    )(rows, counts, blocks, lines)
    scale = pl.pallas_call(
        functools.partial(scale_kernel, plan),
        out_shape=shape((flat, columns), F32),
        in_specs=[whole()],
        out_specs=whole(),
        scratch_shapes=[pltpu.VMEM((max(flat, block), block), F32)],
        compiler_params=params,
        name="scale",
    )(lines)

    middle = chunk // 2
    others = range(1, plan.plane)
    got = {p: plan.swap(send[p], 1) for p in (*others, 0)}
    got[plan.plane - 1], got[0] = lax.optimization_barrier((got[plan.plane - 1], got[0]))
    chip = {}
    for p in others:
        chip[p] = pl.pallas_call(
            functools.partial(chip_kernel, p * chunk),
            out_shape=[shape((middle, columns), BF16)] * 2,
            in_specs=[whole(), whole()],
            out_specs=[whole()] * 2,
            compiler_params=params,
            name="chip_sum",
        )(total, got[p])
    far_sent = [plan.swap_plane(chip[p][0], p) for p in others]
    near_sent = [plan.swap_plane(chip[p][1], p) for p in others]
    far_sent, scale = lax.optimization_barrier((far_sent, scale))

    def plane_sum(sent, start, dtypes):
        return pl.pallas_call(
            functools.partial(plane_kernel, flat, start),
            out_shape=[shape((flat, columns), dtype) for dtype in dtypes],
            in_specs=[whole()] * (2 + len(sent)),
            out_specs=[whole()] * len(dtypes),
            compiler_params=params,
            name="plane_sum",
        )(total, got[0], *sent)

    split_at = plan.line // 2
    far = plane_sum(far_sent, middle, [BF16] * split_at)
    far = [plan.swap_line(part, split_at + q) for q, part in enumerate(far)]
    held, *near = plane_sum(near_sent, 0, [F32] + [BF16] * (split_at - 1))
    near = [plan.swap_line(part, 1 + q) for q, part in enumerate(near)]
    near, far, tiles = lax.optimization_barrier((near, far, tiles))
    mine, rounded = pl.pallas_call(
        line_kernel,
        out_shape=(shape((flat, columns), F32), shape((flat, columns), BF16)),
        in_specs=[whole()] * (1 + plan.line),
        out_specs=(whole(), whole()),
        compiler_params=params,
        name="line_sum",
    )(held, scale, *near, *far)

    line = [rounded] + [plan.swap_line(rounded, q) for q in range(1, plan.line)]
    near, far = jnp.concatenate(line[:split_at], axis=0), jnp.concatenate(line[split_at:], axis=0)
    near = [near] + [plan.swap_plane(near, p) for p in reversed(others)]
    far = [far] + [plan.swap_plane(far, p) for p in others]
    own = far + near
    other = [plan.swap(part, 1) for part in own]

    pieces = own + other
    late = range(len(own) + plan.plane - 1, len(own) + plan.plane)
    gram = pl.pallas_call(
        gram_kernel,
        out_shape=shape((columns, columns), F32),
        in_specs=[whole()] * (len(pieces) - len(late)),
        out_specs=whole(),
        compiler_params=params,
        cost_estimate=pl.CostEstimate(flops=2 * features * columns * columns, bytes_accessed=4 << 20, transcendentals=0),
        name="gram",
    )(*[piece for i, piece in enumerate(pieces) if i not in late])
    return pl.pallas_call(
        functools.partial(last_kernel, plan, features, late),
        out_shape=(shape((flat, columns), F32), shape((documents * block, columns), BF16)),
        in_specs=[scalars()] + [whole()] * (3 + len(pieces)),
        out_specs=(pl.BlockSpec(memory_space=pltpu.HBM),) * 2,
        scratch_shapes=[
            pltpu.VMEM((features, columns), BF16),
            pltpu.VMEM((documents * block, columns), F32),
            pltpu.VMEM((columns, columns), F32),
            pltpu.VMEM((columns, columns), F32),
            pltpu.VMEM((flat, columns), F32),
            pltpu.VMEM((documents * block, columns), BF16),
            pltpu.SemaphoreType.DMA((1 + min(4, documents),)),
        ],
        compiler_params=params,
        name="factors",
    )(rows, tiles, mine, gram, *pieces)


def solution(mesh):
    placed = (
        P(AXES, None, None, None),
        P(AXES, None),
        P(AXES),
        P(AXES, None),
        P(),
    )

    def run(blocks, rows, counts, sketch, weights):
        plan = Plan(mesh.shape["row"], mesh.shape["col"], weights.shape[0], blocks.shape[2])
        return jax.shard_map(
            functools.partial(body, plan),
            mesh=mesh,
            in_specs=placed,
            out_specs=(P(AXES, None), P(AXES, None)),
            check_vma=False,
        )(blocks, rows, counts, sketch, weights)

    return run
```

```python
import functools

import jax
import jax.numpy as jnp
from jax import lax
from jax.experimental import pallas as pl
from jax.experimental.pallas import tpu as pltpu
from jax.sharding import PartitionSpec as P

F32 = jnp.float32
BF16 = jnp.bfloat16
AXES = ("row", "col")
VMEM_BYTES = 48 * 1024 * 1024


def whole():
    return pl.BlockSpec(memory_space=pltpu.VMEM)


def in_hbm(value):
    return pltpu.with_memory_space_constraint(value, pltpu.HBM)


def scalars():
    return pl.BlockSpec(memory_space=pltpu.SMEM)


class Plan:
    def __init__(self, rows, cols, features, block):
        self.count = rows * cols
        self.cols = cols
        self.plane = cols
        self.line = rows // 2
        self.plane_bits = cols.bit_length() - 1
        assert self.plane * self.line * 2 == self.count and self.count & (self.count - 1) == 0
        self.flat = features // self.count
        self.piece = min(self.flat, block)
        self.pieces = block // self.piece
        per_slice = self.flat // self.piece
        self.slice_bits = per_slice.bit_length() - 1
        assert 1 << self.slice_bits == per_slice and self.piece * self.pieces == block

    def me(self):
        return lax.axis_index("row") * self.cols + lax.axis_index("col")

    def start(self, me, feature_block, piece):
        unit = feature_block * self.pieces + piece
        owner = unit >> self.slice_bits
        inside = unit & ((1 << self.slice_bits) - 1)
        apart = owner ^ me
        place = (apart & 1) * self.plane + ((apart >> 1) & (self.plane - 1))
        place = place * self.line + (apart >> (1 + self.plane_bits))
        return pl.multiple_of(place * self.flat + inside * self.piece, self.piece)

    def swap(self, value, mask):
        return lax.ppermute(value, AXES, [(d, d ^ mask) for d in range(self.count)])

    def swap_plane(self, value, member):
        return self.swap(value, member << 1)

    def swap_line(self, value, member):
        return self.swap(value, member << (1 + self.plane_bits))


def sum_kernel(plan, rows_hbm, counts_hbm, blocks_ref, sketch_ref, total_ref, *rest):
    first_ref, tiles_ref, docs_ref, rows_ref, counts_ref, sems, small_sems = rest
    me = plan.me()
    documents, slots, block, _ = tiles_ref.shape
    parts = sems.shape[0]
    per = documents // parts
    small = (
        pltpu.make_async_copy(rows_hbm, rows_ref, small_sems.at[0]),
        pltpu.make_async_copy(counts_hbm, counts_ref, small_sems.at[1]),
    )
    for copy in small:
        copy.start()
    copies = []
    for c in range(parts):
        tiles_at = pl.ds(c * per, per)
        docs_at = pl.ds(c * per * block, per * block)
        pair = (
            pltpu.make_async_copy(blocks_ref.at[tiles_at], tiles_ref.at[tiles_at], sems.at[c, 0]),
            pltpu.make_async_copy(sketch_ref.at[docs_at], docs_ref.at[docs_at], sems.at[c, 1]),
        )
        for copy in pair:
            copy.start()
        copies.append(pair)
    total_ref[...] = jnp.zeros_like(total_ref)
    for copy in small:
        copy.wait()
    for c in range(parts):
        for copy in copies[c]:
            copy.wait()
        for d in range(c * per, (c + 1) * per):
            docs = docs_ref[d * block : (d + 1) * block, :]
            terms = jnp.dot(tiles_ref[d].reshape(slots * block, block), docs, preferred_element_type=F32)
            for s in range(slots):
                term = jnp.where(s < counts_ref[d], terms[s * block : (s + 1) * block], 0.0)
                for p in range(plan.pieces):
                    at = pl.ds(plan.start(me, rows_ref[s, d], p), plan.piece)
                    total_ref[at, :] += term[p * plan.piece : (p + 1) * plan.piece]
    first_ref[...] = total_ref[total_ref.shape[0] - first_ref.shape[0] :, :].astype(BF16)


def later_kernel(total_ref, later_ref):
    half = total_ref.shape[0] // 2
    later_ref[...] = total_ref[half : half + later_ref.shape[0], :].astype(BF16)


def tiles_kernel(rows_ref, counts_ref, blocks_ref, weights_ref, out_ref):
    documents, slots, block, _ = blocks_ref.shape
    for d in range(documents):
        for s in range(slots):
            scale = weights_ref[pl.ds(rows_ref[s, d], 1), :]
            scale = jnp.where(s < counts_ref[d], scale, 0.0)
            high, low = split(blocks_ref[d, s].T.astype(F32) * scale)
            out_ref[d, :block, s * block : (s + 1) * block] = high
            out_ref[d, block:, s * block : (s + 1) * block] = low


def scale_kernel(plan, weights_ref, scale_ref, turned_ref):
    block = weights_ref.shape[1]
    unit = plan.me() << plan.slice_bits
    lines = max(1, plan.flat // block)
    first = unit if plan.pieces == 1 else unit // plan.pieces
    for i in range(lines):
        line = weights_ref[pl.ds(first + i, 1), :]
        turned_ref[i * block : (i + 1) * block, :] = jnp.broadcast_to(line, (block, block)).T
    inside = 0 if plan.pieces == 1 else lax.rem(unit, plan.pieces) * plan.piece
    scale_ref[...] = turned_ref[pl.ds(pl.multiple_of(inside, plan.piece), plan.flat), :]


def chip_kernel(start, got_start, total_ref, got_ref, far_ref, near_ref):
    middle = near_ref.shape[0]
    for ref, at in ((far_ref, middle), (near_ref, 0)):
        held = total_ref[start + at : start + at + middle, :]
        got = got_ref[got_start + at : got_start + at + middle, :]
        ref[...] = (held + got.astype(F32)).astype(BF16)


def plane_kernel(flat, start, total_ref, got_ref, *rest):
    count = rest[0].shape[0] // flat
    parts, out_refs = rest[:-count], rest[-count:]
    for q, out_ref in enumerate(out_refs):
        at = slice(start + q * flat, start + (q + 1) * flat)
        total = total_ref[at, :] + got_ref[at, :].astype(F32)
        for ref in parts:
            total = total + ref[q * flat : (q + 1) * flat, :].astype(F32)
        out_ref[...] = total.astype(out_ref.dtype)


def line_kernel(held_ref, scale_ref, *rest):
    parts, (mine_ref, rounded_ref) = rest[:-2], rest[-2:]
    total = held_ref[...]
    for ref in parts:
        total = total + ref[...].astype(F32)
    total = total * scale_ref[...]
    mine_ref[...] = total
    rounded_ref[...] = total.astype(BF16)


def split(value):
    high = value.astype(BF16)
    return high, (value - high.astype(F32)).astype(BF16)


def dot_t(a, b):
    return lax.dot_general(a, b, (((1,), (1,)), ((), ())), preferred_element_type=F32)


def both(total):
    size = total.shape[1] // 2
    return total[:, :size] + total[:, size:]


def dot_t3(a, b):
    b_high, b_low = split(b)
    top = jnp.concatenate([b_high, b_high], axis=1)
    low = jnp.concatenate([b_low, jnp.zeros_like(b_low)], axis=1)
    return both(dot_t(jnp.concatenate(split(a), axis=1), jnp.concatenate([top, low], axis=0)))


def dot3(a, b):
    b_high, b_low = split(b)
    top = jnp.concatenate([b_high, b_low], axis=1)
    low = jnp.concatenate([b_high, jnp.zeros_like(b_low)], axis=1)
    return both(dot(jnp.concatenate(split(a), axis=1), jnp.concatenate([top, low], axis=0)))


def dot(a, b):
    return jnp.dot(a, b, preferred_element_type=F32)


def dot1(a, b):
    return dot(a.astype(BF16), b.astype(BF16))


def dot_t1(a, b):
    return dot_t(a.astype(BF16), b.astype(BF16))


def eliminate(gram_ref, inverse_ref):
    size = gram_ref.shape[0]
    lane = lax.broadcasted_iota(jnp.int32, (size, size), 1)
    line = lax.broadcasted_iota(jnp.int32, (size, 1), 0)
    first = lax.broadcasted_iota(jnp.int32, (1, size), 1)
    inverse_ref[...] = jnp.where(lane == line, 1.0, 0.0)

    def step(j, carry):
        values = gram_ref[...]
        pivot_row = gram_ref[pl.ds(j, 1), :]
        pivot = jnp.sum(jnp.where(first == j, pivot_row, 0.0), axis=1, keepdims=True)
        scale = 1.0 / jnp.sqrt(pivot)
        column = jnp.sum(jnp.where(lane == j, values, 0.0), axis=1, keepdims=True)
        column = jnp.where(line > j, column * scale, 0.0)
        gram_ref[...] = values - column * (pivot_row * scale)
        own_row = inverse_ref[pl.ds(j, 1), :] * scale
        inverse_ref[...] = jnp.where(line == j, own_row, inverse_ref[...] - column * own_row)
        return carry

    lax.fori_loop(0, size, step, 0)


def newton(gram, inverse_ref):
    size = gram.shape[0]
    line = lax.broadcasted_iota(jnp.int32, (size, size), 0)
    lane = lax.broadcasted_iota(jnp.int32, (size, size), 1)
    same = line == lane
    eye = jnp.where(same, 1.0, 0.0)
    take = jnp.where(line > lane, 1.0, jnp.where(same, 0.5, 0.0))
    diagonal = jnp.where(same, gram, 0.0)
    down = 1.0 / jnp.sqrt(jnp.sum(diagonal, axis=1, keepdims=True))
    across = 1.0 / jnp.sqrt(jnp.sum(diagonal, axis=0, keepdims=True))
    beyond = gram * down * across - eye
    factor = eye - take * beyond
    for product, product_t in ((dot1, dot_t1), (dot3, dot_t3)):
        left = factor - eye + product(factor, beyond)
        residual = factor.T - eye + product_t(left, factor)
        factor = factor - product(take * residual, factor)
    inverse_ref[...] = factor * across
    return jnp.sum(residual * residual)


def gram_kernel(*refs):
    gram = jnp.zeros(refs[-1].shape, F32)
    for ref in refs[:-1]:
        part = ref[...]
        gram += lax.dot_general(part, part, (((0,), (0,)), ((), ())), preferred_element_type=F32)
    refs[-1][...] = gram


def last_kernel(plan, features, late, rows_ref, tiles_ref, mine_ref, early_ref, *rest):
    parts, (basis_ref, factors_ref) = rest[: 4 * plan.plane], rest[4 * plan.plane : 4 * plan.plane + 2]
    all_ref, product_ref, gram_ref, inverse_ref, near_basis_ref, near_factors_ref, sems = rest[4 * plan.plane + 2 :]
    me = plan.me()
    documents = tiles_ref.shape[0]
    block = tiles_ref.shape[1] // 2
    slots = tiles_ref.shape[2] // block
    gram = early_ref[...]
    for i, ref in enumerate(parts):
        size = ref.shape[0]
        core, later = divmod(i, 2 * plan.plane)
        near, member = divmod(later, plan.plane)
        if near and member:
            member = plan.plane - member
        base = ((core * plan.plane + member) * 2 + 1 - near) * size
        part = ref[...]
        all_ref[base : base + size, :] = part
        if i in late:
            gram += lax.dot_general(part, part, (((0,), (0,)), ((), ())), preferred_element_type=F32)
    gram = gram * (1.0 / features)
    residual = newton(gram, inverse_ref)
    for d in range(documents):
        picked = []
        for s in range(slots):
            for p in range(plan.pieces):
                at = pl.ds(plan.start(me, rows_ref[s, d], p), plan.piece)
                picked.append(all_ref[at, :])
        terms = dot(tiles_ref[d], jnp.concatenate(picked, axis=0))
        product_ref[d * block : (d + 1) * block, :] = terms[:block] + terms[block:]

    @pl.when(jnp.logical_not(residual < 1e-3))
    def _():
        gram_ref[...] = gram
        eliminate(gram_ref, inverse_ref)

    inverse = inverse_ref[...]
    near_basis_ref[...] = dot_t3(mine_ref[...], inverse)
    copies = [pltpu.make_async_copy(near_basis_ref, basis_ref, sems.at[0])]
    copies[0].start()
    steps = sems.shape[0] - 1
    size = documents * block // steps
    for i in range(steps):
        at = pl.ds(i * size, size)
        near_factors_ref[at, :] = dot_t3(product_ref[at, :], inverse).astype(BF16)
        copies.append(pltpu.make_async_copy(near_factors_ref.at[at], factors_ref.at[at], sems.at[i + 1]))
        copies[-1].start()
    for copy in copies:
        copy.wait()


def body(plan, blocks, rows, counts, sketch, weights):
    documents, slots, block, _ = blocks.shape
    columns = sketch.shape[1]
    features = weights.shape[0]
    half = features // 2
    chunk = half // plan.plane
    flat = plan.flat
    params = pltpu.CompilerParams(vmem_limit_bytes=VMEM_BYTES)
    shape = jax.ShapeDtypeStruct
    rows = rows.T
    parts = min(4, documents)

    total, first = pl.pallas_call(
        functools.partial(sum_kernel, plan),
        out_shape=(pltpu.VMEM((features, columns), F32), pltpu.VMEM((chunk, columns), BF16)),
        in_specs=[pl.BlockSpec(memory_space=pltpu.HBM)] * 4,
        out_specs=(whole(), whole()),
        scratch_shapes=[
            pltpu.VMEM(blocks.shape, BF16),
            pltpu.VMEM(sketch.shape, BF16),
            pltpu.SMEM(rows.shape, jnp.int32),
            pltpu.SMEM(counts.shape, jnp.int32),
            pltpu.SemaphoreType.DMA((parts, 2)),
            pltpu.SemaphoreType.DMA((2,)),
        ],
        compiler_params=params,
        name="local_sum",
    )(in_hbm(rows), in_hbm(counts), in_hbm(blocks), in_hbm(sketch))

    lines = weights.reshape(features // block, block)
    tiles = pl.pallas_call(
        tiles_kernel,
        out_shape=shape((documents, 2 * block, slots * block), BF16),
        in_specs=[scalars(), scalars(), whole(), whole()],
        out_specs=whole(),
        compiler_params=params,
        cost_estimate=pl.CostEstimate(flops=1 << 20, bytes_accessed=4 << 20, transcendentals=0),
        name="tiles",
    )(rows, counts, blocks, lines)
    scale = pl.pallas_call(
        functools.partial(scale_kernel, plan),
        out_shape=shape((flat, columns), F32),
        in_specs=[whole()],
        out_specs=whole(),
        scratch_shapes=[pltpu.VMEM((max(flat, block), block), F32)],
        compiler_params=params,
        name="scale",
    )(lines)

    middle = chunk // 2
    others = range(1, plan.plane)
    first = plan.swap(first, 1)
    total, first = lax.optimization_barrier((total, first))
    later = pl.pallas_call(
        later_kernel,
        out_shape=shape((half - chunk, columns), BF16),
        in_specs=[whole()],
        out_specs=whole(),
        compiler_params=params,
        name="later",
    )(total)
    later = plan.swap(later, 1)
    chip = {}
    for p in others:
        last = p == plan.plane - 1
        chip[p] = pl.pallas_call(
            functools.partial(chip_kernel, p * chunk, 0 if last else p * chunk),
            out_shape=[shape((middle, columns), BF16)] * 2,
            in_specs=[whole(), whole()],
            out_specs=[whole()] * 2,
            compiler_params=params,
            name="chip_sum",
        )(total, first if last else later)
    far_sent = [plan.swap_plane(chip[p][0], p) for p in others]
    near_sent = [plan.swap_plane(chip[p][1], p) for p in others]
    far_sent, scale = lax.optimization_barrier((far_sent, scale))

    def plane_sum(sent, start, dtypes):
        return pl.pallas_call(
            functools.partial(plane_kernel, flat, start),
            out_shape=[shape((flat, columns), dtype) for dtype in dtypes],
            in_specs=[whole()] * (2 + len(sent)),
            out_specs=[whole()] * len(dtypes),
            compiler_params=params,
            name="plane_sum",
        )(total, later, *sent)

    split_at = plan.line // 2
    far = plane_sum(far_sent, middle, [BF16] * split_at)
    far = [plan.swap_line(part, split_at + q) for q, part in enumerate(far)]
    held, *near = plane_sum(near_sent, 0, [F32] + [BF16] * (split_at - 1))
    near = [plan.swap_line(part, 1 + q) for q, part in enumerate(near)]
    far, near, tiles = lax.optimization_barrier((far, near, tiles))
    mine, rounded = pl.pallas_call(
        line_kernel,
        out_shape=(shape((flat, columns), F32), shape((flat, columns), BF16)),
        in_specs=[whole()] * (1 + plan.line),
        out_specs=(whole(), whole()),
        compiler_params=params,
        name="line_sum",
    )(held, scale, *near, *far)

    line = [rounded] + [plan.swap_line(rounded, q) for q in range(1, plan.line)]
    near, far = jnp.concatenate(line[:split_at], axis=0), jnp.concatenate(line[split_at:], axis=0)
    near = [near] + [plan.swap_plane(near, p) for p in reversed(others)]
    far = [far] + [plan.swap_plane(far, p) for p in others]
    own = far + near
    other = [plan.swap(part, 1) for part in own]

    pieces = own + other
    late = range(len(own) + 1, len(own) + plan.plane)
    gram = pl.pallas_call(
        gram_kernel,
        out_shape=shape((columns, columns), F32),
        in_specs=[whole()] * (len(pieces) - len(late)),
        out_specs=whole(),
        compiler_params=params,
        cost_estimate=pl.CostEstimate(flops=2 * features * columns * columns, bytes_accessed=4 << 20, transcendentals=0),
        name="gram",
    )(*[piece for i, piece in enumerate(pieces) if i not in late])
    return pl.pallas_call(
        functools.partial(last_kernel, plan, features, late),
        out_shape=(shape((flat, columns), F32), shape((documents * block, columns), BF16)),
        in_specs=[scalars()] + [whole()] * (3 + len(pieces)),
        out_specs=(pl.BlockSpec(memory_space=pltpu.HBM),) * 2,
        scratch_shapes=[
            pltpu.VMEM((features, columns), BF16),
            pltpu.VMEM((documents * block, columns), F32),
            pltpu.VMEM((columns, columns), F32),
            pltpu.VMEM((columns, columns), F32),
            pltpu.VMEM((flat, columns), F32),
            pltpu.VMEM((documents * block, columns), BF16),
            pltpu.SemaphoreType.DMA((1 + min(4, documents),)),
        ],
        compiler_params=params,
        name="factors",
    )(rows, tiles, mine, gram, *pieces)


def solution(mesh):
    placed = (
        P(AXES, None, None, None),
        P(AXES, None),
        P(AXES),
        P(AXES, None),
        P(),
    )

    def run(blocks, rows, counts, sketch, weights):
        plan = Plan(mesh.shape["row"], mesh.shape["col"], weights.shape[0], blocks.shape[2])
        return jax.shard_map(
            functools.partial(body, plan),
            mesh=mesh,
            in_specs=placed,
            out_specs=(P(AXES, None), P(AXES, None)),
            check_vma=False,
        )(blocks, rows, counts, sketch, weights)

    return run
```

```python
import functools

import jax
import jax.numpy as jnp
from jax import lax
from jax.experimental import pallas as pl
from jax.experimental.pallas import tpu as pltpu
from jax.sharding import PartitionSpec as P

F32 = jnp.float32
BF16 = jnp.bfloat16
AXES = ("row", "col")
VMEM_BYTES = 48 * 1024 * 1024


def whole():
    return pl.BlockSpec(memory_space=pltpu.VMEM)


def in_hbm(value):
    return pltpu.with_memory_space_constraint(value, pltpu.HBM)


def scalars():
    return pl.BlockSpec(memory_space=pltpu.SMEM)


class Plan:
    def __init__(self, rows, cols, features, block):
        self.count = rows * cols
        self.cols = cols
        self.plane = cols
        self.line = rows // 2
        self.plane_bits = cols.bit_length() - 1
        assert self.plane * self.line * 2 == self.count and self.count & (self.count - 1) == 0
        self.flat = features // self.count
        self.piece = min(self.flat, block)
        self.pieces = block // self.piece
        per_slice = self.flat // self.piece
        self.slice_bits = per_slice.bit_length() - 1
        assert 1 << self.slice_bits == per_slice and self.piece * self.pieces == block

    def me(self):
        return lax.axis_index("row") * self.cols + lax.axis_index("col")

    def start(self, me, feature_block, piece):
        unit = feature_block * self.pieces + piece
        owner = unit >> self.slice_bits
        inside = unit & ((1 << self.slice_bits) - 1)
        apart = owner ^ me
        place = (apart & 1) * self.plane + ((apart >> 1) & (self.plane - 1))
        place = place * self.line + (apart >> (1 + self.plane_bits))
        return pl.multiple_of(place * self.flat + inside * self.piece, self.piece)

    def swap(self, value, mask):
        return lax.ppermute(value, AXES, [(d, d ^ mask) for d in range(self.count)])

    def swap_plane(self, value, member):
        return self.swap(value, member << 1)

    def swap_line(self, value, member):
        return self.swap(value, member << (1 + self.plane_bits))


def sum_kernel(plan, rows_hbm, counts_hbm, blocks_ref, sketch_ref, total_ref, *rest):
    send_refs, (tiles_ref, docs_ref, rows_ref, counts_ref, sems, small_sems) = rest[: plan.plane], rest[plan.plane :]
    me = plan.me()
    documents, slots, block, _ = tiles_ref.shape
    half = total_ref.shape[0] // 2
    parts = sems.shape[0]
    per = documents // parts
    small = (
        pltpu.make_async_copy(rows_hbm, rows_ref, small_sems.at[0]),
        pltpu.make_async_copy(counts_hbm, counts_ref, small_sems.at[1]),
    )
    for copy in small:
        copy.start()
    copies = []
    for c in range(parts):
        tiles_at = pl.ds(c * per, per)
        docs_at = pl.ds(c * per * block, per * block)
        pair = (
            pltpu.make_async_copy(blocks_ref.at[tiles_at], tiles_ref.at[tiles_at], sems.at[c, 0]),
            pltpu.make_async_copy(sketch_ref.at[docs_at], docs_ref.at[docs_at], sems.at[c, 1]),
        )
        for copy in pair:
            copy.start()
        copies.append(pair)
    total_ref[...] = jnp.zeros_like(total_ref)
    for copy in small:
        copy.wait()
    for c in range(parts):
        for copy in copies[c]:
            copy.wait()
        for d in range(c * per, (c + 1) * per):
            docs = docs_ref[d * block : (d + 1) * block, :]
            terms = jnp.dot(tiles_ref[d].reshape(slots * block, block), docs, preferred_element_type=F32)
            for s in range(slots):
                term = jnp.where(s < counts_ref[d], terms[s * block : (s + 1) * block], 0.0)
                for p in range(plan.pieces):
                    at = pl.ds(plan.start(me, rows_ref[s, d], p), plan.piece)
                    total_ref[at, :] += term[p * plan.piece : (p + 1) * plan.piece]
    for p, send_ref in enumerate(send_refs):
        size = send_ref.shape[0]
        send_ref[...] = total_ref[half + p * size : half + (p + 1) * size, :].astype(BF16)


def tiles_kernel(rows_ref, counts_ref, blocks_ref, weights_ref, out_ref):
    documents, slots, block, _ = blocks_ref.shape
    for d in range(documents):
        for s in range(slots):
            scale = weights_ref[pl.ds(rows_ref[s, d], 1), :]
            scale = jnp.where(s < counts_ref[d], scale, 0.0)
            high, low = split(blocks_ref[d, s].T.astype(F32) * scale)
            out_ref[d, :block, s * block : (s + 1) * block] = high
            out_ref[d, block:, s * block : (s + 1) * block] = low


def scale_kernel(plan, weights_ref, scale_ref, turned_ref):
    block = weights_ref.shape[1]
    unit = plan.me() << plan.slice_bits
    lines = max(1, plan.flat // block)
    first = unit if plan.pieces == 1 else unit // plan.pieces
    for i in range(lines):
        line = weights_ref[pl.ds(first + i, 1), :]
        turned_ref[i * block : (i + 1) * block, :] = jnp.broadcast_to(line, (block, block)).T
    inside = 0 if plan.pieces == 1 else lax.rem(unit, plan.pieces) * plan.piece
    scale_ref[...] = turned_ref[pl.ds(pl.multiple_of(inside, plan.piece), plan.flat), :]


def chip_kernel(start, total_ref, got_ref, far_ref, near_ref):
    middle = near_ref.shape[0]
    for ref, at in ((far_ref, middle), (near_ref, 0)):
        held = total_ref[start + at : start + at + middle, :]
        ref[...] = (held + got_ref[at : at + middle, :].astype(F32)).astype(BF16)


def plane_kernel(flat, start, total_ref, got_ref, *rest):
    count = rest[0].shape[0] // flat
    parts, out_refs = rest[:-count], rest[-count:]
    for q, out_ref in enumerate(out_refs):
        at = slice(start + q * flat, start + (q + 1) * flat)
        total = total_ref[at, :] + got_ref[at, :].astype(F32)
        for ref in parts:
            total = total + ref[q * flat : (q + 1) * flat, :].astype(F32)
        out_ref[...] = total.astype(out_ref.dtype)


def line_kernel(held_ref, scale_ref, *rest):
    parts, (mine_ref, rounded_ref) = rest[:-2], rest[-2:]
    total = held_ref[...]
    for ref in parts:
        total = total + ref[...].astype(F32)
    total = total * scale_ref[...]
    mine_ref[...] = total
    rounded_ref[...] = total.astype(BF16)


def split(value):
    high = value.astype(BF16)
    return high, (value - high.astype(F32)).astype(BF16)


def dot_t(a, b):
    return lax.dot_general(a, b, (((1,), (1,)), ((), ())), preferred_element_type=F32)


def both(total):
    size = total.shape[1] // 2
    return total[:, :size] + total[:, size:]


def dot_t3(a, b):
    b_high, b_low = split(b)
    top = jnp.concatenate([b_high, b_high], axis=1)
    low = jnp.concatenate([b_low, jnp.zeros_like(b_low)], axis=1)
    return both(dot_t(jnp.concatenate(split(a), axis=1), jnp.concatenate([top, low], axis=0)))


def dot3(a, b):
    b_high, b_low = split(b)
    top = jnp.concatenate([b_high, b_low], axis=1)
    low = jnp.concatenate([b_high, jnp.zeros_like(b_low)], axis=1)
    return both(dot(jnp.concatenate(split(a), axis=1), jnp.concatenate([top, low], axis=0)))


def dot(a, b):
    return jnp.dot(a, b, preferred_element_type=F32)


def dot1(a, b):
    return dot(a.astype(BF16), b.astype(BF16))


def dot_t1(a, b):
    return dot_t(a.astype(BF16), b.astype(BF16))


def eliminate(gram_ref, inverse_ref):
    size = gram_ref.shape[0]
    lane = lax.broadcasted_iota(jnp.int32, (size, size), 1)
    line = lax.broadcasted_iota(jnp.int32, (size, 1), 0)
    first = lax.broadcasted_iota(jnp.int32, (1, size), 1)
    inverse_ref[...] = jnp.where(lane == line, 1.0, 0.0)

    def step(j, carry):
        values = gram_ref[...]
        pivot_row = gram_ref[pl.ds(j, 1), :]
        pivot = jnp.sum(jnp.where(first == j, pivot_row, 0.0), axis=1, keepdims=True)
        scale = 1.0 / jnp.sqrt(pivot)
        column = jnp.sum(jnp.where(lane == j, values, 0.0), axis=1, keepdims=True)
        column = jnp.where(line > j, column * scale, 0.0)
        gram_ref[...] = values - column * (pivot_row * scale)
        own_row = inverse_ref[pl.ds(j, 1), :] * scale
        inverse_ref[...] = jnp.where(line == j, own_row, inverse_ref[...] - column * own_row)
        return carry

    lax.fori_loop(0, size, step, 0)


def newton(gram, inverse_ref):
    size = gram.shape[0]
    line = lax.broadcasted_iota(jnp.int32, (size, size), 0)
    lane = lax.broadcasted_iota(jnp.int32, (size, size), 1)
    same = line == lane
    eye = jnp.where(same, 1.0, 0.0)
    take = jnp.where(line > lane, 1.0, jnp.where(same, 0.5, 0.0))
    diagonal = jnp.where(same, gram, 0.0)
    down = 1.0 / jnp.sqrt(jnp.sum(diagonal, axis=1, keepdims=True))
    across = 1.0 / jnp.sqrt(jnp.sum(diagonal, axis=0, keepdims=True))
    beyond = gram * down * across - eye
    factor = eye - take * beyond
    for product, product_t in ((dot1, dot_t1), (dot3, dot_t3)):
        left = factor - eye + product(factor, beyond)
        residual = factor.T - eye + product_t(left, factor)
        factor = factor - product(take * residual, factor)
    inverse_ref[...] = factor * across
    return jnp.sum(residual * residual)


def gram_kernel(*refs):
    gram = jnp.zeros(refs[-1].shape, F32)
    for ref in refs[:-1]:
        part = ref[...]
        gram += lax.dot_general(part, part, (((0,), (0,)), ((), ())), preferred_element_type=F32)
    refs[-1][...] = gram


def last_kernel(plan, features, late, rows_ref, tiles_ref, mine_ref, early_ref, *rest):
    parts, (basis_ref, factors_ref) = rest[: 4 * plan.plane], rest[4 * plan.plane : 4 * plan.plane + 2]
    all_ref, product_ref, gram_ref, inverse_ref, near_basis_ref, near_factors_ref, sems = rest[4 * plan.plane + 2 :]
    me = plan.me()
    documents = tiles_ref.shape[0]
    block = tiles_ref.shape[1] // 2
    slots = tiles_ref.shape[2] // block
    gram = early_ref[...]
    for i, ref in enumerate(parts):
        size = ref.shape[0]
        core, later = divmod(i, 2 * plan.plane)
        near, member = divmod(later, plan.plane)
        if near and member:
            member = plan.plane - member
        base = ((core * plan.plane + member) * 2 + 1 - near) * size
        part = ref[...]
        all_ref[base : base + size, :] = part
        if i in late:
            gram += lax.dot_general(part, part, (((0,), (0,)), ((), ())), preferred_element_type=F32)
    gram = gram * (1.0 / features)
    residual = newton(gram, inverse_ref)
    for d in range(documents):
        picked = []
        for s in range(slots):
            for p in range(plan.pieces):
                at = pl.ds(plan.start(me, rows_ref[s, d], p), plan.piece)
                picked.append(all_ref[at, :])
        terms = dot(tiles_ref[d], jnp.concatenate(picked, axis=0))
        product_ref[d * block : (d + 1) * block, :] = terms[:block] + terms[block:]

    @pl.when(jnp.logical_not(residual < 1e-3))
    def _():
        gram_ref[...] = gram
        eliminate(gram_ref, inverse_ref)

    inverse = inverse_ref[...]
    near_basis_ref[...] = dot_t3(mine_ref[...], inverse)
    copies = [pltpu.make_async_copy(near_basis_ref, basis_ref, sems.at[0])]
    copies[0].start()
    steps = sems.shape[0] - 1
    size = documents * block // steps
    for i in range(steps):
        at = pl.ds(i * size, size)
        near_factors_ref[at, :] = dot_t3(product_ref[at, :], inverse).astype(BF16)
        copies.append(pltpu.make_async_copy(near_factors_ref.at[at], factors_ref.at[at], sems.at[i + 1]))
        copies[-1].start()
    for copy in copies:
        copy.wait()


def body(plan, blocks, rows, counts, sketch, weights):
    documents, slots, block, _ = blocks.shape
    columns = sketch.shape[1]
    features = weights.shape[0]
    half = features // 2
    chunk = half // plan.plane
    flat = plan.flat
    params = pltpu.CompilerParams(vmem_limit_bytes=VMEM_BYTES)
    shape = jax.ShapeDtypeStruct
    rows = rows.T
    parts = min(4, documents)

    total, *send = pl.pallas_call(
        functools.partial(sum_kernel, plan),
        out_shape=(pltpu.VMEM((features, columns), F32),) + (pltpu.VMEM((chunk, columns), BF16),) * plan.plane,
        in_specs=[pl.BlockSpec(memory_space=pltpu.HBM)] * 4,
        out_specs=(whole(),) * (1 + plan.plane),
        scratch_shapes=[
            pltpu.VMEM(blocks.shape, BF16),
            pltpu.VMEM(sketch.shape, BF16),
            pltpu.SMEM(rows.shape, jnp.int32),
            pltpu.SMEM(counts.shape, jnp.int32),
            pltpu.SemaphoreType.DMA((parts, 2)),
            pltpu.SemaphoreType.DMA((2,)),
        ],
        compiler_params=params,
        name="local_sum",
    )(in_hbm(rows), in_hbm(counts), in_hbm(blocks), in_hbm(sketch))

    lines = weights.reshape(features // block, block)
    tiles = pl.pallas_call(
        tiles_kernel,
        out_shape=shape((documents, 2 * block, slots * block), BF16),
        in_specs=[scalars(), scalars(), whole(), whole()],
        out_specs=whole(),
        compiler_params=params,
        cost_estimate=pl.CostEstimate(flops=1 << 20, bytes_accessed=4 << 20, transcendentals=0),
        name="tiles",
    )(rows, counts, blocks, lines)
    scale = pl.pallas_call(
        functools.partial(scale_kernel, plan),
        out_shape=shape((flat, columns), F32),
        in_specs=[whole()],
        out_specs=whole(),
        scratch_shapes=[pltpu.VMEM((max(flat, block), block), F32)],
        compiler_params=params,
        name="scale",
    )(lines)

    middle = chunk // 2
    others = range(1, plan.plane)
    got = {p: plan.swap(send[p], 1) for p in (*others, 0)}
    got[plan.plane - 1], got[0] = lax.optimization_barrier((got[plan.plane - 1], got[0]))
    chip = {}
    for p in others:
        chip[p] = pl.pallas_call(
            functools.partial(chip_kernel, p * chunk),
            out_shape=[shape((middle, columns), BF16)] * 2,
            in_specs=[whole(), whole()],
            out_specs=[whole()] * 2,
            compiler_params=params,
            name="chip_sum",
        )(total, got[p])
    far_sent = [plan.swap_plane(chip[p][0], p) for p in others]
    near_sent = [plan.swap_plane(chip[p][1], p) for p in others]
    far_sent, scale = lax.optimization_barrier((far_sent, scale))

    def plane_sum(sent, start, dtypes):
        return pl.pallas_call(
            functools.partial(plane_kernel, flat, start),
            out_shape=[shape((flat, columns), dtype) for dtype in dtypes],
            in_specs=[whole()] * (2 + len(sent)),
            out_specs=[whole()] * len(dtypes),
            compiler_params=params,
            name="plane_sum",
        )(total, got[0], *sent)

    split_at = plan.line // 2
    far = plane_sum(far_sent, middle, [BF16] * split_at)
    far = [plan.swap_line(part, split_at + q) for q, part in enumerate(far)]
    held, *near = plane_sum(near_sent, 0, [F32] + [BF16] * (split_at - 1))
    near = [plan.swap_line(part, 1 + q) for q, part in enumerate(near)]
    near, far, tiles = lax.optimization_barrier((near, far, tiles))
    mine, rounded = pl.pallas_call(
        line_kernel,
        out_shape=(shape((flat, columns), F32), shape((flat, columns), BF16)),
        in_specs=[whole()] * (1 + plan.line),
        out_specs=(whole(), whole()),
        compiler_params=params,
        name="line_sum",
    )(held, scale, *near, *far)

    line = [rounded] + [plan.swap_line(rounded, q) for q in range(1, plan.line)]
    near, far = jnp.concatenate(line[:split_at], axis=0), jnp.concatenate(line[split_at:], axis=0)
    near = [near] + [plan.swap_plane(near, p) for p in reversed(others)]
    far = [far] + [plan.swap_plane(far, p) for p in others]
    own = far + near
    other = [plan.swap(part, 1) for part in own]

    pieces = own + other
    late = range(len(own) + 1, len(own) + plan.plane)
    gram = pl.pallas_call(
        gram_kernel,
        out_shape=shape((columns, columns), F32),
        in_specs=[whole()] * (len(pieces) - len(late)),
        out_specs=whole(),
        compiler_params=params,
        cost_estimate=pl.CostEstimate(flops=2 * features * columns * columns, bytes_accessed=4 << 20, transcendentals=0),
        name="gram",
    )(*[piece for i, piece in enumerate(pieces) if i not in late])
    return pl.pallas_call(
        functools.partial(last_kernel, plan, features, late),
        out_shape=(shape((flat, columns), F32), shape((documents * block, columns), BF16)),
        in_specs=[scalars()] + [whole()] * (3 + len(pieces)),
        out_specs=(pl.BlockSpec(memory_space=pltpu.HBM),) * 2,
        scratch_shapes=[
            pltpu.VMEM((features, columns), BF16),
            pltpu.VMEM((documents * block, columns), F32),
            pltpu.VMEM((columns, columns), F32),
            pltpu.VMEM((columns, columns), F32),
            pltpu.VMEM((flat, columns), F32),
            pltpu.VMEM((documents * block, columns), BF16),
            pltpu.SemaphoreType.DMA((1 + min(4, documents),)),
        ],
        compiler_params=params,
        name="factors",
    )(rows, tiles, mine, gram, *pieces)


def solution(mesh):
    placed = (
        P(AXES, None, None, None),
        P(AXES, None),
        P(AXES),
        P(AXES, None),
        P(),
    )

    def run(blocks, rows, counts, sketch, weights):
        plan = Plan(mesh.shape["row"], mesh.shape["col"], weights.shape[0], blocks.shape[2])
        return jax.shard_map(
            functools.partial(body, plan),
            mesh=mesh,
            in_specs=placed,
            out_specs=(P(AXES, None), P(AXES, None)),
            check_vma=False,
        )(blocks, rows, counts, sketch, weights)

    return run
```

```python
import functools

import jax
import jax.numpy as jnp
from jax import lax
from jax.experimental import pallas as pl
from jax.experimental.pallas import tpu as pltpu
from jax.sharding import PartitionSpec as P

F32 = jnp.float32
BF16 = jnp.bfloat16
AXES = ("row", "col")
VMEM_BYTES = 48 * 1024 * 1024


def whole():
    return pl.BlockSpec(memory_space=pltpu.VMEM)


def in_hbm(value):
    return pltpu.with_memory_space_constraint(value, pltpu.HBM)


def scalars():
    return pl.BlockSpec(memory_space=pltpu.SMEM)


class Plan:
    def __init__(self, rows, cols, features, block):
        self.count = rows * cols
        self.cols = cols
        self.plane = cols
        self.line = rows // 2
        self.plane_bits = cols.bit_length() - 1
        assert self.plane * self.line * 2 == self.count and self.count & (self.count - 1) == 0
        self.flat = features // self.count
        self.piece = min(self.flat, block)
        self.pieces = block // self.piece
        per_slice = self.flat // self.piece
        self.slice_bits = per_slice.bit_length() - 1
        assert 1 << self.slice_bits == per_slice and self.piece * self.pieces == block

    def me(self):
        return lax.axis_index("row") * self.cols + lax.axis_index("col")

    def start(self, me, feature_block, piece):
        unit = feature_block * self.pieces + piece
        owner = unit >> self.slice_bits
        inside = unit & ((1 << self.slice_bits) - 1)
        apart = owner ^ me
        place = (apart & 1) * self.plane + ((apart >> 1) & (self.plane - 1))
        place = place * self.line + (apart >> (1 + self.plane_bits))
        return pl.multiple_of(place * self.flat + inside * self.piece, self.piece)

    def swap(self, value, mask):
        return lax.ppermute(value, AXES, [(d, d ^ mask) for d in range(self.count)])

    def swap_plane(self, value, member):
        return self.swap(value, member << 1)

    def swap_line(self, value, member):
        return self.swap(value, member << (1 + self.plane_bits))


def sum_kernel(plan, rows_hbm, counts_hbm, blocks_ref, sketch_ref, total_ref, *rest):
    send_refs, (tiles_ref, docs_ref, rows_ref, counts_ref, sems, small_sems) = rest[: plan.plane], rest[plan.plane :]
    me = plan.me()
    documents, slots, block, _ = tiles_ref.shape
    half = total_ref.shape[0] // 2
    parts = sems.shape[0]
    per = documents // parts
    small = (
        pltpu.make_async_copy(rows_hbm, rows_ref, small_sems.at[0]),
        pltpu.make_async_copy(counts_hbm, counts_ref, small_sems.at[1]),
    )
    for copy in small:
        copy.start()
    copies = []
    for c in range(parts):
        tiles_at = pl.ds(c * per, per)
        docs_at = pl.ds(c * per * block, per * block)
        pair = (
            pltpu.make_async_copy(blocks_ref.at[tiles_at], tiles_ref.at[tiles_at], sems.at[c, 0]),
            pltpu.make_async_copy(sketch_ref.at[docs_at], docs_ref.at[docs_at], sems.at[c, 1]),
        )
        for copy in pair:
            copy.start()
        copies.append(pair)
    total_ref[...] = jnp.zeros_like(total_ref)
    for copy in small:
        copy.wait()
    for c in range(parts):
        for copy in copies[c]:
            copy.wait()
        for d in range(c * per, (c + 1) * per):
            docs = docs_ref[d * block : (d + 1) * block, :]
            terms = jnp.dot(tiles_ref[d].reshape(slots * block, block), docs, preferred_element_type=F32)
            for s in range(slots):
                term = jnp.where(s < counts_ref[d], terms[s * block : (s + 1) * block], 0.0)
                for p in range(plan.pieces):
                    at = pl.ds(plan.start(me, rows_ref[s, d], p), plan.piece)
                    total_ref[at, :] += term[p * plan.piece : (p + 1) * plan.piece]
    for p, send_ref in enumerate(send_refs):
        size = send_ref.shape[0]
        send_ref[...] = total_ref[half + p * size : half + (p + 1) * size, :].astype(BF16)


def tiles_kernel(rows_ref, counts_ref, blocks_ref, weights_ref, out_ref):
    documents, slots, block, _ = blocks_ref.shape
    for d in range(documents):
        for s in range(slots):
            scale = weights_ref[pl.ds(rows_ref[s, d], 1), :]
            scale = jnp.where(s < counts_ref[d], scale, 0.0)
            high, low = split(blocks_ref[d, s].T.astype(F32) * scale)
            out_ref[d, :block, s * block : (s + 1) * block] = high
            out_ref[d, block:, s * block : (s + 1) * block] = low


def scale_kernel(plan, weights_ref, scale_ref, turned_ref):
    block = weights_ref.shape[1]
    unit = plan.me() << plan.slice_bits
    lines = max(1, plan.flat // block)
    first = unit if plan.pieces == 1 else unit // plan.pieces
    for i in range(lines):
        line = weights_ref[pl.ds(first + i, 1), :]
        turned_ref[i * block : (i + 1) * block, :] = jnp.broadcast_to(line, (block, block)).T
    inside = 0 if plan.pieces == 1 else lax.rem(unit, plan.pieces) * plan.piece
    scale_ref[...] = turned_ref[pl.ds(pl.multiple_of(inside, plan.piece), plan.flat), :]


def chip_kernel(start, total_ref, got_ref, far_ref, near_ref):
    middle = near_ref.shape[0]
    for ref, at in ((far_ref, middle), (near_ref, 0)):
        held = total_ref[start + at : start + at + middle, :]
        ref[...] = (held + got_ref[at : at + middle, :].astype(F32)).astype(BF16)


def plane_kernel(flat, start, total_ref, got_ref, *rest):
    count = rest[0].shape[0] // flat
    parts, out_refs = rest[:-count], rest[-count:]
    for q, out_ref in enumerate(out_refs):
        at = slice(start + q * flat, start + (q + 1) * flat)
        total = total_ref[at, :] + got_ref[at, :].astype(F32)
        for ref in parts:
            total = total + ref[q * flat : (q + 1) * flat, :].astype(F32)
        out_ref[...] = total.astype(out_ref.dtype)


def line_kernel(held_ref, scale_ref, *rest):
    parts, (mine_ref, rounded_ref) = rest[:-2], rest[-2:]
    total = held_ref[...]
    for ref in parts:
        total = total + ref[...].astype(F32)
    total = total * scale_ref[...]
    mine_ref[...] = total
    rounded_ref[...] = total.astype(BF16)


def split(value):
    high = value.astype(BF16)
    return high, (value - high.astype(F32)).astype(BF16)


def dot_t(a, b):
    return lax.dot_general(a, b, (((1,), (1,)), ((), ())), preferred_element_type=F32)


def both(total):
    size = total.shape[1] // 2
    return total[:, :size] + total[:, size:]


def dot_t3(a, b):
    b_high, b_low = split(b)
    top = jnp.concatenate([b_high, b_high], axis=1)
    low = jnp.concatenate([b_low, jnp.zeros_like(b_low)], axis=1)
    return both(dot_t(jnp.concatenate(split(a), axis=1), jnp.concatenate([top, low], axis=0)))


def dot3(a, b):
    b_high, b_low = split(b)
    top = jnp.concatenate([b_high, b_low], axis=1)
    low = jnp.concatenate([b_high, jnp.zeros_like(b_low)], axis=1)
    return both(dot(jnp.concatenate(split(a), axis=1), jnp.concatenate([top, low], axis=0)))


def dot(a, b):
    return jnp.dot(a, b, preferred_element_type=F32)


def dot1(a, b):
    return dot(a.astype(BF16), b.astype(BF16))


def dot_t1(a, b):
    return dot_t(a.astype(BF16), b.astype(BF16))


def eliminate(gram_ref, inverse_ref):
    size = gram_ref.shape[0]
    lane = lax.broadcasted_iota(jnp.int32, (size, size), 1)
    line = lax.broadcasted_iota(jnp.int32, (size, 1), 0)
    first = lax.broadcasted_iota(jnp.int32, (1, size), 1)
    inverse_ref[...] = jnp.where(lane == line, 1.0, 0.0)

    def step(j, carry):
        values = gram_ref[...]
        pivot_row = gram_ref[pl.ds(j, 1), :]
        pivot = jnp.sum(jnp.where(first == j, pivot_row, 0.0), axis=1, keepdims=True)
        scale = 1.0 / jnp.sqrt(pivot)
        column = jnp.sum(jnp.where(lane == j, values, 0.0), axis=1, keepdims=True)
        column = jnp.where(line > j, column * scale, 0.0)
        gram_ref[...] = values - column * (pivot_row * scale)
        own_row = inverse_ref[pl.ds(j, 1), :] * scale
        inverse_ref[...] = jnp.where(line == j, own_row, inverse_ref[...] - column * own_row)
        return carry

    lax.fori_loop(0, size, step, 0)


def newton(gram, inverse_ref):
    size = gram.shape[0]
    line = lax.broadcasted_iota(jnp.int32, (size, size), 0)
    lane = lax.broadcasted_iota(jnp.int32, (size, size), 1)
    same = line == lane
    eye = jnp.where(same, 1.0, 0.0)
    take = jnp.where(line > lane, 1.0, jnp.where(same, 0.5, 0.0))
    diagonal = jnp.where(same, gram, 0.0)
    down = 1.0 / jnp.sqrt(jnp.sum(diagonal, axis=1, keepdims=True))
    across = 1.0 / jnp.sqrt(jnp.sum(diagonal, axis=0, keepdims=True))
    beyond = gram * down * across - eye
    factor = eye - take * beyond
    for product, product_t in ((dot1, dot_t1), (dot3, dot_t3)):
        left = factor - eye + product(factor, beyond)
        residual = factor.T - eye + product_t(left, factor)
        factor = factor - product(take * residual, factor)
    inverse_ref[...] = factor * across
    return jnp.sum(residual * residual)


def gram_kernel(*refs):
    gram = jnp.zeros(refs[-1].shape, F32)
    for ref in refs[:-1]:
        part = ref[...]
        gram += lax.dot_general(part, part, (((0,), (0,)), ((), ())), preferred_element_type=F32)
    refs[-1][...] = gram


def last_kernel(plan, features, late, rows_ref, tiles_ref, mine_ref, early_ref, *rest):
    parts, (basis_ref, factors_ref) = rest[: 4 * plan.plane], rest[4 * plan.plane : 4 * plan.plane + 2]
    all_ref, product_ref, gram_ref, inverse_ref, near_basis_ref, near_factors_ref, sems = rest[4 * plan.plane + 2 :]
    me = plan.me()
    documents = tiles_ref.shape[0]
    block = tiles_ref.shape[1] // 2
    slots = tiles_ref.shape[2] // block
    gram = early_ref[...]
    for i, ref in enumerate(parts):
        size = ref.shape[0]
        core, later = divmod(i, 2 * plan.plane)
        near, member = divmod(later, plan.plane)
        if near and member:
            member = plan.plane - member
        base = ((core * plan.plane + member) * 2 + 1 - near) * size
        part = ref[...]
        all_ref[base : base + size, :] = part
        if i in late:
            gram += lax.dot_general(part, part, (((0,), (0,)), ((), ())), preferred_element_type=F32)
    gram = gram * (1.0 / features)
    residual = newton(gram, inverse_ref)
    for d in range(documents):
        picked = []
        for s in range(slots):
            for p in range(plan.pieces):
                at = pl.ds(plan.start(me, rows_ref[s, d], p), plan.piece)
                picked.append(all_ref[at, :])
        terms = dot(tiles_ref[d], jnp.concatenate(picked, axis=0))
        product_ref[d * block : (d + 1) * block, :] = terms[:block] + terms[block:]

    @pl.when(jnp.logical_not(residual < 1e-3))
    def _():
        gram_ref[...] = gram
        eliminate(gram_ref, inverse_ref)

    inverse = inverse_ref[...]
    near_basis_ref[...] = dot_t3(mine_ref[...], inverse)
    copies = [pltpu.make_async_copy(near_basis_ref, basis_ref, sems.at[0])]
    copies[0].start()
    steps = sems.shape[0] - 1
    size = documents * block // steps
    for i in range(steps):
        at = pl.ds(i * size, size)
        near_factors_ref[at, :] = dot_t3(product_ref[at, :], inverse).astype(BF16)
        copies.append(pltpu.make_async_copy(near_factors_ref.at[at], factors_ref.at[at], sems.at[i + 1]))
        copies[-1].start()
    for copy in copies:
        copy.wait()


def body(plan, blocks, rows, counts, sketch, weights):
    documents, slots, block, _ = blocks.shape
    columns = sketch.shape[1]
    features = weights.shape[0]
    half = features // 2
    chunk = half // plan.plane
    flat = plan.flat
    params = pltpu.CompilerParams(vmem_limit_bytes=VMEM_BYTES)
    shape = jax.ShapeDtypeStruct
    rows = rows.T
    parts = min(4, documents)

    total, *send = pl.pallas_call(
        functools.partial(sum_kernel, plan),
        out_shape=(pltpu.VMEM((features, columns), F32),) + (pltpu.VMEM((chunk, columns), BF16),) * plan.plane,
        in_specs=[pl.BlockSpec(memory_space=pltpu.HBM)] * 4,
        out_specs=(whole(),) * (1 + plan.plane),
        scratch_shapes=[
            pltpu.VMEM(blocks.shape, BF16),
            pltpu.VMEM(sketch.shape, BF16),
            pltpu.SMEM(rows.shape, jnp.int32),
            pltpu.SMEM(counts.shape, jnp.int32),
            pltpu.SemaphoreType.DMA((parts, 2)),
            pltpu.SemaphoreType.DMA((2,)),
        ],
        compiler_params=params,
        name="local_sum",
    )(in_hbm(rows), in_hbm(counts), in_hbm(blocks), in_hbm(sketch))

    lines = weights.reshape(features // block, block)
    tiles = pl.pallas_call(
        tiles_kernel,
        out_shape=shape((documents, 2 * block, slots * block), BF16),
        in_specs=[scalars(), scalars(), whole(), whole()],
        out_specs=whole(),
        compiler_params=params,
        cost_estimate=pl.CostEstimate(flops=1 << 20, bytes_accessed=4 << 20, transcendentals=0),
        name="tiles",
    )(rows, counts, blocks, lines)
    scale = pl.pallas_call(
        functools.partial(scale_kernel, plan),
        out_shape=shape((flat, columns), F32),
        in_specs=[whole()],
        out_specs=whole(),
        scratch_shapes=[pltpu.VMEM((max(flat, block), block), F32)],
        compiler_params=params,
        name="scale",
    )(lines)

    middle = chunk // 2
    others = range(1, plan.plane)
    got = {p: plan.swap(send[p], 1) for p in (*others, 0)}
    chip = {}
    for p in others:
        chip[p] = pl.pallas_call(
            functools.partial(chip_kernel, p * chunk),
            out_shape=[shape((middle, columns), BF16)] * 2,
            in_specs=[whole(), whole()],
            out_specs=[whole()] * 2,
            compiler_params=params,
            name="chip_sum",
        )(total, got[p])
    far_sent = [plan.swap_plane(chip[p][0], p) for p in others]
    near_sent = [plan.swap_plane(chip[p][1], p) for p in others]
    far_sent, scale = lax.optimization_barrier((far_sent, scale))

    def plane_sum(sent, start, dtypes):
        return pl.pallas_call(
            functools.partial(plane_kernel, flat, start),
            out_shape=[shape((flat, columns), dtype) for dtype in dtypes],
            in_specs=[whole()] * (2 + len(sent)),
            out_specs=[whole()] * len(dtypes),
            compiler_params=params,
            name="plane_sum",
        )(total, got[0], *sent)

    split_at = plan.line // 2
    far = plane_sum(far_sent, middle, [BF16] * split_at)
    far = [plan.swap_line(part, split_at + q) for q, part in enumerate(far)]
    held, *near = plane_sum(near_sent, 0, [F32] + [BF16] * (split_at - 1))
    near = [plan.swap_line(part, 1 + q) for q, part in enumerate(near)]
    near, far, tiles = lax.optimization_barrier((near, far, tiles))
    mine, rounded = pl.pallas_call(
        line_kernel,
        out_shape=(shape((flat, columns), F32), shape((flat, columns), BF16)),
        in_specs=[whole()] * (1 + plan.line),
        out_specs=(whole(), whole()),
        compiler_params=params,
        name="line_sum",
    )(held, scale, *near, *far)

    line = [rounded] + [plan.swap_line(rounded, q) for q in range(1, plan.line)]
    near, far = jnp.concatenate(line[:split_at], axis=0), jnp.concatenate(line[split_at:], axis=0)
    near = [near] + [plan.swap_plane(near, p) for p in reversed(others)]
    far = [far] + [plan.swap_plane(far, p) for p in others]
    own = far + near
    other = [plan.swap(part, 1) for part in own]

    pieces = own + other
    late = range(len(own) + 1, len(own) + plan.plane)
    gram = pl.pallas_call(
        gram_kernel,
        out_shape=shape((columns, columns), F32),
        in_specs=[whole()] * (len(pieces) - len(late)),
        out_specs=whole(),
        compiler_params=params,
        cost_estimate=pl.CostEstimate(flops=2 * features * columns * columns, bytes_accessed=4 << 20, transcendentals=0),
        name="gram",
    )(*[piece for i, piece in enumerate(pieces) if i not in late])
    return pl.pallas_call(
        functools.partial(last_kernel, plan, features, late),
        out_shape=(shape((flat, columns), F32), shape((documents * block, columns), BF16)),
        in_specs=[scalars()] + [whole()] * (3 + len(pieces)),
        out_specs=(pl.BlockSpec(memory_space=pltpu.HBM),) * 2,
        scratch_shapes=[
            pltpu.VMEM((features, columns), BF16),
            pltpu.VMEM((documents * block, columns), F32),
            pltpu.VMEM((columns, columns), F32),
            pltpu.VMEM((columns, columns), F32),
            pltpu.VMEM((flat, columns), F32),
            pltpu.VMEM((documents * block, columns), BF16),
            pltpu.SemaphoreType.DMA((1 + min(4, documents),)),
        ],
        compiler_params=params,
        name="factors",
    )(rows, tiles, mine, gram, *pieces)


def solution(mesh):
    placed = (
        P(AXES, None, None, None),
        P(AXES, None),
        P(AXES),
        P(AXES, None),
        P(),
    )

    def run(blocks, rows, counts, sketch, weights):
        plan = Plan(mesh.shape["row"], mesh.shape["col"], weights.shape[0], blocks.shape[2])
        return jax.shard_map(
            functools.partial(body, plan),
            mesh=mesh,
            in_specs=placed,
            out_specs=(P(AXES, None), P(AXES, None)),
            check_vma=False,
        )(blocks, rows, counts, sketch, weights)

    return run
```

```python
import functools

import jax
import jax.numpy as jnp
from jax import lax
from jax.experimental import pallas as pl
from jax.experimental.pallas import tpu as pltpu
from jax.sharding import PartitionSpec as P

F32 = jnp.float32
BF16 = jnp.bfloat16
AXES = ("row", "col")
VMEM_BYTES = 48 * 1024 * 1024


def whole():
    return pl.BlockSpec(memory_space=pltpu.VMEM)


def in_hbm(value):
    return pltpu.with_memory_space_constraint(value, pltpu.HBM)


def scalars():
    return pl.BlockSpec(memory_space=pltpu.SMEM)


class Plan:
    def __init__(self, rows, cols, features, block):
        self.count = rows * cols
        self.cols = cols
        self.plane = cols
        self.line = rows // 2
        self.plane_bits = cols.bit_length() - 1
        assert self.plane * self.line * 2 == self.count and self.count & (self.count - 1) == 0
        self.flat = features // self.count
        self.piece = min(self.flat, block)
        self.pieces = block // self.piece
        per_slice = self.flat // self.piece
        self.slice_bits = per_slice.bit_length() - 1
        assert 1 << self.slice_bits == per_slice and self.piece * self.pieces == block

    def me(self):
        return lax.axis_index("row") * self.cols + lax.axis_index("col")

    def start(self, me, feature_block, piece):
        unit = feature_block * self.pieces + piece
        owner = unit >> self.slice_bits
        inside = unit & ((1 << self.slice_bits) - 1)
        apart = owner ^ me
        place = (apart & 1) * self.plane + ((apart >> 1) & (self.plane - 1))
        place = place * self.line + (apart >> (1 + self.plane_bits))
        return pl.multiple_of(place * self.flat + inside * self.piece, self.piece)

    def swap(self, value, mask):
        return lax.ppermute(value, AXES, [(d, d ^ mask) for d in range(self.count)])

    def swap_plane(self, value, member):
        return self.swap(value, member << 1)

    def swap_line(self, value, member):
        return self.swap(value, member << (1 + self.plane_bits))


def sum_kernel(plan, rows_hbm, counts_hbm, blocks_ref, sketch_ref, total_ref, *rest):
    send_refs, (tiles_ref, docs_ref, rows_ref, counts_ref, sems, small_sems) = rest[: plan.plane], rest[plan.plane :]
    me = plan.me()
    documents, slots, block, _ = tiles_ref.shape
    half = total_ref.shape[0] // 2
    parts = sems.shape[0]
    per = documents // parts
    small = (
        pltpu.make_async_copy(rows_hbm, rows_ref, small_sems.at[0]),
        pltpu.make_async_copy(counts_hbm, counts_ref, small_sems.at[1]),
    )
    for copy in small:
        copy.start()
    copies = []
    for c in range(parts):
        tiles_at = pl.ds(c * per, per)
        docs_at = pl.ds(c * per * block, per * block)
        pair = (
            pltpu.make_async_copy(blocks_ref.at[tiles_at], tiles_ref.at[tiles_at], sems.at[c, 0]),
            pltpu.make_async_copy(sketch_ref.at[docs_at], docs_ref.at[docs_at], sems.at[c, 1]),
        )
        for copy in pair:
            copy.start()
        copies.append(pair)
    total_ref[...] = jnp.zeros_like(total_ref)
    for copy in small:
        copy.wait()
    for c in range(parts):
        for copy in copies[c]:
            copy.wait()
        for d in range(c * per, (c + 1) * per):
            docs = docs_ref[d * block : (d + 1) * block, :]
            terms = jnp.dot(tiles_ref[d].reshape(slots * block, block), docs, preferred_element_type=F32)
            for s in range(slots):
                term = jnp.where(s < counts_ref[d], terms[s * block : (s + 1) * block], 0.0)
                for p in range(plan.pieces):
                    at = pl.ds(plan.start(me, rows_ref[s, d], p), plan.piece)
                    total_ref[at, :] += term[p * plan.piece : (p + 1) * plan.piece]
    for p, send_ref in enumerate(send_refs):
        size = send_ref.shape[0]
        send_ref[...] = total_ref[half + p * size : half + (p + 1) * size, :].astype(BF16)


def tiles_kernel(rows_ref, counts_ref, blocks_ref, weights_ref, out_ref):
    documents, slots, block, _ = blocks_ref.shape
    for d in range(documents):
        for s in range(slots):
            scale = weights_ref[pl.ds(rows_ref[s, d], 1), :]
            scale = jnp.where(s < counts_ref[d], scale, 0.0)
            high, low = split(blocks_ref[d, s].T.astype(F32) * scale)
            out_ref[d, :block, s * block : (s + 1) * block] = high
            out_ref[d, block:, s * block : (s + 1) * block] = low


def scale_kernel(plan, weights_ref, scale_ref, turned_ref):
    block = weights_ref.shape[1]
    unit = plan.me() << plan.slice_bits
    lines = max(1, plan.flat // block)
    first = unit if plan.pieces == 1 else unit // plan.pieces
    for i in range(lines):
        line = weights_ref[pl.ds(first + i, 1), :]
        turned_ref[i * block : (i + 1) * block, :] = jnp.broadcast_to(line, (block, block)).T
    inside = 0 if plan.pieces == 1 else lax.rem(unit, plan.pieces) * plan.piece
    scale_ref[...] = turned_ref[pl.ds(pl.multiple_of(inside, plan.piece), plan.flat), :]


def chip_kernel(start, total_ref, got_ref, far_ref, near_ref):
    middle = near_ref.shape[0]
    for ref, at in ((far_ref, middle), (near_ref, 0)):
        held = total_ref[start + at : start + at + middle, :]
        ref[...] = (held + got_ref[at : at + middle, :].astype(F32)).astype(BF16)


def plane_kernel(flat, start, total_ref, got_ref, *rest):
    count = rest[0].shape[0] // flat
    parts, out_refs = rest[:-count], rest[-count:]
    for q, out_ref in enumerate(out_refs):
        at = slice(start + q * flat, start + (q + 1) * flat)
        total = total_ref[at, :] + got_ref[at, :].astype(F32)
        for ref in parts:
            total = total + ref[q * flat : (q + 1) * flat, :].astype(F32)
        out_ref[...] = total.astype(out_ref.dtype)


def line_kernel(held_ref, scale_ref, *rest):
    parts, (mine_ref, rounded_ref) = rest[:-2], rest[-2:]
    total = held_ref[...]
    for ref in parts:
        total = total + ref[...].astype(F32)
    total = total * scale_ref[...]
    mine_ref[...] = total
    rounded_ref[...] = total.astype(BF16)


def split(value):
    high = value.astype(BF16)
    return high, (value - high.astype(F32)).astype(BF16)


def dot_t(a, b):
    return lax.dot_general(a, b, (((1,), (1,)), ((), ())), preferred_element_type=F32)


def both(total):
    size = total.shape[1] // 2
    return total[:, :size] + total[:, size:]


def dot_t3(a, b):
    b_high, b_low = split(b)
    top = jnp.concatenate([b_high, b_high], axis=1)
    low = jnp.concatenate([b_low, jnp.zeros_like(b_low)], axis=1)
    return both(dot_t(jnp.concatenate(split(a), axis=1), jnp.concatenate([top, low], axis=0)))


def dot3(a, b):
    b_high, b_low = split(b)
    top = jnp.concatenate([b_high, b_low], axis=1)
    low = jnp.concatenate([b_high, jnp.zeros_like(b_low)], axis=1)
    return both(dot(jnp.concatenate(split(a), axis=1), jnp.concatenate([top, low], axis=0)))


def dot(a, b):
    return jnp.dot(a, b, preferred_element_type=F32)


def dot1(a, b):
    return dot(a.astype(BF16), b.astype(BF16))


def dot_t1(a, b):
    return dot_t(a.astype(BF16), b.astype(BF16))


def eliminate(gram_ref, inverse_ref):
    size = gram_ref.shape[0]
    lane = lax.broadcasted_iota(jnp.int32, (size, size), 1)
    line = lax.broadcasted_iota(jnp.int32, (size, 1), 0)
    first = lax.broadcasted_iota(jnp.int32, (1, size), 1)
    inverse_ref[...] = jnp.where(lane == line, 1.0, 0.0)

    def step(j, carry):
        values = gram_ref[...]
        pivot_row = gram_ref[pl.ds(j, 1), :]
        pivot = jnp.sum(jnp.where(first == j, pivot_row, 0.0), axis=1, keepdims=True)
        scale = 1.0 / jnp.sqrt(pivot)
        column = jnp.sum(jnp.where(lane == j, values, 0.0), axis=1, keepdims=True)
        column = jnp.where(line > j, column * scale, 0.0)
        gram_ref[...] = values - column * (pivot_row * scale)
        own_row = inverse_ref[pl.ds(j, 1), :] * scale
        inverse_ref[...] = jnp.where(line == j, own_row, inverse_ref[...] - column * own_row)
        return carry

    lax.fori_loop(0, size, step, 0)


def newton(gram, inverse_ref, fill):
    size = gram.shape[0]
    line = lax.broadcasted_iota(jnp.int32, (size, size), 0)
    lane = lax.broadcasted_iota(jnp.int32, (size, size), 1)
    same = line == lane
    eye = jnp.where(same, 1.0, 0.0)
    take = jnp.where(line > lane, 1.0, jnp.where(same, 0.5, 0.0))
    diagonal = jnp.where(same, gram, 0.0)
    down = 1.0 / jnp.sqrt(jnp.sum(diagonal, axis=1, keepdims=True))
    across = 1.0 / jnp.sqrt(jnp.sum(diagonal, axis=0, keepdims=True))
    beyond = gram * down * across - eye
    factor = eye - take * beyond
    for product, product_t in ((dot1, dot_t1), (dot3, dot_t3)):
        left = factor - eye + product(factor, beyond)
        fill()
        residual = factor.T - eye + product_t(left, factor)
        fill()
        factor = factor - product(take * residual, factor)
        fill()
    inverse_ref[...] = factor * across
    return jnp.sum(residual * residual)


def gram_kernel(*refs):
    gram = jnp.zeros(refs[-1].shape, F32)
    for ref in refs[:-1]:
        part = ref[...]
        gram += lax.dot_general(part, part, (((0,), (0,)), ((), ())), preferred_element_type=F32)
    refs[-1][...] = gram


def last_kernel(plan, features, late, rows_ref, tiles_ref, mine_ref, early_ref, *rest):
    parts, (basis_ref, factors_ref) = rest[: 4 * plan.plane], rest[4 * plan.plane : 4 * plan.plane + 2]
    all_ref, product_ref, gram_ref, inverse_ref, near_basis_ref, near_factors_ref, sems = rest[4 * plan.plane + 2 :]
    me = plan.me()
    documents = tiles_ref.shape[0]
    block = tiles_ref.shape[1] // 2
    slots = tiles_ref.shape[2] // block
    gram = early_ref[...]
    for i, ref in enumerate(parts):
        size = ref.shape[0]
        core, later = divmod(i, 2 * plan.plane)
        near, member = divmod(later, plan.plane)
        if near and member:
            member = plan.plane - member
        base = ((core * plan.plane + member) * 2 + 1 - near) * size
        part = ref[...]
        all_ref[base : base + size, :] = part
        if i in late:
            gram += lax.dot_general(part, part, (((0,), (0,)), ((), ())), preferred_element_type=F32)
    gram = gram * (1.0 / features)
    left = list(range(documents))
    share = -(-documents // 6)

    def fill():
        for d in left[:share]:
            picked = []
            for s in range(slots):
                for p in range(plan.pieces):
                    at = pl.ds(plan.start(me, rows_ref[s, d], p), plan.piece)
                    picked.append(all_ref[at, :])
            terms = dot(tiles_ref[d], jnp.concatenate(picked, axis=0))
            product_ref[d * block : (d + 1) * block, :] = terms[:block] + terms[block:]
        del left[:share]

    residual = newton(gram, inverse_ref, fill)
    assert not left

    @pl.when(jnp.logical_not(residual < 1e-3))
    def _():
        gram_ref[...] = gram
        eliminate(gram_ref, inverse_ref)

    inverse = inverse_ref[...]
    near_basis_ref[...] = dot_t3(mine_ref[...], inverse)
    copies = [pltpu.make_async_copy(near_basis_ref, basis_ref, sems.at[0])]
    copies[0].start()
    steps = sems.shape[0] - 1
    size = documents * block // steps
    for i in range(steps):
        at = pl.ds(i * size, size)
        near_factors_ref[at, :] = dot_t3(product_ref[at, :], inverse).astype(BF16)
        copies.append(pltpu.make_async_copy(near_factors_ref.at[at], factors_ref.at[at], sems.at[i + 1]))
        copies[-1].start()
    for copy in copies:
        copy.wait()


def body(plan, blocks, rows, counts, sketch, weights):
    documents, slots, block, _ = blocks.shape
    columns = sketch.shape[1]
    features = weights.shape[0]
    half = features // 2
    chunk = half // plan.plane
    flat = plan.flat
    params = pltpu.CompilerParams(vmem_limit_bytes=VMEM_BYTES)
    shape = jax.ShapeDtypeStruct
    rows = rows.T
    parts = min(4, documents)

    total, *send = pl.pallas_call(
        functools.partial(sum_kernel, plan),
        out_shape=(pltpu.VMEM((features, columns), F32),) + (pltpu.VMEM((chunk, columns), BF16),) * plan.plane,
        in_specs=[pl.BlockSpec(memory_space=pltpu.HBM)] * 4,
        out_specs=(whole(),) * (1 + plan.plane),
        scratch_shapes=[
            pltpu.VMEM(blocks.shape, BF16),
            pltpu.VMEM(sketch.shape, BF16),
            pltpu.SMEM(rows.shape, jnp.int32),
            pltpu.SMEM(counts.shape, jnp.int32),
            pltpu.SemaphoreType.DMA((parts, 2)),
            pltpu.SemaphoreType.DMA((2,)),
        ],
        compiler_params=params,
        name="local_sum",
    )(in_hbm(rows), in_hbm(counts), in_hbm(blocks), in_hbm(sketch))

    lines = weights.reshape(features // block, block)
    tiles = pl.pallas_call(
        tiles_kernel,
        out_shape=shape((documents, 2 * block, slots * block), BF16),
        in_specs=[scalars(), scalars(), whole(), whole()],
        out_specs=whole(),
        compiler_params=params,
        cost_estimate=pl.CostEstimate(flops=1 << 20, bytes_accessed=4 << 20, transcendentals=0),
        name="tiles",
    )(rows, counts, blocks, lines)
    scale = pl.pallas_call(
        functools.partial(scale_kernel, plan),
        out_shape=shape((flat, columns), F32),
        in_specs=[whole()],
        out_specs=whole(),
        scratch_shapes=[pltpu.VMEM((max(flat, block), block), F32)],
        compiler_params=params,
        name="scale",
    )(lines)

    middle = chunk // 2
    others = range(1, plan.plane)
    got = {p: plan.swap(send[p], 1) for p in (*others, 0)}
    got[plan.plane - 1], got[0] = lax.optimization_barrier((got[plan.plane - 1], got[0]))
    chip = {}
    for p in others:
        chip[p] = pl.pallas_call(
            functools.partial(chip_kernel, p * chunk),
            out_shape=[shape((middle, columns), BF16)] * 2,
            in_specs=[whole(), whole()],
            out_specs=[whole()] * 2,
            compiler_params=params,
            name="chip_sum",
        )(total, got[p])
    far_sent = [plan.swap_plane(chip[p][0], p) for p in others]
    near_sent = [plan.swap_plane(chip[p][1], p) for p in others]
    far_sent, scale = lax.optimization_barrier((far_sent, scale))

    def plane_sum(sent, start, dtypes):
        return pl.pallas_call(
            functools.partial(plane_kernel, flat, start),
            out_shape=[shape((flat, columns), dtype) for dtype in dtypes],
            in_specs=[whole()] * (2 + len(sent)),
            out_specs=[whole()] * len(dtypes),
            compiler_params=params,
            name="plane_sum",
        )(total, got[0], *sent)

    split_at = plan.line // 2
    far = plane_sum(far_sent, middle, [BF16] * split_at)
    far = [plan.swap_line(part, split_at + q) for q, part in enumerate(far)]
    held, *near = plane_sum(near_sent, 0, [F32] + [BF16] * (split_at - 1))
    near = [plan.swap_line(part, 1 + q) for q, part in enumerate(near)]
    near, far, tiles = lax.optimization_barrier((near, far, tiles))
    mine, rounded = pl.pallas_call(
        line_kernel,
        out_shape=(shape((flat, columns), F32), shape((flat, columns), BF16)),
        in_specs=[whole()] * (1 + plan.line),
        out_specs=(whole(), whole()),
        compiler_params=params,
        name="line_sum",
    )(held, scale, *near, *far)

    line = [rounded] + [plan.swap_line(rounded, q) for q in range(1, plan.line)]
    near, far = jnp.concatenate(line[:split_at], axis=0), jnp.concatenate(line[split_at:], axis=0)
    near = [near] + [plan.swap_plane(near, p) for p in reversed(others)]
    far = [far] + [plan.swap_plane(far, p) for p in others]
    own = far + near
    other = [plan.swap(part, 1) for part in own]

    pieces = own + other
    late = range(len(own) + 1, len(own) + plan.plane)
    gram = pl.pallas_call(
        gram_kernel,
        out_shape=shape((columns, columns), F32),
        in_specs=[whole()] * (len(pieces) - len(late)),
        out_specs=whole(),
        compiler_params=params,
        cost_estimate=pl.CostEstimate(flops=2 * features * columns * columns, bytes_accessed=4 << 20, transcendentals=0),
        name="gram",
    )(*[piece for i, piece in enumerate(pieces) if i not in late])
    return pl.pallas_call(
        functools.partial(last_kernel, plan, features, late),
        out_shape=(shape((flat, columns), F32), shape((documents * block, columns), BF16)),
        in_specs=[scalars()] + [whole()] * (3 + len(pieces)),
        out_specs=(pl.BlockSpec(memory_space=pltpu.HBM),) * 2,
        scratch_shapes=[
            pltpu.VMEM((features, columns), BF16),
            pltpu.VMEM((documents * block, columns), F32),
            pltpu.VMEM((columns, columns), F32),
            pltpu.VMEM((columns, columns), F32),
            pltpu.VMEM((flat, columns), F32),
            pltpu.VMEM((documents * block, columns), BF16),
            pltpu.SemaphoreType.DMA((1 + min(4, documents),)),
        ],
        compiler_params=params,
        name="factors",
    )(rows, tiles, mine, gram, *pieces)


def solution(mesh):
    placed = (
        P(AXES, None, None, None),
        P(AXES, None),
        P(AXES),
        P(AXES, None),
        P(),
    )

    def run(blocks, rows, counts, sketch, weights):
        plan = Plan(mesh.shape["row"], mesh.shape["col"], weights.shape[0], blocks.shape[2])
        return jax.shard_map(
            functools.partial(body, plan),
            mesh=mesh,
            in_specs=placed,
            out_specs=(P(AXES, None), P(AXES, None)),
            check_vma=False,
        )(blocks, rows, counts, sketch, weights)

    return run
```
